32 devices in a mesh: fsdp: 8 (over z, x), rep: 4 (over y, core).
Axes of the slice: x: 2, y: 2, z: 4, core: 2. Of those that a mesh axis runs over, the one named last changes fastest.
Arguments:
- tokens: bfloat16 [16384, 1024], P(('fsdp', 'rep')), may hold values from -6 to 6
- cond: bfloat16 [64, 768], P(('fsdp', 'rep')), may hold values from -4 to 4
- sigma_idx: int32 [64], P(('fsdp', 'rep')), may hold values from 0 to 63
- pos_rows: int32 [16384], P(('fsdp', 'rep')), may hold values from 0 to 15
- pos_cols: int32 [16384], P(('fsdp', 'rep')), may hold values from 0 to 15
- attn_scale: float32 [16], replicated, may hold values from 6 to 16
- w_mod1: bfloat16 [768, 1024], P('fsdp'), may hold values from -0.21875 to 0.21875
- w_qkv: bfloat16 [1024, 3072], P('fsdp'), may hold values from -0.1875 to 0.1875
- w_out: bfloat16 [1024, 1024], P('fsdp'), may hold values from -0.5 to 0.5
- w_mod2: bfloat16 [768, 1024], P('fsdp'), may hold values from -0.21875 to 0.21875
- w_up: bfloat16 [1024, 6144], P('fsdp'), may hold values from -0.1875 to 0.1875
- w_down: bfloat16 [3072, 1024], P('fsdp'), may hold values from -0.15625 to 0.15625
- cotangent: bfloat16 [16384, 1024], P(('fsdp', 'rep')), may hold values from -6 to 6
Outputs:
- out: bfloat16 [16384, 1024], P(('fsdp', 'rep'))
- d_tokens: bfloat16 [16384, 1024], P(('fsdp', 'rep'))
- d_cond: float32 [64, 768], P(('fsdp', 'rep'))
- d_attn_scale: float32 [16], replicated
- g_mod1: float32 [768, 1024], P('fsdp')
- g_qkv: float32 [1024, 3072], P('fsdp')
- g_out: float32 [1024, 1024], P('fsdp')
- g_mod2: float32 [768, 1024], P('fsdp')
- g_up: float32 [1024, 6144], P('fsdp')
- g_down: float32 [3072, 1024], P('fsdp')
The draws below stay inside these ranges and needn't reach their ends.
All inputs are finite; a program needn't handle non-finite values.
Results may differ from the reference program's by a relative error of at most 0.02.
Values may be sent and summed in bfloat16 or wider, within the bound.
A program may use at most 256 MiB of HBM per device.

```python
import math
import jax
import jax.numpy as jnp
from jax import lax

D = 1024
FF = 3072
MAP = 768
HEADS = 16
GRID = 16
IMG_TOK = 256
NB = 64
IMAGES = 64
TOKENS = 16384


def set_ends(entries, rng, low, largest):
    longest = entries.shape.index(max(entries.shape))
    spots = []
    for shift in (0, 1):
        where = [jax.random.randint(jax.random.fold_in(rng, axis), (), 0, length) for axis, length in enumerate(entries.shape)]
        where[longest] = (where[longest] + shift) % entries.shape[longest]
        spots.append(tuple(where))
    return entries.at[spots[0]].set(low).at[spots[1]].set(largest)


def level_of(key, dims, cuts, smallest, largest):
    gain, own = 1.0, jax.random.fold_in(key, 6)
    for axis_at, parts in cuts:
        heights = jnp.exp(jax.random.uniform(jax.random.fold_in(own, axis_at), (parts,), jnp.float32, smallest / len(cuts), largest / len(cuts)))
        gain = gain * jnp.repeat(heights, dims[axis_at] // parts).reshape([-1 if axis == axis_at else 1 for axis in range(len(dims))])
    return gain


def gaussian(key, dims, deviation, limit, shards=(), kind=jnp.bfloat16):
    values = jax.random.normal(key, dims, jnp.float32) * deviation
    if len(shards) > 0:
        values = level_of(key, dims, shards, -0.22, 0.18) * values
    return jnp.clip(values, min=-limit, max=limit).astype(kind)


def setup_inputs(seed: int = 0) -> dict:
    splits = jax.random.split(jax.random.key(seed), 14)
    return {
        "tokens": gaussian(splits[0], (TOKENS, D), 1.0, 6.0, ((0, 32),)),
        "cond": gaussian(splits[1], (IMAGES, MAP), 0.5, 4.0, ((0, 32),)),
        "sigma_idx": set_ends(jax.random.randint(splits[2], (IMAGES,), 0, NB), jax.random.fold_in(splits[2], 1), 0, NB - 1).astype(jnp.int32),
        "pos_rows": set_ends(jax.random.randint(splits[3], (TOKENS,), 0, GRID), jax.random.fold_in(splits[3], 1), 0, GRID - 1).astype(jnp.int32),
        "pos_cols": set_ends(jax.random.randint(splits[4], (TOKENS,), 0, GRID), jax.random.fold_in(splits[4], 1), 0, GRID - 1).astype(jnp.int32),
        "attn_scale": jnp.clip(jnp.exp(jax.random.uniform(splits[5], (HEADS,), jnp.float32, math.log(6.0), math.log(16.0))), 6.0, 16.0),
        "w_mod1": gaussian(splits[6], (MAP, D), MAP ** -0.5, 0.21875, ((0, 8),)),
        "w_qkv": gaussian(splits[7], (D, 3 * D), D ** -0.5, 0.1875, ((0, 8),)),
        "w_out": gaussian(splits[8], (D, D), (D // 8) ** -0.5, 0.5, ((0, 8),)),
        "w_mod2": gaussian(splits[9], (MAP, D), MAP ** -0.5, 0.21875, ((0, 8),)),
        "w_up": gaussian(splits[10], (D, 2 * FF), D ** -0.5, 0.1875, ((0, 8),)),
        "w_down": gaussian(splits[11], (FF, D), (FF // 2) ** -0.5, 0.15625, ((0, 8),)),
        "cotangent": gaussian(splits[12], (TOKENS, D), 1.0, 6.0, ((0, 32),)),
    }


@jax.custom_vjp
def low(v):
    return lax.optimization_barrier(v.astype(jnp.bfloat16)).astype(jnp.float32)

@jax.custom_vjp
def low_back(v):
    return v

def low_keep(v):
    return (low(v), None)

def low_pass(kept, grad):
    return (grad,)

def back_keep(v):
    return (v, None)

def back_low(kept, grad):
    return (low(grad),)
low.defvjp(low_keep, low_pass)
low_back.defvjp(back_keep, back_low)

def sigma_weight(bucket):
    level = bucket.astype(jnp.float32) / (NB - 1)
    sigma = jnp.exp(-2.0 + 3.2 * level)
    return 1.0 / (1.0 + 4.0 * sigma * sigma) + 0.25

def ada_norm(values, modulation):
    factor = lax.rsqrt(lax.optimization_barrier(jnp.mean(values * values, axis=-1, keepdims=True)) + 1e-06)
    return values * factor * (1.0 + modulation)[:, None, :]

def axial_rope(values, rows, cols):
    head_dim = values.shape[-1]
    turned = head_dim // 2
    pairs = turned // 2
    quarter = pairs // 2
    steps = jnp.arange(quarter, dtype=jnp.float32)
    freqs = math.pi * jnp.exp(math.log(10.0) * steps / max(quarter - 1, 1))
    row_pos = (rows.astype(jnp.float32) + 0.5) * (2.0 / GRID) - 1.0
    col_pos = (cols.astype(jnp.float32) + 0.5) * (2.0 / GRID) - 1.0
    angles = jnp.concatenate([row_pos[..., None] * freqs, col_pos[..., None] * freqs], axis=-1)
    cosine = jnp.cos(angles)[:, :, None, :]
    sine = jnp.sin(angles)[:, :, None, :]
    first = values[..., :pairs]
    second = values[..., pairs:turned]
    rest = values[..., turned:]
    return jnp.concatenate([first * cosine - second * sine, first * sine + second * cosine, rest], axis=-1)

def cosine_rope(query, keys, scale, rows, cols):
    root = jnp.sqrt(scale)[None, None, :, None]
    query_n = query * lax.rsqrt(lax.optimization_barrier(jnp.sum(query * query, axis=-1, keepdims=True)) + 1e-06) * root
    keys_n = keys * lax.rsqrt(lax.optimization_barrier(jnp.sum(keys * keys, axis=-1, keepdims=True)) + 1e-06) * root
    return (axial_rope(query_n, rows, cols), axial_rope(keys_n, rows, cols))

def geglu_gate(upward):
    hidden = upward.shape[-1] // 2
    return upward[..., :hidden] * jax.nn.gelu(upward[..., hidden:], approximate=False)

def block_layer(inputs, conds, scale, w_mod1, w_qkv, w_out, w_mod2, w_up, w_down, rows, cols):
    high = lax.Precision.HIGHEST
    images, length, width = inputs.shape
    heads = scale.shape[0]
    head_dim = width // heads
    mod_one = low_back(jnp.dot(conds, w_mod1, precision=high))
    normed = low(ada_norm(inputs, mod_one))
    project = low_back(jnp.einsum('ild,de->ile', normed, w_qkv, precision=high))
    query = project[..., :width].reshape(images, length, heads, head_dim)
    keys = project[..., width:2 * width].reshape(images, length, heads, head_dim)
    value = low(project[..., 2 * width:].reshape(images, length, heads, head_dim))
    query_rot, keys_rot = cosine_rope(query, keys, scale, rows, cols)
    query_rot = low(query_rot)
    keys_rot = low(keys_rot)
    scores = low_back(jnp.einsum('ilhd,imhd->ihlm', query_rot, keys_rot, precision=high))
    probs = low(jax.nn.softmax(scores, axis=-1))
    attended = jnp.einsum('ihlm,imhd->ilhd', probs, value, precision=high)
    attended = low(low_back(attended.reshape(images, length, width)))
    middle = inputs + low_back(jnp.einsum('ild,de->ile', attended, w_out, precision=high))
    mod_two = low_back(jnp.dot(conds, w_mod2, precision=high))
    normed_two = low(ada_norm(middle, mod_two))
    upward = low_back(jnp.einsum('ild,df->ilf', normed_two, w_up, precision=high))
    hidden = low(geglu_gate(upward))
    return middle + low_back(jnp.einsum('ilf,fd->ild', hidden, w_down, precision=high))

def reference(tokens, cond, sigma_idx, pos_rows, pos_cols, attn_scale, w_mod1, w_qkv, w_out, w_mod2, w_up, w_down, cotangent):
    group = 16
    blocks = IMAGES // group
    weights = tuple((w.astype(jnp.float32) for w in (w_mod1, w_qkv, w_out, w_mod2, w_up, w_down)))
    inputs = tokens.astype(jnp.float32).reshape(blocks, group, IMG_TOK, D)
    conds = cond.astype(jnp.float32).reshape(blocks, group, MAP)
    factor = sigma_weight(sigma_idx).reshape(blocks, group, 1, 1)
    grads_in = cotangent.astype(jnp.float32).reshape(blocks, group, IMG_TOK, D) * factor
    rows = pos_rows.reshape(blocks, group, IMG_TOK)
    cols = pos_cols.reshape(blocks, group, IMG_TOK)

    def one_step(carry, item):
        part_in, part_cond, part_rows, part_cols, part_grad = item

        def forward(values, conditions, scale, *mats):
            return block_layer(values, conditions, scale, *mats, part_rows, part_cols)
        result, backward = jax.vjp(forward, part_in, part_cond, attn_scale, *weights)
        grads = backward(part_grad)
        carry = tuple((c + g for c, g in zip(carry, grads[2:])))
        return (carry, (result.astype(jnp.bfloat16), grads[0].astype(jnp.bfloat16), grads[1]))
    start = (jnp.zeros_like(attn_scale),) + tuple((jnp.zeros_like(w) for w in weights))
    totals, (result, d_in, d_cond) = lax.scan(one_step, start, (inputs, conds, rows, cols, grads_in))
    return (result.reshape(TOKENS, D), d_in.reshape(TOKENS, D), d_cond.reshape(IMAGES, MAP), totals[0], totals[1], totals[2], totals[3], totals[4], totals[5], totals[6])
```

```python
import functools
import math

import jax
import jax.numpy as jnp
from jax import lax
from jax.experimental import pallas as pl
from jax.experimental.pallas import tpu as pltpu
from jax.sharding import PartitionSpec as P

GRID = 16
NB = 64

MESH = pl.DeviceIdType.MESH
CH = 512

def place():
    f, r = lax.axis_index("fsdp"), lax.axis_index("rep")
    return f // 2, f % 2, r // 2, r % 2

def is_c(i):
    return (i * 3) % 11 >= 11 - 3

def remote(src, dst, send, recv, z, x, y, c):
    return pltpu.make_async_remote_copy(src_ref=src, dst_ref=dst, send_sem=send, recv_sem=recv,
        device_id=(z * 2 + x, y * 2 + c), device_id_type=MESH)

def wait_bytes(ref, sem):
    pltpu.make_async_copy(ref, ref, sem).wait()

def enter(Z, z, x, y, c):
    barrier = pltpu.get_barrier_semaphore()
    for d in range(1, Z):
        pl.semaphore_signal(barrier, inc=1, device_id=((z + d) % Z * 2 + x, y * 2 + c), device_id_type=MESH)
    for where in ((z * 2 + 1 - x, y * 2 + c), (z * 2 + x, (1 - y) * 2 + c), (z * 2 + x, y * 2 + 1 - c)):
        pl.semaphore_signal(barrier, inc=1, device_id=where, device_id_type=MESH)
    pl.semaphore_wait(barrier, Z + 2)

def gather_ops(src, buf, sends, recvs, own):
    n, Z = buf.shape[0], buf.shape[1]
    z, x, y, c = place()
    zs, xs, ys, yt, cs, ct, cu, cv = (sends.at[k] for k in range(8))
    zr, xr, yr, yq, cr, cq, cp, co = (recvs.at[k] for k in range(8))
    def cols_of(width, k):
        return pl.ds(pl.multiple_of(k * width, 128), width)
    def both(i, fn):
        inside = (i >= 0) & (i < n)
        @pl.when(inside & jnp.logical_not(is_c(i)))
        def _(): fn(128, 2 * y + c, False)
        @pl.when(inside & is_c(i))
        def _(): fn(256, c, True)
    def stage_z(i):
        def go(width, k, cc):
            cols = cols_of(width, k)
            for d in range(1, Z):
                remote(src.at[i, :, cols], buf.at[i, z, x, :, cols], zs.at[i], zr.at[i], (z + d) % Z, x, y, c).start()
            remote(src.at[i, :, cols], buf.at[i, z, x, :, cols], xs.at[i], xr.at[i], z, 1 - x, y, c).start()
        both(i, go)
    def others(i, cols, send, recv, *to):
        for d in range(1, Z):
            zz = (z + d) % Z
            remote(buf.at[i, zz, x, :, cols], buf.at[i, zz, x, :, cols], send, recv, *to).start()
    def partner(i, cols, send, recv, *to):
        part = buf.at[i, :, 1 - x, :, cols]
        remote(part, part, send, recv, *to).start()
    def stage_x(i):
        def go(width, k, cc):
            cols = cols_of(width, k)
            wait_bytes(buf.at[i, 0:Z - 1, 0, :, cols], zr.at[i])
            others(i, cols, xs.at[i], xr.at[i], z, 1 - x, y, c)
            if not cc:
                others(i, cols, ys.at[i], yr.at[i], z, x, 1 - y, c)
            others(i, cols, cs.at[i], cr.at[i], z, x, y, 1 - c)
        both(i, go)
    def stage_y(i):
        def go(width, k, cc):
            cols = cols_of(width, k)
            wait_bytes(buf.at[i, :, 0, :, cols], xr.at[i])
            if not cc:
                partner(i, cols, yt.at[i], yq.at[i], z, x, 1 - y, c)
            partner(i, cols, ct.at[i], cq.at[i], z, x, y, 1 - c)
        both(i, go)
    def stage_c(i):
        def go(width, k, cc):
            if cc: return
            cols = cols_of(width, k)
            wait_bytes(buf.at[i, 0:Z - 1, 0, :, cols], yr.at[i])
            wait_bytes(buf.at[i, :, 0, :, cols], yq.at[i])
            mine = cols_of(128, 2 * (1 - y) + c)
            others(i, mine, cu.at[i], cp.at[i], z, x, y, 1 - c)
            partner(i, mine, cv.at[i], co.at[i], z, x, y, 1 - c)
        both(i, go)
    def core_waits(i, one, two, three, four):
        def go(width, k, cc):
            cols = pl.ds(0, width)
            wait_bytes(buf.at[i, 0:Z - 1, 0, :, cols], one.at[i])
            wait_bytes(buf.at[i, :, 0, :, cols], two.at[i])
            if not cc:
                wait_bytes(buf.at[i, 0:Z - 1, 0, :, cols], three.at[i])
                wait_bytes(buf.at[i, :, 0, :, cols], four.at[i])
        both(i, go)
    def ready(i):
        core_waits(i, cr, cq, cp, co)
    def finish():
        def body(i, _):
            def go(width, k, cc):
                cols = cols_of(width, k)
                wait_bytes(buf.at[i, 0:Z - 1, 0, :, cols], zs.at[i])
                wait_bytes(buf.at[i, :, 0, :, cols], xs.at[i])
                if not cc:
                    wait_bytes(buf.at[i, 0:Z - 1, 0, :, cols], ys.at[i])
                    wait_bytes(buf.at[i, :, 0, :, cols], yt.at[i])
            both(i, go)
            core_waits(i, cs, ct, cu, cv)
            return 0
        lax.fori_loop(0, n, body, 0)
    return stage_z, stage_x, stage_y, stage_c, ready, finish

LAG = (0, 2, 4, 6, 7)
def gather_kernel(lag, src, buf, sends, recvs, own):
    n, Z = buf.shape[0], buf.shape[1]
    z, x, y, c = place()
    enter(Z, z, x, y, c)
    keep = pltpu.make_async_copy(src, buf.at[:, z, x], own)
    keep.start()
    stage_z, stage_x, stage_y, stage_c, ready, finish = gather_ops(src, buf, sends, recvs, own)
    def body(t, _):
        stage_z(t - lag[0])
        stage_x(t - lag[1])
        stage_y(t - lag[2])
        stage_c(t - lag[3])
        ready(t - lag[4])
        return 0
    lax.fori_loop(0, n + lag[4], body, 0)
    keep.wait()
    finish()

def gather(src, F, lag=LAG, cid=0):
    n, R, w = src.shape
    return pl.pallas_call(functools.partial(gather_kernel, lag),
        out_shape=jax.ShapeDtypeStruct((n, F // 2, 2, R, w), src.dtype),
        in_specs=[pl.BlockSpec(memory_space=pltpu.HBM)], out_specs=pl.BlockSpec(memory_space=pltpu.HBM),
        scratch_shapes=[pltpu.SemaphoreType.DMA((8, n)), pltpu.SemaphoreType.DMA((8, n)), pltpu.SemaphoreType.DMA],
        compiler_params=pltpu.CompilerParams(collective_id=cid, has_side_effects=True))(src)

SLOTS = 4
def r_is_c(i):
    return (i * 5) % 11 >= 11 - 5

def lanes(k, width):
    return pl.ds(pl.multiple_of(k * width, 128), width)

def plus(a, b):
    return (a.astype(jnp.float32) + b.astype(jnp.float32)).astype(jnp.bfloat16)

def scatter_ops(n, g, rc, ry, rx, rz, rl, out, sends, recvs):
    Z = rc.shape[1]
    z, x, y, c = place()
    def both(i, fn_a, fn_c):
        inside = (i >= 0) & (i < n)
        @pl.when(inside & jnp.logical_not(r_is_c(i)))
        def _(): fn_a()
        @pl.when(inside & r_is_c(i))
        def _(): fn_c()
    def each(fn):
        lax.fori_loop(0, Z, lambda k, _: (fn(k), 0)[1], 0)
    def s0(i):
        @pl.when((i >= 0) & (i < n))
        def _():
            remote(g.at[i % SLOTS, :, :, :, lanes(1 - c, 256)], rc.at[i], sends.at[0, i], recvs.at[0, i], z, x, y, 1 - c).start()
    def free(i):
        @pl.when((i >= 0) & (i < n))
        def _(): wait_bytes(rc.at[i], sends.at[0, i])
    def s1(i):
        def add():
            wait_bytes(rc.at[i], recvs.at[0, i])
            def one(k):
                rc[i, k] = plus(rc[i, k], g[i % SLOTS, k, :, :, lanes(c, 256)])
            each(one)
        def a():
            add()
            remote(rc.at[i, :, :, :, lanes(1 - y, 128)], ry.at[i], sends.at[1, i], recvs.at[1, i], z, x, 1 - y, c).start()
        def cc():
            add()
            remote(rc.at[i, :, 1 - x], rx.at[i], sends.at[2, i], recvs.at[2, i], z, 1 - x, y, c).start()
        both(i, a, cc)
    def s2(i):
        def a():
            wait_bytes(ry.at[i], recvs.at[1, i])
            def one(k):
                ry[i, k] = plus(ry[i, k], rc[i, k, :, :, lanes(y, 128)])
            each(one)
            remote(ry.at[i, :, 1 - x], rx.at[i, :, :, pl.ds(0, 128)], sends.at[2, i], recvs.at[2, i], z, 1 - x, y, c).start()
        both(i, a, lambda: None)
    def s3(i):
        def a():
            wait_bytes(rx.at[i, :, :, pl.ds(0, 128)], recvs.at[2, i])
            def one(k):
                rx[i, k, :, 0:128] = plus(rx[i, k, :, 0:128], ry[i, k, x])
            each(one)
            for d in range(1, Z):
                zz = (z + d) % Z
                remote(rx.at[i, zz, :, pl.ds(0, 128)], rz.at[i, d - 1, :, pl.ds(0, 128)], sends.at[3, i], recvs.at[3, i], zz, x, y, c).start()
        def cc():
            wait_bytes(rx.at[i], recvs.at[2, i])
            def one(k):
                rx[i, k] = plus(rx[i, k], rc[i, k, x])
            each(one)
            for d in range(1, Z):
                zz = (z + d) % Z
                remote(rx.at[i, zz], rz.at[i, d - 1], sends.at[3, i], recvs.at[3, i], zz, x, y, c).start()
        both(i, a, cc)
    def s4(i):
        def total(part):
            s = rx[i, z, :, part].astype(jnp.float32)
            for d in range(1, Z):
                s = s + rz[i, d - 1, :, part].astype(jnp.float32)
            return s.astype(jnp.bfloat16)
        def a():
            wait_bytes(rz.at[i, :, :, pl.ds(0, 128)], recvs.at[3, i])
            mine = lanes(2 * c + y, 128)
            out[i, :, mine] = total(pl.ds(0, 128))
            remote(out.at[i, :, mine], out.at[i, :, mine], sends.at[4, i], recvs.at[4, i], z, x, 1 - y, c).start()
        def cc():
            wait_bytes(rz.at[i], recvs.at[3, i])
            out[i, :, lanes(c, 256)] = total(pl.ds(0, 256))
            remote(out.at[i, :, lanes(c, 256)], rl.at[i], sends.at[4, i], recvs.at[4, i], z, x, 1 - y, c).start()
        both(i, a, cc)
    def s5(i):
        mine = lanes(c, 256)
        def fwd():
            remote(out.at[i, :, mine], out.at[i, :, mine], sends.at[5, i], recvs.at[5, i], z, x, y, 1 - c).start()
        def a():
            wait_bytes(out.at[i, :, pl.ds(0, 128)], recvs.at[4, i])
            fwd()
        def cc():
            wait_bytes(rl.at[i], recvs.at[4, i])
            wait_bytes(rl.at[i], sends.at[4, i])
            out[i, :, mine] = plus(out[i, :, mine], rl[i])
            fwd()
        both(i, a, cc)
    def finish():
        def body(i, _):
            def a():
                wait_bytes(ry.at[i], sends.at[1, i])
                wait_bytes(rx.at[i, :, :, pl.ds(0, 128)], sends.at[2, i])
                wait_bytes(rz.at[i, :, :, pl.ds(0, 128)], sends.at[3, i])
                wait_bytes(out.at[i, :, pl.ds(0, 128)], sends.at[4, i])
            def cc():
                wait_bytes(rx.at[i], sends.at[2, i])
                wait_bytes(rz.at[i], sends.at[3, i])
            both(i, a, cc)
            wait_bytes(rl.at[i], sends.at[5, i])
            wait_bytes(rl.at[i], recvs.at[5, i])
            return 0
        lax.fori_loop(0, n, body, 0)
    return s0, free, s1, s2, s3, s4, s5, finish

RLAG = (0, 1, 3, 5, 7, 9)
def scatter_kernel(lag, gsrc, out, g, rc, ry, rx, rz, rl, sends, recvs, gs):
    n, Z = rc.shape[0], rc.shape[1]
    z, x, y, c = place()
    enter(Z, z, x, y, c)
    s0, free, s1, s2, s3, s4, s5, finish = scatter_ops(n, g, rc, ry, rx, rz, rl, out, sends, recvs)
    def load(i):
        @pl.when(i < n)
        def _(): pltpu.make_async_copy(gsrc.at[i], g.at[i % SLOTS], gs.at[i % SLOTS]).start()
    load(0)
    def body(t, _):
        free(t + 1 - SLOTS)
        load(t + 1)
        @pl.when(t < n)
        def _(): pltpu.make_async_copy(gsrc.at[t], g.at[t % SLOTS], gs.at[t % SLOTS]).wait()
        s0(t - lag[0])
        s1(t - lag[1])
        s2(t - lag[2])
        s3(t - lag[3])
        s4(t - lag[4])
        s5(t - lag[5])
        return 0
    lax.fori_loop(0, n + lag[5] + 1, body, 0)
    finish()

def scatter(gsrc, lag=RLAG, cid=1):
    n, Z, _, R, w = gsrc.shape
    B = jnp.bfloat16
    return pl.pallas_call(functools.partial(scatter_kernel, lag),
        out_shape=jax.ShapeDtypeStruct((n, R, w), B),
        in_specs=[pl.BlockSpec(memory_space=pltpu.HBM)], out_specs=pl.BlockSpec(memory_space=pltpu.VMEM),
        scratch_shapes=[pltpu.VMEM((SLOTS, Z, 2, R, w), B), pltpu.VMEM((n, Z, 2, R, w//2), B), pltpu.VMEM((n, Z, 2, R, w//4), B),
            pltpu.VMEM((n, Z, R, w//2), B), pltpu.VMEM((n, Z-1, R, w//2), B), pltpu.VMEM((n, R, w//2), B),
            pltpu.SemaphoreType.DMA((6, n)), pltpu.SemaphoreType.DMA((6, n)), pltpu.SemaphoreType.DMA((SLOTS,))],
        compiler_params=pltpu.CompilerParams(collective_id=cid, has_side_effects=True, vmem_limit_bytes=58*2**20))(gsrc)


EPS = 1e-06
LOW = jnp.bfloat16
FULL = jnp.float32
VMEM_LIMIT = 60 * 2**20
F_LAG = (0, 2, 3, 5, 6)
W_SLOTS = 3


def nn(a, b):
    return jnp.dot(a, b, preferred_element_type=FULL)


def nt(a, b):
    return lax.dot_general(a, b, (((1,), (1,)), ((), ())), preferred_element_type=FULL)


def tn(a, b):
    return lax.dot_general(a, b, (((0,), (0,)), ((), ())), preferred_element_type=FULL)


def at(k, size):
    return pl.ds(pl.multiple_of(k * size, size), size)


def head_sum(v):
    one = lax.broadcasted_iota(jnp.int32, (128, 128), 0) // 64
    two = lax.broadcasted_iota(jnp.int32, (128, 128), 1) // 64
    same = (one == two).astype(LOW)
    high = v.astype(LOW)
    rest = v - high.astype(FULL)
    return nn(high, same) + nn(rest.astype(LOW), same)


def head_mask(rows, second):
    lane = lax.broadcasted_iota(jnp.int32, (rows, 128), 1)
    return (lane >= 64) if second else (lane < 64)


def turn(v, cosine, sine_up, sine_down):
    return v * cosine + pltpu.roll(v, 16, 1) * sine_up + pltpu.roll(v, 112, 1) * sine_down


def norm_rows(src_ref, mods_ref, side, images, dst_ref, x_ref=None):
    rows, width = src_ref.shape
    length = rows // images
    block = 64
    def body(i, _):
        r = at(i, block)
        v = src_ref[r, :].astype(FULL)
        factor = lax.rsqrt(jnp.mean(v * v, axis=1, keepdims=True) + EPS)
        m = mods_ref[pl.ds(i // (length // block), 1), side * width : (side + 1) * width]
        dst_ref[r, :] = (v * factor * (1.0 + m)).astype(LOW)
        return 0
    lax.fori_loop(0, rows // block, body, 0)


def forward_kernel(
    images, tokens, cparts, wm, cosine, sine_up, sine_down, roots, src,
    buf, out, x1_o, qr_o, kr_o, vb_o, rq_o, rk_o, p_o, o_o, h_o, ga_o, gb_o, mods_o, call_o,
    n1, qkv, rqk, probs, att, x1, n2, hid, ga, gb, up, acc, slots, mods, call, mpart, mrecv,
    sends, recvs, own, wsem, osem, csem, msem, lsem,
):
    n, Z = buf.shape[0], buf.shape[1]
    shards = 2 * Z
    rows, width = tokens.shape
    length = rows // images
    half_heads = width // CH
    z, x, y, c = place()
    f = z * 2 + x
    r = y * 2 + c
    barrier = pltpu.get_barrier_semaphore()
    def greet(d, _):
        pl.semaphore_signal(barrier, inc=1, device_id=((f + d) % shards, r), device_id_type=MESH)
        return 0
    lax.fori_loop(1, shards, greet, 0)
    for where in ((f, (1 - y) * 2 + c), (f, y * 2 + 1 - c)):
        pl.semaphore_signal(barrier, inc=1, device_id=where, device_id_type=MESH)
    pl.semaphore_wait(barrier, shards + 1)
    keep = pltpu.make_async_copy(src, buf.at[:, z, x], own)
    keep.start()
    stage_z, stage_x, stage_y, stage_c, ready, finish = gather_ops(src, buf, sends, recvs, own)

    def give(d, _):
        to = (f + d) % shards
        pltpu.make_async_remote_copy(src_ref=cparts.at[to], dst_ref=call.at[f], send_sem=csem.at[0], recv_sem=csem.at[1],
            device_id=(to, r), device_id_type=MESH).start()
        return 0
    lax.fori_loop(1, shards, give, 0)
    call[f] = cparts[f]

    def load(j):
        return pltpu.make_async_copy(buf.at[j], slots.at[j % W_SLOTS], wsem.at[j % W_SLOTS])

    def step(t):
        stage_z(t - F_LAG[0])
        stage_x(t - F_LAG[1])
        stage_y(t - F_LAG[2])
        stage_c(t - F_LAG[3])
        ready(t - F_LAG[4])
        @pl.when((t >= F_LAG[4]) & (t < n + F_LAG[4]))
        def _(): load(t - F_LAG[4]).start()

    def begin(j):
        step(j + F_LAG[4] + 1)
        load(j).wait()
        return j % W_SLOTS

    def weights(slot):
        return slots[slot].reshape(width, CH)

    step(0)
    step(1)
    wait_bytes(call.at[pl.ds(0, shards - 1)], csem.at[1])
    flat = call[...].reshape(shards * call.shape[1], call.shape[2])
    mpart[...] = nn(flat, wm[...]).reshape(mpart.shape)
    def back(d, _):
        to = (f + d) % shards
        pltpu.make_async_remote_copy(src_ref=mpart.at[to, pl.ds(0, 8)], dst_ref=mrecv.at[f], send_sem=msem.at[0], recv_sem=msem.at[1],
            device_id=(to, r), device_id_type=MESH).start()
        return 0
    lax.fori_loop(1, shards, back, 0)
    mrecv[f] = mpart[f, 0:8]
    step(2)
    step(3)
    wait_bytes(mrecv.at[pl.ds(0, shards - 1)], msem.at[1])
    mods[...] = jnp.sum(mrecv[...], axis=0)
    norm_rows(tokens, mods, 0, images, n1)
    keep.wait()
    lax.fori_loop(4, F_LAG[4] + 1, lambda t, _: (step(t), 0)[1], 0)

    def project(half, _):
        lanes_of = lambda s: pl.ds(pl.multiple_of(half * CH + s * 128, 128), 128)
        for part in range(2):
            slot = begin(half * 3 + part)
            v = nn(n1[...], weights(slot))
            for s in range(CH // 128):
                one = v[:, s * 128 : (s + 1) * 128]
                scale = lax.rsqrt(head_sum(one * one) + EPS) * roots[0:1, lanes_of(s)]
                rqk[part, :, lanes_of(s)] = scale
                qkv[part, :, lanes_of(s)] = turn(one * scale, cosine[...], sine_up[...], sine_down[...]).astype(LOW)
        slot = begin(half * 3 + 2)
        qkv[2, :, at(half, CH)] = nn(n1[...], weights(slot)).astype(LOW)
        def pair(k, _):
            image, s = k // (CH // 128), k % (CH // 128)
            tok = at(image, length)
            lane = pl.ds(pl.multiple_of(half * CH + s * 128, 128), 128)
            q, keys, val = qkv[0, tok, lane], qkv[1, tok, lane], qkv[2, tok, lane]
            total = None
            for second in range(2):
                mask = head_mask(length, second)
                scores = jnp.exp(nt(jnp.where(mask, q, jnp.zeros_like(q)), keys))
                p = (scores * (1.0 / jnp.sum(scores, axis=1, keepdims=True))).astype(LOW)
                probs[half * (CH // 128) + s, image, second] = p
                o = nn(p, jnp.where(mask, val, jnp.zeros_like(val)))
                total = o if total is None else total + o
            att[tok, lane] = total.astype(LOW)
            return 0
        lax.fori_loop(0, images * (CH // 128), pair, 0)
        return 0
    lax.fori_loop(0, half_heads, project, 0)
    outs = [
        (qkv.at[0], qr_o), (qkv.at[1], kr_o), (qkv.at[2], vb_o), (rqk.at[0], rq_o), (rqk.at[1], rk_o), (probs, p_o), (att, o_o),
        (mods, mods_o), (call, call_o),
    ]
    later = [(x1, x1_o), (hid, h_o), (ga, ga_o), (gb, gb_o), (n2, out)]
    copies = [pltpu.make_async_copy(a, b, osem.at[k]) for k, (a, b) in enumerate(outs + later)]
    for k in range(len(outs)):
        copies[k].start()

    at_out = 3 * half_heads
    def project_out(j, _):
        slot = begin(at_out + j)
        lane = at(j, CH)
        x1[:, lane] = tokens[:, lane].astype(FULL) + nn(att[...], weights(slot))
        return 0
    lax.fori_loop(0, half_heads, project_out, 0)
    copies[len(outs)].start()
    norm_rows(x1, mods, 1, images, n2)

    at_up = at_out + half_heads
    def widen(j, _):
        up[...] = nn(n2[...], weights(begin(at_up + 2 * j)))
        gate = nn(n2[...], weights(begin(at_up + 2 * j + 1)))
        lane_of = lambda s: pl.ds(pl.multiple_of(j * CH + s * 128, 128), 128)
        for s in range(CH // 128):
            g = gate[:, s * 128 : (s + 1) * 128]
            u = up[:, s * 128 : (s + 1) * 128]
            phi = 0.5 + 0.5 * lax.erf(g * math.sqrt(0.5))
            gelu = g * phi
            slope = phi + g * (jnp.exp(-0.5 * g * g) * (1.0 / math.sqrt(2.0 * math.pi)))
            hid[:, lane_of(s)] = (u * gelu).astype(LOW)
            ga[:, lane_of(s)] = gelu.astype(LOW)
            gb[:, lane_of(s)] = (u * slope).astype(LOW)
        return 0
    hidden = hid.shape[1]
    lax.fori_loop(0, hidden // CH, widen, 0)
    for k in range(1, 4):
        copies[len(outs) + k].start()

    at_down = at_up + 2 * hidden // CH
    def narrow(k, _):
        for j in range(width // CH):
            slot = begin(at_down + k * (width // CH) + j)
            part = nn(hid[:, at(k, width)], weights(slot))
            cols = slice(j * CH, (j + 1) * CH)
            acc[:, cols] = part + jnp.where(k == 0, x1[:, cols], acc[:, cols])
        return 0
    lax.fori_loop(0, hidden // width, narrow, 0)
    n2[...] = acc[...].astype(LOW)
    copies[-1].start()
    for copy in copies:
        copy.wait()
    finish()
    wait_bytes(call.at[pl.ds(0, shards - 1)], csem.at[0])
    wait_bytes(mrecv.at[pl.ds(0, shards - 1)], msem.at[0])


def forward(tokens, cparts, wm, tables, roots, src, shards, images, hidden):
    rows, width = tokens.shape
    n, R, w = src.shape
    Z = shards // 2
    length = rows // images
    pairs = width // 128
    def array(shape, kind):
        return jax.ShapeDtypeStruct(shape, kind)
    wide = (rows, width)
    out_shape = (
        array((n, Z, 2, R, w), LOW), array(wide, LOW), array(wide, FULL), array(wide, LOW), array(wide, LOW), array(wide, LOW),
        array(wide, FULL), array(wide, FULL), array((pairs, images, 2, length, length), LOW), array(wide, LOW),
        array((rows, hidden), LOW), array((rows, hidden), LOW), array((rows, hidden), LOW), array((8, 2 * width), FULL),
        array(cparts.shape, LOW),
    )
    vm = lambda *shape_kind: pltpu.VMEM(*shape_kind)
    scratch = [
        vm(wide, LOW), vm((3, *wide), LOW), vm((2, *wide), FULL), vm((pairs, images, 2, length, length), LOW), vm(wide, LOW),
        vm(wide, FULL), vm(wide, LOW), vm((rows, hidden), LOW), vm((rows, hidden), LOW), vm((rows, hidden), LOW),
        vm((rows, w), FULL), vm(wide, FULL), vm((W_SLOTS, Z, 2, R, w), LOW), vm((8, 2 * width), FULL), vm(cparts.shape, LOW),
        vm((shards, cparts.shape[1], 2 * width), FULL), vm((shards, 8, 2 * width), FULL),
        pltpu.SemaphoreType.DMA((8, n)), pltpu.SemaphoreType.DMA((8, n)), pltpu.SemaphoreType.DMA,
        pltpu.SemaphoreType.DMA((W_SLOTS,)), pltpu.SemaphoreType.DMA((14,)), pltpu.SemaphoreType.DMA((2,)),
        pltpu.SemaphoreType.DMA((2,)), pltpu.SemaphoreType.DMA,
    ]
    hbm, vmem = pl.BlockSpec(memory_space=pltpu.HBM), pl.BlockSpec(memory_space=pltpu.VMEM)
    return pl.pallas_call(
        functools.partial(forward_kernel, images),
        out_shape=out_shape,
        in_specs=[vmem] * 7 + [hbm],
        out_specs=tuple([hbm] * len(out_shape)),
        scratch_shapes=scratch,
        compiler_params=pltpu.CompilerParams(collective_id=0, has_side_effects=True, vmem_limit_bytes=VMEM_LIMIT),
    )(tokens, cparts, wm, *tables, roots, src)


def prepare(tokens, cond, pos_rows, pos_cols, attn_scale, w_mod1, w_qkv, w_out, w_mod2, w_up, w_down, shards):
    rows, width = w_qkv.shape[0], tokens.shape[1]
    per = width // CH
    blocks = w_down.shape[0] // rows
    qkv = w_qkv.reshape(rows, 3, per, CH).transpose(2, 1, 0, 3).reshape(-1, rows, CH)
    out = w_out.reshape(rows, per, CH).transpose(1, 0, 2)
    up = w_up.reshape(rows, 2, shards, blocks, rows).transpose(0, 1, 3, 2, 4)
    up = up.reshape(rows, 2, -1, CH).transpose(2, 1, 0, 3).reshape(-1, rows, CH)
    down = w_down.reshape(blocks, rows, per, CH).transpose(0, 2, 1, 3).reshape(-1, rows, CH)
    src = jnp.concatenate([qkv, out, up, down])
    images, wide = cond.shape
    own = wide // shards
    cparts = cond.reshape(images, shards, own).transpose(1, 0, 2)
    cparts = jnp.pad(cparts, ((0, 0), (0, 16 - images), (0, 128 - own)))
    wm = jnp.pad(jnp.concatenate([w_mod1, w_mod2], axis=1), ((0, 128 - own), (0, 0)))
    head = width // attn_scale.shape[0]
    roots = jnp.broadcast_to(jnp.repeat(jnp.sqrt(attn_scale), head)[None], (8, width))
    turned = head // 2
    quarter = turned // 4
    steps = jnp.arange(quarter, dtype=FULL)
    freqs = math.pi * jnp.exp(math.log(10.0) * steps / max(quarter - 1, 1))
    row_pos = (pos_rows.astype(FULL) + 0.5) * (2.0 / GRID) - 1.0
    col_pos = (pos_cols.astype(FULL) + 0.5) * (2.0 / GRID) - 1.0
    angles = jnp.concatenate([row_pos[:, None] * freqs, col_pos[:, None] * freqs], axis=1)
    cos, sin = jnp.cos(angles), jnp.sin(angles)
    zero, rest = jnp.zeros_like(sin), jnp.zeros((sin.shape[0], head - turned), FULL)
    def pair(*parts):
        one = jnp.concatenate(parts, axis=1)
        return jnp.concatenate([one, one], axis=1)
    tables = (pair(cos, cos, rest + 1.0), pair(zero, sin, rest), pair(-sin, zero, rest))
    return src, cparts, wm, roots, tables


def split_chunks(w_qkv, w_out, w_up, w_down):
    rows = w_qkv.shape[0]
    def across(w):
        return w.reshape(rows, -1, CH).transpose(1, 0, 2)
    qkv, out, up = across(w_qkv), across(w_out), across(w_up)
    heads = qkv.shape[0] // 3
    qkv = qkv.reshape(3, heads, rows, CH).transpose(1, 0, 2, 3).reshape(-1, rows, CH)
    half = up.shape[0] // 2
    up = up.reshape(2, half, rows, CH).transpose(1, 0, 2, 3).reshape(-1, rows, CH)
    down = w_down.reshape(-1, rows, w_down.shape[1] // CH, CH).transpose(0, 2, 1, 3).reshape(-1, rows, CH)
    return jnp.concatenate([qkv, out, up, down])


def join_chunks(chunks, width, hidden):
    lead = chunks.shape[1:-2]
    rows = chunks.shape[-2]
    per = width // CH
    sizes = [3 * per, per, 2 * hidden // CH]
    qkv, out, up, down = jnp.split(chunks, [sizes[0], sizes[0] + sizes[1], sum(sizes)])
    qkv = jnp.swapaxes(qkv.reshape(per, 3, *qkv.shape[1:]), 0, 1).reshape(qkv.shape)
    up = jnp.swapaxes(up.reshape(-1, 2, *up.shape[1:]), 0, 1).reshape(up.shape)
    def across(w):
        w = jnp.moveaxis(w, 0, -2)
        return w.reshape(math.prod(lead) * rows, -1)
    parts = down.shape[0] // per
    down = down.reshape(parts, per, *down.shape[1:])
    down = jnp.moveaxis(jnp.moveaxis(down, 1, -2), 0, len(lead))
    down = down.reshape(math.prod(lead) * parts * rows, -1)
    return across(qkv), across(out), across(up), down


def cut_grads(g_qkv, g_out, g_up, g_down, shards):
    width, hidden = g_out.shape[1], g_down.shape[0]
    rows = width // shards
    per = width // CH
    def across(g):
        return g.reshape(shards, rows, -1, CH).transpose(2, 0, 1, 3)
    qkv, out, up = across(g_qkv), across(g_out), across(g_up)
    qkv = jnp.swapaxes(qkv.reshape(3, per, *qkv.shape[1:]), 0, 1).reshape(qkv.shape)
    up = jnp.swapaxes(up.reshape(2, -1, *up.shape[1:]), 0, 1).reshape(up.shape)
    down = g_down.reshape(shards, -1, rows, per, CH).transpose(1, 3, 0, 2, 4).reshape(-1, shards, rows, CH)
    chunks = jnp.concatenate([qkv, out, up, down])[::-1]
    return chunks.reshape(-1, shards // 2, 2, rows, CH)


def sigma_weight(bucket):
    level = bucket.astype(jnp.float32) / (NB - 1)
    sigma = jnp.exp(-2.0 + 3.2 * level)
    return 1.0 / (1.0 + 4.0 * sigma * sigma) + 0.25


def ada_norm(values, modulation):
    factor = lax.rsqrt(jnp.mean(values * values, axis=-1, keepdims=True) + 1e-06)
    return values * factor * (1.0 + modulation)[:, None, :]


def axial_rope(values, rows, cols):
    head_dim = values.shape[-1]
    turned = head_dim // 2
    pairs = turned // 2
    quarter = pairs // 2
    steps = jnp.arange(quarter, dtype=jnp.float32)
    freqs = math.pi * jnp.exp(math.log(10.0) * steps / max(quarter - 1, 1))
    row_pos = (rows.astype(jnp.float32) + 0.5) * (2.0 / GRID) - 1.0
    col_pos = (cols.astype(jnp.float32) + 0.5) * (2.0 / GRID) - 1.0
    angles = jnp.concatenate([row_pos[..., None] * freqs, col_pos[..., None] * freqs], axis=-1)
    cosine = jnp.cos(angles)[:, :, None, :]
    sine = jnp.sin(angles)[:, :, None, :]
    first = values[..., :pairs]
    second = values[..., pairs:turned]
    rest = values[..., turned:]
    return jnp.concatenate(
        [first * cosine - second * sine, first * sine + second * cosine, rest], axis=-1
    )


def cosine_rope(query, keys, scale, rows, cols):
    root = jnp.sqrt(scale)[None, None, :, None]
    query_n = query * lax.rsqrt(jnp.sum(query * query, axis=-1, keepdims=True) + 1e-06) * root
    keys_n = keys * lax.rsqrt(jnp.sum(keys * keys, axis=-1, keepdims=True) + 1e-06) * root
    return (axial_rope(query_n, rows, cols), axial_rope(keys_n, rows, cols))


def geglu_gate(upward):
    hidden = upward.shape[-1] // 2
    return upward[..., :hidden] * jax.nn.gelu(upward[..., hidden:], approximate=False)


def attn_probs(query_low, keys_low, log_total):
    scores = jnp.einsum("ilhd,imhd->ihlm", query_low, keys_low, preferred_element_type=jnp.float32)
    return jnp.exp(scores - log_total[..., None])


def local(
    tokens,
    cond,
    sigma_idx,
    pos_rows,
    pos_cols,
    attn_scale,
    w_mod1,
    w_qkv,
    w_out,
    w_mod2,
    w_up,
    w_down,
    cotangent,
):
    images = cond.shape[0]
    total_rows = tokens.shape[0]
    length = total_rows // images
    width = tokens.shape[1]
    heads = attn_scale.shape[0]
    head_dim = width // heads
    shards = lax.axis_size("fsdp")
    width_own, hidden = tokens.shape[1], w_down.shape[0] * shards
    fs = lax.axis_index("fsdp")
    map_rows = w_mod1.shape[0]
    src, cparts, wm, roots, tables = prepare(tokens, cond, pos_rows, pos_cols, attn_scale, w_mod1, w_qkv, w_out, w_mod2, w_up, w_down, shards)
    (chunks, result, x1, qr, kr, vb, rq, rk, probs, att, h_p, ga_p, gb_p, mods, call) = forward(tokens, cparts, wm, tables, roots, src, shards, images, hidden)
    full_qkv, full_out, full_up, full_down = join_chunks(
        chunks.reshape(chunks.shape[0], shards, *chunks.shape[3:]), width_own, hidden
    )
    blocks = hidden // width_own
    def unperm(v):
        return v.reshape(-1, blocks, shards, width_own // shards).transpose(0, 2, 1, 3).reshape(-1, hidden)
    back_qkv, back_out, back_down = full_qkv, full_out, full_down
    back_up = jnp.concatenate([unperm(full_up[:, :hidden]), unperm(full_up[:, hidden:])], axis=1)
    hidden_low, ga, gb = unperm(h_p), unperm(ga_p), unperm(gb_p)
    mod_one, mod_two = mods[:images, :width_own], mods[:images, width_own:]
    inputs = tokens.astype(jnp.float32).reshape(images, length, width)
    normed = ada_norm(inputs, mod_one).astype(jnp.bfloat16).reshape(total_rows, width)
    middle = x1.reshape(images, length, width)
    normed_two = ada_norm(middle, mod_two).astype(jnp.bfloat16).reshape(total_rows, width)
    attended_low = att
    rows = pos_rows.reshape(images, length)
    cols = pos_cols.reshape(images, length)
    project = jnp.dot(normed, full_qkv, preferred_element_type=jnp.float32).reshape(images, length, 3 * width)
    query = project[..., :width].reshape(images, length, heads, head_dim)
    keys = project[..., width : 2 * width].reshape(images, length, heads, head_dim)
    value_low = vb.reshape(images, length, heads, head_dim)
    query_low = qr.reshape(images, length, heads, head_dim)
    keys_low = kr.reshape(images, length, heads, head_dim)
    factor = sigma_weight(sigma_idx)
    grad_out = cotangent.astype(jnp.float32).reshape(images, length, width) * factor[:, None, None]
    down_low = grad_out.reshape(total_rows, width).astype(jnp.bfloat16)
    grad_down = jnp.einsum("tf,td->fd", hidden_low, down_low, preferred_element_type=jnp.float32)
    grad_hidden = jnp.einsum("td,fd->tf", down_low, back_down, preferred_element_type=jnp.float32)
    upward_low = jnp.concatenate([grad_hidden * ga.astype(FULL), grad_hidden * gb.astype(FULL)], axis=1).astype(jnp.bfloat16)
    grad_up = jnp.einsum("td,tf->df", normed_two, upward_low, preferred_element_type=jnp.float32)
    grad_normed_two = jnp.einsum(
        "tf,df->td", upward_low, back_up, preferred_element_type=jnp.float32
    )
    unused, norm_back_two = jax.vjp(ada_norm, middle, mod_two)
    grad_mid_norm, grad_mod_two = norm_back_two(grad_normed_two.reshape(images, length, width))
    grad_middle = grad_out + grad_mid_norm
    mod_two_low = grad_mod_two.astype(jnp.bfloat16)
    proj_low = grad_middle.reshape(total_rows, width).astype(jnp.bfloat16)
    grad_outw = jnp.einsum("td,te->de", attended_low, proj_low, preferred_element_type=jnp.float32)
    grad_att = jnp.einsum("te,de->td", proj_low, back_out, preferred_element_type=jnp.float32)
    att_low = grad_att.astype(jnp.bfloat16).reshape(images, length, heads, head_dim)
    probs = probs.transpose(1, 0, 2, 3, 4).reshape(images, heads, length, length).astype(FULL)
    grad_probs = jnp.einsum(
        "ilhd,imhd->ihlm", att_low, value_low, preferred_element_type=jnp.float32
    )
    grad_value = jnp.einsum(
        "ihlm,ilhd->imhd", probs.astype(jnp.bfloat16), att_low, preferred_element_type=jnp.float32
    )
    score_low = (probs * (grad_probs - jnp.sum(grad_probs * probs, axis=-1, keepdims=True))).astype(
        jnp.bfloat16
    )
    grad_qrot = jnp.einsum(
        "ihlm,imhd->ilhd", score_low, keys_low, preferred_element_type=jnp.float32
    )
    grad_krot = jnp.einsum(
        "ihlm,ilhd->imhd", score_low, query_low, preferred_element_type=jnp.float32
    )

    def rotary_part(query_in, keys_in, scale_in):
        return cosine_rope(query_in, keys_in, scale_in, rows, cols)

    unused, rope_back = jax.vjp(rotary_part, query, keys, attn_scale)
    grad_query, grad_keys, grad_scale = rope_back((grad_qrot, grad_krot))
    qkv_low = jnp.concatenate(
        [
            grad_query.reshape(total_rows, width),
            grad_keys.reshape(total_rows, width),
            grad_value.reshape(total_rows, width),
        ],
        axis=1,
    ).astype(jnp.bfloat16)
    grad_qkvw = jnp.einsum("td,te->de", normed, qkv_low, preferred_element_type=jnp.float32)
    grad_normed = jnp.einsum("te,de->td", qkv_low, back_qkv, preferred_element_type=jnp.float32)
    unused, norm_back_one = jax.vjp(ada_norm, inputs, mod_one)
    grad_in_norm, grad_mod_one = norm_back_one(grad_normed.reshape(images, length, width))
    grad_tokens = (grad_middle + grad_in_norm).reshape(total_rows, width).astype(jnp.bfloat16)
    mod_one_low = grad_mod_one.astype(jnp.bfloat16)
    low = jnp.bfloat16
    grads = cut_grads(grad_qkvw.astype(low), grad_outw.astype(low), grad_up.astype(low), grad_down.astype(low), shards)
    summed = scatter(grads)[::-1].astype(jnp.float32)
    g_qkv, g_out, g_up, g_down = join_chunks(summed, width_own, hidden)
    small = jnp.concatenate([cond, mod_one_low, mod_two_low], axis=1)
    everyone = lax.all_gather(small, ("fsdp", "rep"), axis=0, tiled=True)
    wide = cond.shape[1]
    cond_rows = lax.dynamic_slice_in_dim(everyone[:, :wide], fs * map_rows, map_rows, 1)
    g_mod = lax.dot_general(cond_rows, everyone[:, wide:], (((0,), (0,)), ((), ())), preferred_element_type=jnp.float32)
    g_mod1, g_mod2 = g_mod[:, :width_own], g_mod[:, width_own:]
    rep = lax.axis_index("rep")
    group = everyone[:, wide:].reshape(shards, -1, images, 2 * width_own)
    group = lax.dynamic_index_in_dim(group, rep, 1, keepdims=False)
    d_part = jnp.einsum("fid,cd->fic", group, jnp.concatenate([w_mod1, w_mod2], axis=1), preferred_element_type=jnp.float32)
    grad_cond = lax.all_to_all(d_part, "fsdp", 0, 0, tiled=False)
    grad_cond = jnp.swapaxes(grad_cond, 0, 1).reshape(images, wide)
    scale_total = lax.psum(grad_scale, ("fsdp", "rep"))
    return (
        result,
        grad_tokens,
        grad_cond,
        scale_total,
        g_mod1,
        g_qkv,
        g_out,
        g_mod2,
        g_up,
        g_down,
    )


def solution(mesh):
    placed = (
        P(("fsdp", "rep"), None),
        P(("fsdp", "rep"), None),
        P(("fsdp", "rep")),
        P(("fsdp", "rep")),
        P(("fsdp", "rep")),
        P(),
        P("fsdp", None),
        P("fsdp", None),
        P("fsdp", None),
        P("fsdp", None),
        P("fsdp", None),
        P("fsdp", None),
        P(("fsdp", "rep"), None),
    )
    return jax.shard_map(
        local,
        mesh=mesh,
        in_specs=placed,
        out_specs=(
            P(("fsdp", "rep"), None),
            P(("fsdp", "rep"), None),
            P(("fsdp", "rep"), None),
            P(),
            P("fsdp", None),
            P("fsdp", None),
            P("fsdp", None),
            P("fsdp", None),
            P("fsdp", None),
            P("fsdp", None),
        ),
        check_vma=False,
    )
```

```python
import functools
import math

import jax
import jax.numpy as jnp
from jax import lax
from jax.experimental import pallas as pl
from jax.experimental.pallas import tpu as pltpu
from jax.sharding import PartitionSpec as P

GRID = 16
NB = 64

MESH = pl.DeviceIdType.MESH
CH = 512

def place():
    f, r = lax.axis_index("fsdp"), lax.axis_index("rep")
    return f // 2, f % 2, r // 2, r % 2

def is_c(i):
    return (i * 3) % 11 >= 11 - 3

def remote(src, dst, send, recv, z, x, y, c):
    return pltpu.make_async_remote_copy(src_ref=src, dst_ref=dst, send_sem=send, recv_sem=recv,
        device_id=(z * 2 + x, y * 2 + c), device_id_type=MESH)

def wait_bytes(ref, sem):
    pltpu.make_async_copy(ref, ref, sem).wait()

def gather_ops(src, buf, sends, recvs, own):
    n, Z = buf.shape[0], buf.shape[1]
    z, x, y, c = place()
    zs, xs, ys, yt, cs, ct, cu, cv = (sends.at[k] for k in range(8))
    zr, xr, yr, yq, cr, cq, cp, co = (recvs.at[k] for k in range(8))
    def cols_of(width, k):
        return pl.ds(pl.multiple_of(k * width, 128), width)
    def both(i, fn):
        inside = (i >= 0) & (i < n)
        @pl.when(inside & jnp.logical_not(is_c(i)))
        def _(): fn(128, 2 * y + c, False)
        @pl.when(inside & is_c(i))
        def _(): fn(256, c, True)
    def keep(i):
        return pltpu.make_async_copy(src.at[i], buf.at[i, z, x], own.at[i])
    def stage_z(i):
        @pl.when((i >= 0) & (i < n))
        def _(): keep(i).start()
        def go(width, k, cc):
            cols = cols_of(width, k)
            for d in range(1, Z):
                remote(src.at[i, :, cols], buf.at[i, z, x, :, cols], zs.at[i], zr.at[i], (z + d) % Z, x, y, c).start()
            remote(src.at[i, :, cols], buf.at[i, z, x, :, cols], xs.at[i], xr.at[i], z, 1 - x, y, c).start()
        both(i, go)
    def others(i, cols, send, recv, *to):
        for d in range(1, Z):
            zz = (z + d) % Z
            remote(buf.at[i, zz, x, :, cols], buf.at[i, zz, x, :, cols], send, recv, *to).start()
    def partner(i, cols, send, recv, *to):
        part = buf.at[i, :, 1 - x, :, cols]
        remote(part, part, send, recv, *to).start()
    def stage_x(i):
        def go(width, k, cc):
            cols = cols_of(width, k)
            wait_bytes(buf.at[i, 0:Z - 1, 0, :, cols], zr.at[i])
            others(i, cols, xs.at[i], xr.at[i], z, 1 - x, y, c)
            if not cc:
                others(i, cols, ys.at[i], yr.at[i], z, x, 1 - y, c)
            others(i, cols, cs.at[i], cr.at[i], z, x, y, 1 - c)
        both(i, go)
    def stage_y(i):
        def go(width, k, cc):
            cols = cols_of(width, k)
            wait_bytes(buf.at[i, :, 0, :, cols], xr.at[i])
            if not cc:
                partner(i, cols, yt.at[i], yq.at[i], z, x, 1 - y, c)
            partner(i, cols, ct.at[i], cq.at[i], z, x, y, 1 - c)
        both(i, go)
    def stage_c(i):
        def go(width, k, cc):
            if cc: return
            cols = cols_of(width, k)
            wait_bytes(buf.at[i, 0:Z - 1, 0, :, cols], yr.at[i])
            wait_bytes(buf.at[i, :, 0, :, cols], yq.at[i])
            mine = cols_of(128, 2 * (1 - y) + c)
            others(i, mine, cu.at[i], cp.at[i], z, x, y, 1 - c)
            partner(i, mine, cv.at[i], co.at[i], z, x, y, 1 - c)
        both(i, go)
    def core_waits(i, one, two, three, four):
        def go(width, k, cc):
            cols = pl.ds(0, width)
            wait_bytes(buf.at[i, 0:Z - 1, 0, :, cols], one.at[i])
            wait_bytes(buf.at[i, :, 0, :, cols], two.at[i])
            if not cc:
                wait_bytes(buf.at[i, 0:Z - 1, 0, :, cols], three.at[i])
                wait_bytes(buf.at[i, :, 0, :, cols], four.at[i])
        both(i, go)
    def ready(i):
        @pl.when((i >= 0) & (i < n))
        def _(): keep(i).wait()
        core_waits(i, cr, cq, cp, co)
    def finish():
        def body(i, _):
            def go(width, k, cc):
                cols = cols_of(width, k)
                wait_bytes(buf.at[i, 0:Z - 1, 0, :, cols], zs.at[i])
                wait_bytes(buf.at[i, :, 0, :, cols], xs.at[i])
                if not cc:
                    wait_bytes(buf.at[i, 0:Z - 1, 0, :, cols], ys.at[i])
                    wait_bytes(buf.at[i, :, 0, :, cols], yt.at[i])
            both(i, go)
            core_waits(i, cs, ct, cu, cv)
            return 0
        lax.fori_loop(0, n, body, 0)
    return stage_z, stage_x, stage_y, stage_c, ready, finish


EPS = 1e-06
LOW = jnp.bfloat16
FULL = jnp.float32
VMEM_LIMIT = 60 * 2**20
F_LAG = (0, 2, 3, 5, 6)
W_SLOTS = 3


def nn(a, b):
    return jnp.dot(a, b, preferred_element_type=FULL)


def nt(a, b):
    return lax.dot_general(a, b, (((1,), (1,)), ((), ())), preferred_element_type=FULL)


def tn(a, b):
    return lax.dot_general(a, b, (((0,), (0,)), ((), ())), preferred_element_type=FULL)


def at(k, size):
    return pl.ds(pl.multiple_of(k * size, size), size)


def head_sum(v):
    one = lax.broadcasted_iota(jnp.int32, (128, 128), 0) // 64
    two = lax.broadcasted_iota(jnp.int32, (128, 128), 1) // 64
    same = (one == two).astype(LOW)
    high = v.astype(LOW)
    rest = v - high.astype(FULL)
    return nn(high, same) + nn(rest.astype(LOW), same)


def head_mask(rows, second):
    lane = lax.broadcasted_iota(jnp.int32, (rows, 128), 1)
    return (lane >= 64) if second else (lane < 64)


def turn(v, cosine, sine_up, sine_down):
    return v * cosine + pltpu.roll(v, 16, 1) * sine_up + pltpu.roll(v, 112, 1) * sine_down


def norm_rows(src_ref, mods_ref, side, images, dst_ref, x_ref=None):
    rows, width = src_ref.shape
    length = rows // images
    block = 64
    def body(i, _):
        r = at(i, block)
        v = src_ref[r, :].astype(FULL)
        factor = lax.rsqrt(jnp.mean(v * v, axis=1, keepdims=True) + EPS)
        m = mods_ref[pl.ds(i // (length // block), 1), side * width : (side + 1) * width]
        dst_ref[r, :] = (v * factor * (1.0 + m)).astype(LOW)
        return 0
    lax.fori_loop(0, rows // block, body, 0)


def forward_kernel(
    images, tokens, cparts, wm, cosine, sine_up, sine_down, roots, src,
    buf, out, x1_o, qr_o, kr_o, vb_o, rq_o, rk_o, p_o, o_o, h_o, ga_o, gb_o, mods_o, call_o,
    n1, qkv, rqk, probs, att, x1, n2, hid, ga, gb, up, acc, slots, mods, call, mpart, mrecv,
    sends, recvs, own, wsem, osem, csem, msem, lsem,
):
    n, Z = buf.shape[0], buf.shape[1]
    shards = 2 * Z
    rows, width = tokens.shape
    length = rows // images
    half_heads = width // CH
    z, x, y, c = place()
    f = z * 2 + x
    r = y * 2 + c
    barrier = pltpu.get_barrier_semaphore()
    def greet(d, _):
        pl.semaphore_signal(barrier, inc=1, device_id=((f + d) % shards, r), device_id_type=MESH)
        return 0
    lax.fori_loop(1, shards, greet, 0)
    for where in ((f, (1 - y) * 2 + c), (f, y * 2 + 1 - c)):
        pl.semaphore_signal(barrier, inc=1, device_id=where, device_id_type=MESH)
    pl.semaphore_wait(barrier, shards + 1)
    stage_z, stage_x, stage_y, stage_c, ready, finish = gather_ops(src, buf, sends, recvs, own)

    def give(d, _):
        to = (f + d) % shards
        pltpu.make_async_remote_copy(src_ref=cparts.at[to], dst_ref=call.at[f], send_sem=csem.at[0], recv_sem=csem.at[1],
            device_id=(to, r), device_id_type=MESH).start()
        return 0
    lax.fori_loop(1, shards, give, 0)
    call[f] = cparts[f]

    def load(j):
        return pltpu.make_async_copy(buf.at[j], slots.at[j % W_SLOTS], wsem.at[j % W_SLOTS])

    def step(t):
        stage_z(t - F_LAG[0])
        stage_x(t - F_LAG[1])
        stage_y(t - F_LAG[2])
        stage_c(t - F_LAG[3])
        ready(t - F_LAG[4])
        @pl.when((t >= F_LAG[4]) & (t < n + F_LAG[4]))
        def _(): load(t - F_LAG[4]).start()

    def begin(j):
        step(j + F_LAG[4] + 1)
        load(j).wait()
        return j % W_SLOTS

    def weights(slot):
        return slots[slot].reshape(width, CH)

    step(0)
    step(1)
    wait_bytes(call.at[pl.ds(0, shards - 1)], csem.at[1])
    flat = call[...].reshape(shards * call.shape[1], call.shape[2])
    mpart[...] = nn(flat, wm[...]).reshape(mpart.shape)
    def back(d, _):
        to = (f + d) % shards
        pltpu.make_async_remote_copy(src_ref=mpart.at[to, pl.ds(0, 8)], dst_ref=mrecv.at[f], send_sem=msem.at[0], recv_sem=msem.at[1],
            device_id=(to, r), device_id_type=MESH).start()
        return 0
    lax.fori_loop(1, shards, back, 0)
    mrecv[f] = mpart[f, 0:8]
    step(2)
    step(3)
    wait_bytes(mrecv.at[pl.ds(0, shards - 1)], msem.at[1])
    mods[...] = jnp.sum(mrecv[...], axis=0)
    norm_rows(tokens, mods, 0, images, n1)
    lax.fori_loop(4, F_LAG[4] + 1, lambda t, _: (step(t), 0)[1], 0)

    def project(half, _):
        lanes_of = lambda s: pl.ds(pl.multiple_of(half * CH + s * 128, 128), 128)
        for part in range(2):
            slot = begin(half * 3 + part)
            v = nn(n1[...], weights(slot))
            for s in range(CH // 128):
                one = v[:, s * 128 : (s + 1) * 128]
                scale = lax.rsqrt(head_sum(one * one) + EPS) * roots[0:1, lanes_of(s)]
                rqk[part, :, lanes_of(s)] = scale
                qkv[part, :, lanes_of(s)] = turn(one * scale, cosine[...], sine_up[...], sine_down[...]).astype(LOW)
        slot = begin(half * 3 + 2)
        qkv[2, :, at(half, CH)] = nn(n1[...], weights(slot)).astype(LOW)
        def pair(k, _):
            image, s = k // (CH // 128), k % (CH // 128)
            tok = at(image, length)
            lane = pl.ds(pl.multiple_of(half * CH + s * 128, 128), 128)
            q, keys, val = qkv[0, tok, lane], qkv[1, tok, lane], qkv[2, tok, lane]
            total = None
            for second in range(2):
                mask = head_mask(length, second)
                scores = jnp.exp(nt(jnp.where(mask, q, jnp.zeros_like(q)), keys))
                p = (scores * (1.0 / jnp.sum(scores, axis=1, keepdims=True))).astype(LOW)
                probs[half * (CH // 128) + s, image, second] = p
                o = nn(p, jnp.where(mask, val, jnp.zeros_like(val)))
                total = o if total is None else total + o
            att[tok, lane] = total.astype(LOW)
            return 0
        lax.fori_loop(0, images * (CH // 128), pair, 0)
        return 0
    lax.fori_loop(0, half_heads, project, 0)
    outs = [
        (qkv.at[0], qr_o), (qkv.at[1], kr_o), (qkv.at[2], vb_o), (rqk.at[0], rq_o), (rqk.at[1], rk_o), (probs, p_o), (att, o_o),
        (mods, mods_o), (call, call_o),
    ]
    later = [(x1, x1_o), (hid, h_o), (ga, ga_o), (gb, gb_o), (n2, out)]
    copies = [pltpu.make_async_copy(a, b, osem.at[k]) for k, (a, b) in enumerate(outs + later)]
    for k in range(len(outs)):
        copies[k].start()

    at_out = 3 * half_heads
    def project_out(j, _):
        slot = begin(at_out + j)
        lane = at(j, CH)
        x1[:, lane] = tokens[:, lane].astype(FULL) + nn(att[...], weights(slot))
        return 0
    lax.fori_loop(0, half_heads, project_out, 0)
    copies[len(outs)].start()
    norm_rows(x1, mods, 1, images, n2)

    at_up = at_out + half_heads
    def widen(j, _):
        up[...] = nn(n2[...], weights(begin(at_up + 2 * j)))
        gate = nn(n2[...], weights(begin(at_up + 2 * j + 1)))
        lane_of = lambda s: pl.ds(pl.multiple_of(j * CH + s * 128, 128), 128)
        for s in range(CH // 128):
            g = gate[:, s * 128 : (s + 1) * 128]
            u = up[:, s * 128 : (s + 1) * 128]
            phi = 0.5 + 0.5 * lax.erf(g * math.sqrt(0.5))
            gelu = g * phi
            slope = phi + g * (jnp.exp(-0.5 * g * g) * (1.0 / math.sqrt(2.0 * math.pi)))
            hid[:, lane_of(s)] = (u * gelu).astype(LOW)
            ga[:, lane_of(s)] = gelu.astype(LOW)
            gb[:, lane_of(s)] = (u * slope).astype(LOW)
        return 0
    hidden = hid.shape[1]
    lax.fori_loop(0, hidden // CH, widen, 0)
    for k in range(1, 4):
        copies[len(outs) + k].start()

    at_down = at_up + 2 * hidden // CH
    def narrow(k, _):
        for j in range(width // CH):
            slot = begin(at_down + k * (width // CH) + j)
            part = nn(hid[:, at(k, width)], weights(slot))
            cols = slice(j * CH, (j + 1) * CH)
            acc[:, cols] = part + jnp.where(k == 0, x1[:, cols], acc[:, cols])
        return 0
    lax.fori_loop(0, hidden // width, narrow, 0)
    n2[...] = acc[...].astype(LOW)
    copies[-1].start()
    for copy in copies:
        copy.wait()
    finish()
    wait_bytes(call.at[pl.ds(0, shards - 1)], csem.at[0])
    wait_bytes(mrecv.at[pl.ds(0, shards - 1)], msem.at[0])


def forward(tokens, cparts, wm, tables, roots, src, shards, images, hidden):
    rows, width = tokens.shape
    n, R, w = src.shape
    Z = shards // 2
    length = rows // images
    pairs = width // 128
    def array(shape, kind):
        return jax.ShapeDtypeStruct(shape, kind)
    wide = (rows, width)
    out_shape = (
        array((n, Z, 2, R, w), LOW), array(wide, LOW), array(wide, FULL), array(wide, LOW), array(wide, LOW), array(wide, LOW),
        array(wide, FULL), array(wide, FULL), array((pairs, images, 2, length, length), LOW), array(wide, LOW),
        array((rows, hidden), LOW), array((rows, hidden), LOW), array((rows, hidden), LOW), array((8, 2 * width), FULL),
        array(cparts.shape, LOW),
    )
    vm = lambda *shape_kind: pltpu.VMEM(*shape_kind)
    scratch = [
        vm(wide, LOW), vm((3, *wide), LOW), vm((2, *wide), FULL), vm((pairs, images, 2, length, length), LOW), vm(wide, LOW),
        vm(wide, FULL), vm(wide, LOW), vm((rows, hidden), LOW), vm((rows, hidden), LOW), vm((rows, hidden), LOW),
        vm((rows, w), FULL), vm(wide, FULL), vm((W_SLOTS, Z, 2, R, w), LOW), vm((8, 2 * width), FULL), vm(cparts.shape, LOW),
        vm((shards, cparts.shape[1], 2 * width), FULL), vm((shards, 8, 2 * width), FULL),
        pltpu.SemaphoreType.DMA((8, n)), pltpu.SemaphoreType.DMA((8, n)), pltpu.SemaphoreType.DMA((n,)),
        pltpu.SemaphoreType.DMA((W_SLOTS,)), pltpu.SemaphoreType.DMA((14,)), pltpu.SemaphoreType.DMA((2,)),
        pltpu.SemaphoreType.DMA((2,)), pltpu.SemaphoreType.DMA,
    ]
    hbm, vmem = pl.BlockSpec(memory_space=pltpu.HBM), pl.BlockSpec(memory_space=pltpu.VMEM)
    return pl.pallas_call(
        functools.partial(forward_kernel, images),
        out_shape=out_shape,
        in_specs=[vmem] * 7 + [hbm],
        out_specs=tuple([hbm] * len(out_shape)),
        scratch_shapes=scratch,
        compiler_params=pltpu.CompilerParams(collective_id=0, has_side_effects=True, vmem_limit_bytes=VMEM_LIMIT),
    )(tokens, cparts, wm, *tables, roots, src)


def prepare(tokens, cond, pos_rows, pos_cols, attn_scale, w_mod1, w_qkv, w_out, w_mod2, w_up, w_down, shards):
    rows, width = w_qkv.shape[0], tokens.shape[1]
    per = width // CH
    blocks = w_down.shape[0] // rows
    qkv = w_qkv.reshape(rows, 3, per, CH).transpose(2, 1, 0, 3).reshape(-1, rows, CH)
    out = w_out.reshape(rows, per, CH).transpose(1, 0, 2)
    up = w_up.reshape(rows, 2, shards, blocks, rows).transpose(0, 1, 3, 2, 4)
    up = up.reshape(rows, 2, -1, CH).transpose(2, 1, 0, 3).reshape(-1, rows, CH)
    down = w_down.reshape(blocks, rows, per, CH).transpose(0, 2, 1, 3).reshape(-1, rows, CH)
    src = jnp.concatenate([qkv, out, up, down])
    images, wide = cond.shape
    own = wide // shards
    cparts = cond.reshape(images, shards, own).transpose(1, 0, 2)
    cparts = jnp.pad(cparts, ((0, 0), (0, 8 - images), (0, 128 - own)))
    cparts = jnp.concatenate([cparts, cparts], axis=1)
    wm = jnp.pad(jnp.concatenate([w_mod1, w_mod2], axis=1), ((0, 128 - own), (0, 0)))
    head = width // attn_scale.shape[0]
    roots = jnp.broadcast_to(jnp.repeat(jnp.sqrt(attn_scale), head)[None], (8, width))
    turned = head // 2
    quarter = turned // 4
    steps = jnp.arange(quarter, dtype=FULL)
    freqs = math.pi * jnp.exp(math.log(10.0) * steps / max(quarter - 1, 1))
    row_pos = (pos_rows.astype(FULL) + 0.5) * (2.0 / GRID) - 1.0
    col_pos = (pos_cols.astype(FULL) + 0.5) * (2.0 / GRID) - 1.0
    angles = jnp.concatenate([row_pos[:, None] * freqs, col_pos[:, None] * freqs], axis=1)
    cos, sin = jnp.cos(angles), jnp.sin(angles)
    zero, rest = jnp.zeros_like(sin), jnp.zeros((sin.shape[0], head - turned), FULL)
    def pair(*parts):
        one = jnp.concatenate(parts, axis=1)
        return jnp.concatenate([one, one], axis=1)
    tables = (pair(cos, cos, rest + 1.0), pair(zero, sin, rest), pair(-sin, zero, rest))
    return src, cparts, wm, roots, tables


Q_SLOTS = 9
RING = 7
A_SLOTS = 2
B_SLOTS = 2
B_LAG = (0, 1, 3, 5, 7, 9)


def of_c(i):
    return (i * 5) % 11 >= 6


def rank_c(i):
    return (i * 5) // 11


def rank_a(i):
    return i - rank_c(i)


def plus(a, b):
    return (a.astype(FULL) + b.astype(FULL)).astype(LOW)


def scatter_ops(n, queue, rc, ry, rxa, rxc, rza, rzc, rl, out, sends, recvs, credit):
    Z = rc.shape[1]
    z, x, y, c = place()
    def cols(k, width):
        return pl.ds(pl.multiple_of(k * width, 128), width)
    def both(i, fn_a, fn_c):
        inside = (i >= 0) & (i < n)
        @pl.when(inside & jnp.logical_not(of_c(i)))
        def _(): fn_a(rank_a(i))
        @pl.when(inside & of_c(i))
        def _(): fn_c(rank_c(i))
    def each(fn):
        lax.fori_loop(0, Z, lambda k, _: (fn(k), 0)[1], 0)
    def s0(i):
        @pl.when((i >= 0) & (i < n))
        def _():
            @pl.when(i >= RING)
            def _(): pl.semaphore_wait(credit, 1)
            remote(queue.at[i % Q_SLOTS, :, :, :, cols(1 - c, 256)], rc.at[i % RING], sends.at[0, i], recvs.at[0, i], z, x, y, 1 - c).start()
    def free(i):
        @pl.when(i >= 0)
        def _(): wait_bytes(rc.at[0], sends.at[0, i])
    def s1(i):
        w = i % RING
        def add():
            wait_bytes(rc.at[w], recvs.at[0, i])
            def one(k):
                rc[w, k] = plus(rc[w, k], queue[i % Q_SLOTS, k, :, :, cols(c, 256)])
            each(one)
        def a(k):
            add()
            remote(rc.at[w, :, :, :, cols(1 - y, 128)], ry.at[k], sends.at[1, i], recvs.at[1, i], z, x, 1 - y, c).start()
        def cc(k):
            add()
            remote(rc.at[w, :, 1 - x], rxc.at[k], sends.at[2, i], recvs.at[2, i], z, 1 - x, y, c).start()
        both(i, a, cc)
    def s2(i):
        w = i % RING
        def a(q):
            wait_bytes(ry.at[q], recvs.at[1, i])
            def one(k):
                ry[q, k] = plus(ry[q, k], rc[w, k, :, :, cols(y, 128)])
            each(one)
            remote(ry.at[q, :, 1 - x], rxa.at[q], sends.at[2, i], recvs.at[2, i], z, 1 - x, y, c).start()
        both(i, a, lambda k: None)
    def s3(i):
        w = i % RING
        def across(rx, rz, q):
            for d in range(1, Z):
                zz = (z + d) % Z
                remote(rx.at[q, zz], rz.at[q, d - 1], sends.at[3, i], recvs.at[3, i], zz, x, y, c).start()
        def done():
            @pl.when(i + RING < n)
            def _(): pl.semaphore_signal(credit, inc=1, device_id=(z * 2 + x, y * 2 + 1 - c), device_id_type=MESH)
        def a(q):
            wait_bytes(rxa.at[q], recvs.at[2, i])
            def one(k):
                rxa[q, k] = plus(rxa[q, k], ry[q, k, x])
            each(one)
            across(rxa, rza, q)
            wait_bytes(ry.at[q], sends.at[1, i])
            done()
        def cc(q):
            wait_bytes(rxc.at[q], recvs.at[2, i])
            def one(k):
                rxc[q, k] = plus(rxc[q, k], rc[w, k, x])
            each(one)
            across(rxc, rzc, q)
            wait_bytes(rxc.at[q], sends.at[2, i])
            done()
        both(i, a, cc)
    def total(rx, rz, q):
        s = rx[q, z].astype(FULL)
        for d in range(1, Z):
            s = s + rz[q, d - 1].astype(FULL)
        return s.astype(LOW)
    def s4(i):
        def a(q):
            wait_bytes(rza.at[q], recvs.at[3, i])
            mine = out.at[i, :, cols(2 * c + y, 128)]
            out[i, :, cols(2 * c + y, 128)] = total(rxa, rza, q)
            remote(mine, mine, sends.at[4, i], recvs.at[4, i], z, x, 1 - y, c).start()
        def cc(q):
            wait_bytes(rzc.at[q], recvs.at[3, i])
            mine = out.at[i, :, cols(c, 256)]
            out[i, :, cols(c, 256)] = total(rxc, rzc, q)
            remote(mine, rl.at[q], sends.at[4, i], recvs.at[4, i], z, x, 1 - y, c).start()
        both(i, a, cc)
    def s5(i):
        mine = out.at[i, :, cols(c, 256)]
        def fwd():
            remote(mine, mine, sends.at[5, i], recvs.at[5, i], z, x, y, 1 - c).start()
        def a(q):
            wait_bytes(out.at[i, :, pl.ds(0, 128)], recvs.at[4, i])
            wait_bytes(out.at[i, :, pl.ds(0, 128)], sends.at[4, i])
            fwd()
        def cc(q):
            wait_bytes(rl.at[q], recvs.at[4, i])
            wait_bytes(rl.at[q], sends.at[4, i])
            out[i, :, cols(c, 256)] = plus(out[i, :, cols(c, 256)], rl[q])
            fwd()
        both(i, a, cc)
    def finish():
        def body(i, _):
            def a(q):
                wait_bytes(rxa.at[q], sends.at[2, i])
                wait_bytes(rza.at[q], sends.at[3, i])
            def cc(q):
                wait_bytes(rzc.at[q], sends.at[3, i])
            both(i, a, cc)
            wait_bytes(rl.at[0], sends.at[5, i])
            wait_bytes(rl.at[0], recvs.at[5, i])
            return 0
        lax.fori_loop(0, n, body, 0)
        lax.fori_loop(n - Q_SLOTS, n, lambda i, _: (free(i), 0)[1], 0)
    return s0, free, s1, s2, s3, s4, s5, finish


def backward_kernel(
    images, wimg, cot, tokens, mods, wm, cosine, sine_up, sine_down, roots, call,
    buf, x1_h, qr_h, kr_h, vb_h, rq_h, rk_h, p_h, o_h, h_h, ga_h, gb_h,
    grads, dtok, gmod, dcond, dscale,
    down, hid, ga, gb, x1, nrm, att, acc, dob, slots, aq, ak, av, arq, ark, ap, dmf, dmx, pm, pr, psum, py, dpart, dcr, dsc, dsr,
    queue, rc, ry, rxa, rxc, rza, rzc, rl, sends, recvs, credit, wsem, lsem, asem, msem, osem,
):
    n, Z, R = buf.shape[0], buf.shape[1], buf.shape[3]
    shards = 2 * Z
    rows, width = tokens.shape
    hidden = hid.shape[1]
    length = rows // images
    per = width // CH
    n_down, n_up, n_out = hidden // width * per, 2 * hidden // CH, per
    z, x, y, c = place()
    f = z * 2 + x
    r = y * 2 + c
    barrier = pltpu.get_barrier_semaphore()
    def greet(d, _):
        pl.semaphore_signal(barrier, inc=1, device_id=((f + d) % shards, r), device_id_type=MESH)
        return 0
    lax.fori_loop(1, shards, greet, 0)
    for where in ((f, (1 - y) * 2 + c), (f, y * 2 + 1 - c)):
        pl.semaphore_signal(barrier, inc=1, device_id=where, device_id_type=MESH)
    given = pltpu.make_async_copy(cot, dob, lsem.at[6])
    given.start()
    loads = [pltpu.make_async_copy(a, b, lsem.at[k]) for k, (a, b) in enumerate(
        [(h_h, hid), (ga_h, ga), (gb_h, gb), (x1_h, x1), (o_h, att)])]
    for one in loads:
        one.start()
    def chunk_of(s):
        first = jnp.where(s < n_down, n - n_down + s, 3 * per + n_out + s - n_down)
        last = jnp.where(s < n_down + n_up + n_out, 3 * per + s - n_down - n_up, s - n_down - n_up - n_out)
        return jnp.where(s < n_down + n_up, first, last)
    def load(s):
        return pltpu.make_async_copy(buf.at[chunk_of(s)], slots.at[s % B_SLOTS], wsem.at[s % B_SLOTS])
    load(0).start()
    def weights(s):
        load(s).wait()
        @pl.when(s + 1 < n)
        def _(): load(s + 1).start()
        return slots[s % B_SLOTS].reshape(width, CH)

    s0, free, s1, s2, s3, s4, s5, finish = scatter_ops(n, queue, rc, ry, rxa, rxc, rza, rzc, rl, grads, sends, recvs, credit)
    def step(t):
        s0(t - B_LAG[0])
        s1(t - B_LAG[1])
        s2(t - B_LAG[2])
        s3(t - B_LAG[3])
        s4(t - B_LAG[4])
        s5(t - B_LAG[5])
    def produce(i, left, right):
        free(i - Q_SLOTS)
        queue[i % Q_SLOTS] = tn(left, right).astype(LOW).reshape(Z, 2, R, CH)

    block = 64
    def blocks(fn):
        lax.fori_loop(0, rows // block, lambda i, _: (fn(at(i, block), i // (length // block)), 0)[1], 0)
    def weigh(k, image):
        down[k, :] = (dob[k, :].astype(FULL) * wimg[image]).astype(LOW)
    given.wait()
    blocks(weigh)
    dmf[...] = jnp.zeros_like(dmf)
    dsc[...] = jnp.zeros_like(dsc)
    pl.semaphore_wait(barrier, shards + 1)
    loads[0].wait()

    def narrow(k, _):
        left = hid[:, at(k, width)]
        for j in range(per):
            produce(k * per + j, left, down[:, j * CH : (j + 1) * CH])
        step(k)
        @pl.when(k == 0)
        def _():
            loads[1].wait()
            loads[2].wait()
        for j in range(per):
            part = nt(down[:, j * CH : (j + 1) * CH], weights(k * per + j))
            acc[...] = part if j == 0 else acc[...] + part
        def gate(q, image):
            ga[q, at(k, width)] = (acc[q, :] * ga[q, at(k, width)].astype(FULL)).astype(LOW)
            gb[q, at(k, width)] = (acc[q, :] * gb[q, at(k, width)].astype(FULL)).astype(LOW)
        blocks(gate)
        return 0
    lax.fori_loop(0, n_down // per, narrow, 0)

    loads[3].wait()
    norm_rows(x1, mods, 1, images, nrm)
    acc[...] = jnp.zeros_like(acc)
    done = n_down // per
    def widen(j, _):
        for side, ref in ((0, ga), (1, gb)):
            s = n_down + 2 * j + side
            produce(s, nrm[...], ref[:, at(j, CH)])
            acc[...] += nt(ref[:, at(j, CH)], weights(s))
        t = done + j + jnp.maximum(j - 3, 0)
        step(t)
        @pl.when(j >= 3)
        def _(): step(t + 1)
        return 0
    lax.fori_loop(0, n_up // 2, widen, 0)
    done = done + n_up // 2 + max(n_up // 2 - 3, 0)

    def norm_back(src_ref, side, base, dst):
        def one(q, image):
            v = src_ref[q, :].astype(FULL)
            dn = acc[q, :]
            factor = lax.rsqrt(jnp.mean(v * v, axis=1, keepdims=True) + EPS)
            m = mods[pl.ds(image, 1), side * width : (side + 1) * width]
            g = dn * (1.0 + m)
            mean = jnp.mean(v * g, axis=1, keepdims=True)
            dst(q, base(q, image) + factor * g - v * (factor * factor * factor * mean))
            dmf[pl.ds(side * 8 + image, 1), :] += jnp.sum(v * factor * dn, axis=0, keepdims=True)
        blocks(one)
    def keep_two(q, value):
        x1[q, :] = value
        down[q, :] = value.astype(LOW)
    norm_back(x1, 1, lambda q, image: dob[q, :].astype(FULL) * wimg[image], keep_two)

    step(done)
    done += 1

    loads[4].wait()
    first_out = n_down + n_up
    for j in range(per):
        right = down[:, j * CH : (j + 1) * CH]
        produce(first_out + j, att[...], right)
        part = nt(right, weights(first_out + j))
        acc[...] = part if j == 0 else acc[...] + part
        step(done)
        done += 1
    dob[...] = acc[...].astype(LOW)
    fill = pltpu.make_async_copy(tokens, att, lsem.at[5])
    fill.start()

    pairs_half = CH // 128
    in_half = images * pairs_half
    def spots(k):
        half, rest = k // in_half, k % in_half
        image, s = rest // pairs_half, half * pairs_half + rest % pairs_half
        return image, s, at(image, length), pl.ds(pl.multiple_of(s * 128, 128), 128)
    def fetch(k):
        image, s, tok, lane = spots(k)
        w = k % A_SLOTS
        refs = [(qr_h.at[tok, lane], aq), (kr_h.at[tok, lane], ak), (vb_h.at[tok, lane], av), (rq_h.at[tok, lane], arq), (rk_h.at[tok, lane], ark), (p_h.at[s, image], ap)]
        return [pltpu.make_async_copy(a, b.at[w], asem.at[e, w]) for e, (a, b) in enumerate(refs)]
    for one in fetch(0):
        one.start()
    acc[...] = jnp.zeros_like(acc)
    total_pairs = images * (width // 128)
    first_qkv = first_out + n_out
    def attend(k, _):
        image, s, tok, lane = spots(k)
        w = k % A_SLOTS
        for one in fetch(k):
            one.wait()
        @pl.when(k + 1 < total_pairs)
        def _():
            for one in fetch(k + 1):
                one.start()
        q, keys, val, dout = aq[w], ak[w], av[w], dob[tok, lane]
        zero = jnp.zeros_like(q)
        dq = dk = dv = None
        for second in range(2):
            mask = head_mask(length, second)
            d_one = jnp.where(mask, dout, zero)
            p = ap[w, second]
            pf = p.astype(FULL)
            dp = nt(d_one, val)
            ds = (pf * (dp - jnp.sum(dp * pf, axis=1, keepdims=True))).astype(LOW)
            dv_one = tn(p, d_one)
            dq_one = nn(ds, jnp.where(mask, keys, zero))
            dk_one = tn(ds, jnp.where(mask, q, zero))
            dq, dk, dv = (dq_one, dk_one, dv_one) if dq is None else (dq + dq_one, dk + dk_one, dv + dv_one)
        inverse = 1.0 / (roots[0:1, lane] * roots[0:1, lane])
        hid[tok, pl.ds(pl.multiple_of(2 * width + s * 128, 128), 128)] = dv.astype(LOW)
        gain = None
        for part, (g, v, scale) in enumerate(((dq, q, arq), (dk, keys, ark))):
            v = v.astype(FULL)
            dot = g * v
            gain = dot if gain is None else gain + dot
            g = g - v * (head_sum(dot) * inverse)
            g = g * cosine[tok, :] - pltpu.roll(g, 112, 1) * sine_down[tok, :] - pltpu.roll(g, 16, 1) * sine_up[tok, :]
            hid[tok, pl.ds(pl.multiple_of(part * width + s * 128, 128), 128)] = (g * scale[w]).astype(LOW)
        dsc[0, pl.ds(s, 1), :] += jnp.sum(gain, axis=0, keepdims=True)
        return 0
    def project(half, t):
        def some(k, t):
            attend(half * in_half + 2 * k, 0)
            attend(half * in_half + 2 * k + 1, 0)
            now = ((half == 0) & (k % 2 == 0)) | ((half > 0) & (k % 2 == 1))
            @pl.when(now)
            def _(): step(t)
            return t + now.astype(jnp.int32)
        t = lax.fori_loop(0, in_half // 2, some, t)
        @pl.when(half == 0)
        def _():
            fill.wait()
            norm_rows(att, mods, 0, images, nrm)
        for part in range(3):
            i = first_qkv + half * 3 + part
            cut = hid[:, pl.ds(pl.multiple_of(part * width + half * CH, CH), CH)]
            produce(i, nrm[...], cut)
            acc[...] += nt(cut, weights(i))
            step(t + part)
        return t + 3
    t = lax.fori_loop(0, per, project, jnp.int32(done))

    def keep_one(q, value):
        down[q, :] = value.astype(LOW)
    norm_back(att, 0, lambda q, image: x1[q, :], keep_one)
    result = pltpu.make_async_copy(down, dtok, osem)
    result.start()
    dmx[f] = dmf[...].astype(LOW)
    def share(d, _):
        pltpu.make_async_remote_copy(src_ref=dmx.at[f], dst_ref=dmx.at[f], send_sem=msem.at[0, 0], recv_sem=msem.at[1, 0],
            device_id=((f + d) % shards, r), device_id_type=MESH).start()
        return 0
    lax.fori_loop(1, shards, share, 0)
    def swap(k, *to):
        return remote(dsc.at[k], dsr.at[k], msem.at[0, 2 + k], msem.at[1, 2 + k], *to)
    swap(0, z, 1 - x, y, c).start()
    step(t)
    wait_bytes(dmx.at[pl.ds(0, shards - 1)], msem.at[1, 0])
    flat = dmx[...].reshape(shards * 16, width)
    group = call[...].reshape(shards * 16, 128)
    upper = lax.broadcasted_iota(jnp.int32, group.shape, 0) % 16 < 8
    nothing = jnp.zeros_like(group)
    pm[:, 0:width] = tn(jnp.where(upper, group, nothing), flat).astype(LOW)
    pm[:, width:] = tn(jnp.where(upper, nothing, group), flat).astype(LOW)
    core_swap = remote(pm, pr, msem.at[0, 5], msem.at[1, 5], z, x, y, 1 - c)
    core_swap.start()
    for side in range(2):
        part = nt(flat, wm[:, side * width : (side + 1) * width]).reshape(shards, 16, 128)[:, side * 8 : side * 8 + 8]
        dpart[...] = part if side == 0 else dpart[...] + part
    def back(d, _):
        to = (f + d) % shards
        pltpu.make_async_remote_copy(src_ref=dpart.at[to], dst_ref=dcr.at[f], send_sem=msem.at[0, 6], recv_sem=msem.at[1, 6],
            device_id=(to, r), device_id_type=MESH).start()
        return 0
    lax.fori_loop(1, shards, back, 0)
    dcr[f] = dpart[f]
    def settle(k):
        swap(k, z, x, y, c).wait()
        dsc[k + 1] = dsc[k] + dsr[k]
    settle(0)
    swap(1, z, x, 1 - y, c).start()
    step(t + 1)
    core_swap.wait()
    half_c = pl.ds(pl.multiple_of(c * width, 128), width)
    psum[...] = plus(pm[:, half_c], pr[:, half_c])
    y_swap = remote(psum, py, msem.at[0, 7], msem.at[1, 7], z, x, 1 - y, c)
    y_swap.start()
    settle(1)
    swap(2, z, x, y, 1 - c).start()
    step(t + 2)
    settle(2)
    dsr[3] = dsc[3]
    def round_z(d):
        return remote(dsr.at[3], dsr.at[4 + z], msem.at[0, 8], msem.at[1, 8], (z + d) % Z, x, y, c)
    for d in range(1, Z):
        round_z(d).start()
    dsr[4 + z] = dsc[3]
    step(t + 3)
    y_swap.wait()
    gmod[:, half_c] = plus(psum[...], py[...])
    last = remote(gmod.at[:, half_c], gmod.at[:, half_c], msem.at[0, 9], msem.at[1, 9], z, x, y, 1 - c)
    last.start()
    wait_bytes(dsr.at[pl.ds(4, Z - 1)], msem.at[1, 8])
    total = dsr[4]
    for k in range(1, Z):
        total = total + dsr[4 + k]
    dscale[...] = total
    step(t + 4)
    wait_bytes(dcr.at[pl.ds(0, shards - 1)], msem.at[1, 6])
    dcond[...] = dcr[...]
    lax.fori_loop(t + 5, n + B_LAG[5], lambda s, _: (step(s), 0)[1], 0)
    last.wait()
    wait_bytes(dmx.at[pl.ds(0, shards - 1)], msem.at[0, 0])
    wait_bytes(dcr.at[pl.ds(0, shards - 1)], msem.at[0, 6])
    wait_bytes(dsr.at[pl.ds(4, Z - 1)], msem.at[0, 8])
    result.wait()
    finish()


def backward(wimg, cot, tokens, mods, wm, tables, roots, call, saved):
    images = wimg.shape[0]
    rows, width = tokens.shape
    n, Z, _, R, w = saved[0].shape
    hidden = saved[9].shape[1]
    length = rows // images
    shards = 2 * Z
    n_c = rank_c(n)
    n_a = n - n_c
    vm, dma = pltpu.VMEM, pltpu.SemaphoreType.DMA
    wide = (rows, width)
    slab = (A_SLOTS, length, 128)
    scratch = [
        vm(wide, LOW), vm((rows, hidden), LOW), vm((rows, hidden), LOW), vm((rows, hidden), LOW), vm(wide, FULL), vm(wide, LOW),
        vm(wide, LOW), vm(wide, FULL), vm(wide, LOW), vm((B_SLOTS, Z, 2, R, w), LOW), vm(slab, LOW), vm(slab, LOW), vm(slab, LOW),
        vm(slab, FULL), vm(slab, FULL), vm((A_SLOTS, 2, length, length), LOW), vm((16, width), FULL), vm((shards, 16, width), LOW),
        vm((128, 2 * width), LOW), vm((128, 2 * width), LOW), vm((128, width), LOW), vm((128, width), LOW),
        vm((shards, 8, 128), FULL), vm((shards, 8, 128), FULL), vm((4, width // 128, 128), FULL), vm((4 + Z, width // 128, 128), FULL),
        vm((Q_SLOTS, Z, 2, R, w), LOW), vm((RING, Z, 2, R, w // 2), LOW), vm((n_a, Z, 2, R, w // 4), LOW), vm((n_a, Z, R, w // 4), LOW),
        vm((n_c, Z, R, w // 2), LOW), vm((n_a, Z - 1, R, w // 4), LOW), vm((n_c, Z - 1, R, w // 2), LOW), vm((n_c, R, w // 2), LOW),
        dma((6, n)), dma((6, n)), pltpu.SemaphoreType.REGULAR, dma((B_SLOTS,)), dma((7,)), dma((6, A_SLOTS)), dma((2, 10)), dma,
    ]
    hbm, vmem = pl.BlockSpec(memory_space=pltpu.HBM), pl.BlockSpec(memory_space=pltpu.VMEM)
    smem = pl.BlockSpec(memory_space=pltpu.SMEM)
    array = jax.ShapeDtypeStruct
    return pl.pallas_call(
        functools.partial(backward_kernel, images),
        out_shape=(array((n, R, w), LOW), array(wide, LOW), array((128, 2 * width), LOW), array((shards, 8, 128), FULL), array((width // 128, 128), FULL)),
        in_specs=[smem, hbm, hbm] + [vmem] * 7 + [hbm] * 12,
        out_specs=(vmem, hbm, vmem, vmem, vmem),
        scratch_shapes=scratch,
        compiler_params=pltpu.CompilerParams(collective_id=1, has_side_effects=True, vmem_limit_bytes=VMEM_LIMIT),
    )(wimg, cot, tokens, mods, wm, *tables, roots, call, *saved)


def local(tokens, cond, sigma_idx, pos_rows, pos_cols, attn_scale, w_mod1, w_qkv, w_out, w_mod2, w_up, w_down, cotangent):
    shards = lax.axis_size("fsdp")
    images, wide = cond.shape
    R, width = w_out.shape
    own = w_mod1.shape[0]
    hidden = w_down.shape[0] * shards
    src, cparts, wm, roots, tables = prepare(tokens, cond, pos_rows, pos_cols, attn_scale, w_mod1, w_qkv, w_out, w_mod2, w_up, w_down, shards)
    (chunks, out, x1, qr, kr, vb, rq, rk, probs, att, h, ga, gb, mods, call) = forward(tokens, cparts, wm, tables, roots, src, shards, images, hidden)
    saved = (chunks, x1, qr, kr, vb, rq, rk, probs, att, h, ga, gb)
    grads, d_tokens, g_mod, d_cond, d_scale = backward(sigma_weight(sigma_idx), cotangent, tokens, mods, wm, tables, roots, call, saved)
    d_cond = d_cond[:, :images, :own].transpose(1, 0, 2).reshape(images, wide)
    d_scale = jnp.sum(d_scale.reshape(attn_scale.shape[0], -1), axis=1) / (2.0 * attn_scale)
    per = width // CH
    blocks = w_down.shape[0] // R
    cuts = [blocks * per, blocks * per + 2 * hidden // CH, blocks * per + 2 * hidden // CH + per]
    down, up, proj, qkv = jnp.split(grads.astype(FULL), cuts)
    g_down = down.reshape(blocks, per, R, CH).transpose(0, 2, 1, 3).reshape(blocks * R, width)
    up = up.reshape(-1, 2, R, CH).transpose(2, 1, 0, 3).reshape(R, 2, blocks, shards, R)
    g_up = up.transpose(0, 1, 3, 2, 4).reshape(R, 2 * hidden)
    g_out = proj.transpose(1, 0, 2).reshape(R, width)
    g_qkv = qkv.reshape(per, 3, R, CH).transpose(2, 1, 0, 3).reshape(R, 3 * width)
    g_mod = g_mod[:own].astype(FULL)
    return out, d_tokens, d_cond, d_scale, g_mod[:, :width], g_qkv, g_out, g_mod[:, width:], g_up, g_down


def sigma_weight(bucket):
    level = bucket.astype(jnp.float32) / (NB - 1)
    sigma = jnp.exp(-2.0 + 3.2 * level)
    return 1.0 / (1.0 + 4.0 * sigma * sigma) + 0.25


def solution(mesh):
    placed = (
        P(("fsdp", "rep"), None),
        P(("fsdp", "rep"), None),
        P(("fsdp", "rep")),
        P(("fsdp", "rep")),
        P(("fsdp", "rep")),
        P(),
        P("fsdp", None),
        P("fsdp", None),
        P("fsdp", None),
        P("fsdp", None),
        P("fsdp", None),
        P("fsdp", None),
        P(("fsdp", "rep"), None),
    )
    return jax.shard_map(
        local,
        mesh=mesh,
        in_specs=placed,
        out_specs=(
            P(("fsdp", "rep"), None),
            P(("fsdp", "rep"), None),
            P(("fsdp", "rep"), None),
            P(),
            P("fsdp", None),
            P("fsdp", None),
            P("fsdp", None),
            P("fsdp", None),
            P("fsdp", None),
            P("fsdp", None),
        ),
        check_vma=False,
    )
```

```python
import functools
import math

import jax
import jax.numpy as jnp
from jax import lax
from jax.experimental import pallas as pl
from jax.experimental.pallas import tpu as pltpu
from jax.sharding import PartitionSpec as P

GRID = 16
NB = 64

MESH = pl.DeviceIdType.MESH
CH = 512

def place():
    f, r = lax.axis_index("fsdp"), lax.axis_index("rep")
    return f // 2, f % 2, r // 2, r % 2

def is_c(i):
    return (i * 3) % 11 >= 11 - 3

def remote(src, dst, send, recv, z, x, y, c):
    return pltpu.make_async_remote_copy(src_ref=src, dst_ref=dst, send_sem=send, recv_sem=recv,
        device_id=(z * 2 + x, y * 2 + c), device_id_type=MESH)

def wait_bytes(ref, sem):
    pltpu.make_async_copy(ref, ref, sem).wait()

def gather_ops(src, buf, sends, recvs, own):
    n, Z = buf.shape[0], buf.shape[1]
    z, x, y, c = place()
    zs, xs, ys, yt, cs, ct, cu, cv = (sends.at[k] for k in range(8))
    zr, xr, yr, yq, cr, cq, cp, co = (recvs.at[k] for k in range(8))
    def cols_of(width, k):
        return pl.ds(pl.multiple_of(k * width, 128), width)
    def both(i, fn):
        inside = (i >= 0) & (i < n)
        @pl.when(inside & jnp.logical_not(is_c(i)))
        def _(): fn(128, 2 * y + c, False)
        @pl.when(inside & is_c(i))
        def _(): fn(256, c, True)
    def inside_of(i, low, high, fn):
        @pl.when((i >= low) & (i < high))
        def _(): fn(i - low)
    def stage_z(i):
        low = 0
        for count, blocks_of in src:
            def start(j, i=i, blocks_of=blocks_of):
                for ref, first, width in blocks_of(j, 0, CH):
                    pltpu.make_async_copy(ref, buf.at[i, z, x, :, pl.ds(first, width)], own.at[i]).start()
                def go(width, k, cc):
                    for ref, first, w in blocks_of(j, k * width, width):
                        cols = pl.ds(pl.multiple_of(k * width + first, 128), w)
                        for d in range(1, Z):
                            remote(ref, buf.at[i, z, x, :, cols], zs.at[i], zr.at[i], (z + d) % Z, x, y, c).start()
                        remote(ref, buf.at[i, z, x, :, cols], xs.at[i], xr.at[i], z, 1 - x, y, c).start()
                both(i, go)
            inside_of(i, low, low + count, start)
            low += count
    def others(i, cols, send, recv, *to):
        for d in range(1, Z):
            zz = (z + d) % Z
            remote(buf.at[i, zz, x, :, cols], buf.at[i, zz, x, :, cols], send, recv, *to).start()
    def partner(i, cols, send, recv, *to):
        part = buf.at[i, :, 1 - x, :, cols]
        remote(part, part, send, recv, *to).start()
    def stage_x(i):
        def go(width, k, cc):
            cols = cols_of(width, k)
            wait_bytes(buf.at[i, 0:Z - 1, 0, :, cols], zr.at[i])
            others(i, cols, xs.at[i], xr.at[i], z, 1 - x, y, c)
            if not cc:
                others(i, cols, ys.at[i], yr.at[i], z, x, 1 - y, c)
            others(i, cols, cs.at[i], cr.at[i], z, x, y, 1 - c)
        both(i, go)
    def stage_y(i):
        def go(width, k, cc):
            cols = cols_of(width, k)
            wait_bytes(buf.at[i, :, 0, :, cols], xr.at[i])
            if not cc:
                partner(i, cols, yt.at[i], yq.at[i], z, x, 1 - y, c)
            partner(i, cols, ct.at[i], cq.at[i], z, x, y, 1 - c)
        both(i, go)
    def stage_c(i):
        def go(width, k, cc):
            if cc: return
            cols = cols_of(width, k)
            wait_bytes(buf.at[i, 0:Z - 1, 0, :, cols], yr.at[i])
            wait_bytes(buf.at[i, :, 0, :, cols], yq.at[i])
            mine = cols_of(128, 2 * (1 - y) + c)
            others(i, mine, cu.at[i], cp.at[i], z, x, y, 1 - c)
            partner(i, mine, cv.at[i], co.at[i], z, x, y, 1 - c)
        both(i, go)
    def core_waits(i, one, two, three, four):
        def go(width, k, cc):
            cols = pl.ds(0, width)
            wait_bytes(buf.at[i, 0:Z - 1, 0, :, cols], one.at[i])
            wait_bytes(buf.at[i, :, 0, :, cols], two.at[i])
            if not cc:
                wait_bytes(buf.at[i, 0:Z - 1, 0, :, cols], three.at[i])
                wait_bytes(buf.at[i, :, 0, :, cols], four.at[i])
        both(i, go)
    def ready(i):
        @pl.when((i >= 0) & (i < n))
        def _(): wait_bytes(buf.at[i, z, x], own.at[i])
        core_waits(i, cr, cq, cp, co)
    def finish():
        def body(i, _):
            def go(width, k, cc):
                cols = cols_of(width, k)
                wait_bytes(buf.at[i, 0:Z - 1, 0, :, cols], zs.at[i])
                wait_bytes(buf.at[i, :, 0, :, cols], xs.at[i])
                if not cc:
                    wait_bytes(buf.at[i, 0:Z - 1, 0, :, cols], ys.at[i])
                    wait_bytes(buf.at[i, :, 0, :, cols], yt.at[i])
            both(i, go)
            core_waits(i, cs, ct, cu, cv)
            return 0
        lax.fori_loop(0, n, body, 0)
    return stage_z, stage_x, stage_y, stage_c, ready, finish


EPS = 1e-06
LOW = jnp.bfloat16
FULL = jnp.float32
VMEM_LIMIT = 60 * 2**20
F_LAG = (0, 2, 4, 6, 7)
W_SLOTS = 3


def nn(a, b):
    return jnp.dot(a, b, preferred_element_type=FULL)


def nt(a, b):
    return lax.dot_general(a, b, (((1,), (1,)), ((), ())), preferred_element_type=FULL)


def tn(a, b):
    return lax.dot_general(a, b, (((0,), (0,)), ((), ())), preferred_element_type=FULL)


def at(k, size):
    return pl.ds(pl.multiple_of(k * size, size), size)


def head_sum(v):
    one = lax.broadcasted_iota(jnp.int32, (128, 128), 0) // 64
    two = lax.broadcasted_iota(jnp.int32, (128, 128), 1) // 64
    same = (one == two).astype(LOW)
    high = v.astype(LOW)
    rest = v - high.astype(FULL)
    return nn(high, same) + nn(rest.astype(LOW), same)


def head_mask(rows, second):
    lane = lax.broadcasted_iota(jnp.int32, (rows, 128), 1)
    return (lane >= 64) if second else (lane < 64)


def turn(v, cosine, sine_up, sine_down):
    return v * cosine + pltpu.roll(v, 16, 1) * sine_up + pltpu.roll(v, 112, 1) * sine_down


def norm_rows(src_ref, mods_ref, side, images, dst_ref, x_ref=None):
    rows, width = src_ref.shape
    length = rows // images
    block = 64
    def body(i, _):
        r = at(i, block)
        v = src_ref[r, :].astype(FULL)
        factor = lax.rsqrt(jnp.mean(v * v, axis=1, keepdims=True) + EPS)
        m = mods_ref[pl.ds(i // (length // block), 1), side * width : (side + 1) * width]
        dst_ref[r, :] = (v * factor * (1.0 + m)).astype(LOW)
        return 0
    lax.fori_loop(0, rows // block, body, 0)


def three(v):
    one = v.astype(LOW)
    rest = v - one.astype(FULL)
    two = rest.astype(LOW)
    return one, two, (rest - two.astype(FULL)).astype(LOW)


def rope_tables(pos, tab, head):
    grid = lax.broadcasted_iota(jnp.int32, (2 * GRID, 128), 0)
    lane = lax.broadcasted_iota(jnp.int32, (2 * GRID, 128), 1) % head
    pairs = head // 4
    quarter = pairs // 2
    j = lane % pairs
    place = ((grid % GRID).astype(FULL) + 0.5) * (2.0 / GRID) - 1.0
    freq = math.pi * jnp.exp(math.log(10.0) * (j % quarter).astype(FULL) / max(quarter - 1, 1))
    angle = place * freq
    mine = (lane < 2 * pairs) & ((grid // GRID) == (j // quarter))
    cos, sin = jnp.cos(angle), jnp.sin(angle)
    zero = jnp.zeros_like(cos)
    kinds = (
        jnp.where(mine, cos, zero),
        jnp.where(mine & (lane >= pairs), sin, zero),
        jnp.where(mine & (lane < pairs), -sin, zero),
    )
    rows = pos.shape[1]
    spot = lax.broadcasted_iota(jnp.int32, (GRID, rows), 0)
    hot = jnp.concatenate([(spot == pos[0:1, :]).astype(FULL), (spot == pos[1:2, :]).astype(FULL)], axis=0).astype(LOW)
    for k, kind in enumerate(kinds):
        total = None
        for part in three(kind):
            one = tn(hot, part)
            total = one if total is None else total + one
        if k == 0:
            plain = lax.broadcasted_iota(jnp.int32, (rows, 128), 1) % head >= 2 * pairs
            total = total + plain.astype(FULL)
        tab[k] = total


def forward_kernel(
    images, heads, tokens, cond, pos, w_mod1, w_mod2, scale, w_qkv, w_out, w_up, w_down,
    buf, out, x1_o, qr_o, kr_o, vb_o, rq_o, rk_o, p_o, o_o, h_o, ga_o, gb_o, mods_o, call_o, wm_o, tab_o, roots_o,
    n1, qkv, rqk, probs, att, x1, n2, hid, ga, gb, up, acc, slots, mods, call, mpart, mrecv, cparts, wide_c, wm, tab, roots,
    sends, recvs, own, wsem, osem, csem, msem,
):
    n, Z, R = buf.shape[0], buf.shape[1], buf.shape[3]
    shards = 2 * Z
    rows, width = tokens.shape
    hidden = hid.shape[1]
    length = rows // images
    half_heads = width // CH
    z, x, y, c = place()
    f = z * 2 + x
    r = y * 2 + c
    barrier = pltpu.get_barrier_semaphore()
    def greet(d, _):
        pl.semaphore_signal(barrier, inc=1, device_id=((f + d) % shards, r), device_id_type=MESH)
        return 0
    lax.fori_loop(1, shards, greet, 0)
    for where in ((f, (1 - y) * 2 + c), (f, y * 2 + 1 - c)):
        pl.semaphore_signal(barrier, inc=1, device_id=where, device_id_type=MESH)
    wide_c[...] = jnp.zeros_like(wide_c)
    for k in range(2):
        wide_c[k * images : (k + 1) * images, :] = cond[...].astype(FULL)
    map_rows = w_mod1.shape[0]
    def cut(k, _):
        full = wide_c.shape[1]
        moved = pltpu.roll(wide_c[...], (full - k * map_rows) % full, 1)[:, 0:128]
        lane = lax.broadcasted_iota(jnp.int32, moved.shape, 1)
        cparts[k] = jnp.where(lane < map_rows, moved, 0.0).astype(LOW)
        return 0
    lax.fori_loop(0, shards, cut, 0)
    call[f] = cparts[f]
    pl.semaphore_wait(barrier, shards + 1)

    blocks = w_down.shape[0] // R
    def columns(ref, at_row, at_col):
        def of(j, first, size):
            return [(ref.at[at_row(j), pl.ds(pl.multiple_of(at_col(j) + first, 128), size)], 0, size)]
        return of
    every = lambda j: slice(None)
    def of_up(j, first, size):
        if R != 128:
            return columns(w_up, every, lambda j: (j % 2) * hidden + (j // 2) * CH)(j, first, size)
        found = []
        for b in range(size // 128):
            unit = (j // 2) * (CH // 128) + first // 128 + b
            spot = (j % 2) * hidden + ((unit % shards) * blocks + unit // shards) * 128
            found.append((w_up.at[:, pl.ds(pl.multiple_of(spot, 128), 128)], b * 128, 128))
        return found
    src = [
        (3 * half_heads, columns(w_qkv, every, lambda j: (j % 3) * width + (j // 3) * CH)),
        (half_heads, columns(w_out, every, lambda j: j * CH)),
        (2 * hidden // CH, of_up),
        (blocks * half_heads, columns(w_down, lambda j: at(j // half_heads, R), lambda j: (j % half_heads) * CH)),
    ]
    stage_z, stage_x, stage_y, stage_c, ready, finish = gather_ops(src, buf, sends, recvs, own)

    def give(d, _):
        to = (f + d) % shards
        pltpu.make_async_remote_copy(src_ref=cparts.at[to], dst_ref=call.at[f], send_sem=csem.at[0], recv_sem=csem.at[1],
            device_id=(to, r), device_id_type=MESH).start()
        return 0

    def load(j):
        return pltpu.make_async_copy(buf.at[j], slots.at[j % W_SLOTS], wsem.at[j % W_SLOTS])

    def step(t):
        @pl.when(t >= 2)
        def _(): stage_z(t)
        stage_x(t - F_LAG[1])
        stage_y(t - F_LAG[2])
        stage_c(t - F_LAG[3])
        ready(t - F_LAG[4])
        @pl.when((t >= F_LAG[4]) & (t < n + F_LAG[4]))
        def _(): load(t - F_LAG[4]).start()

    def begin(j):
        step(j + F_LAG[4] + 1)
        load(j).wait()
        return j % W_SLOTS

    def weights(slot):
        return slots[slot].reshape(width, CH)

    stage_z(0)
    lax.fori_loop(1, shards, give, 0)
    stage_z(1)
    for side, ref in enumerate((w_mod1, w_mod2)):
        acc[0:128, :] = jnp.zeros((128, width), FULL)
        acc[0:map_rows, :] = ref[...].astype(FULL)
        wm[:, side * width : (side + 1) * width] = acc[0:128, :].astype(LOW)
    wait_bytes(call.at[pl.ds(0, shards - 1)], csem.at[1])
    flat = call[...].reshape(shards * 16, 128)
    mpart[...] = nn(flat, wm[...]).reshape(shards, 16, 2 * width)[:, 0:images]
    def back(d, _):
        to = (f + d) % shards
        pltpu.make_async_remote_copy(src_ref=mpart.at[to], dst_ref=mrecv.at[f], send_sem=msem.at[0], recv_sem=msem.at[1],
            device_id=(to, r), device_id_type=MESH).start()
        return 0
    lax.fori_loop(1, shards, back, 0)
    mrecv[f] = mpart[f]
    step(2)
    which = lax.broadcasted_iota(jnp.int32, roots.shape, 1) // (width // heads)
    row = jnp.zeros(roots.shape, FULL)
    for h in range(heads):
        row = jnp.where(which == h, scale[h], row)
    roots[...] = jnp.sqrt(row)
    rope_tables(pos, tab, width // heads)
    step(3)
    wait_bytes(mrecv.at[pl.ds(0, shards - 1)], msem.at[1])
    mods[...] = jnp.zeros_like(mods)
    total = mrecv[0]
    for k in range(1, shards):
        total = total + mrecv[k]
    mods[0:images, :] = total
    norm_rows(tokens, mods, 0, images, n1)
    lax.fori_loop(4, F_LAG[4] + 1, lambda t, _: (step(t), 0)[1], 0)

    def project(half, _):
        lanes_of = lambda s: pl.ds(pl.multiple_of(half * CH + s * 128, 128), 128)
        for part in range(2):
            slot = begin(half * 3 + part)
            v = nn(n1[...], weights(slot))
            for s in range(CH // 128):
                one = v[:, s * 128 : (s + 1) * 128]
                scale = lax.rsqrt(head_sum(one * one) + EPS) * roots[0:1, lanes_of(s)]
                rqk[part, :, lanes_of(s)] = scale
                qkv[part, :, lanes_of(s)] = turn(one * scale, tab[0], tab[1], tab[2]).astype(LOW)
        slot = begin(half * 3 + 2)
        qkv[2, :, at(half, CH)] = nn(n1[...], weights(slot)).astype(LOW)
        def pair(k, _):
            image, s = k // (CH // 128), k % (CH // 128)
            tok = at(image, length)
            lane = pl.ds(pl.multiple_of(half * CH + s * 128, 128), 128)
            q, keys, val = qkv[0, tok, lane], qkv[1, tok, lane], qkv[2, tok, lane]
            total = None
            for second in range(2):
                mask = head_mask(length, second)
                scores = jnp.exp(nt(jnp.where(mask, q, jnp.zeros_like(q)), keys))
                p = (scores * (1.0 / jnp.sum(scores, axis=1, keepdims=True))).astype(LOW)
                probs[half * (CH // 128) + s, image, second] = p
                o = nn(p, jnp.where(mask, val, jnp.zeros_like(val)))
                total = o if total is None else total + o
            att[tok, lane] = total.astype(LOW)
            return 0
        lax.fori_loop(0, images * (CH // 128), pair, 0)
        return 0
    lax.fori_loop(0, half_heads, project, 0)
    outs = [
        (qkv.at[0], qr_o), (qkv.at[1], kr_o), (qkv.at[2], vb_o), (rqk.at[0], rq_o), (rqk.at[1], rk_o), (probs, p_o), (att, o_o),
        (mods, mods_o), (call, call_o), (wm, wm_o), (tab, tab_o), (roots, roots_o),
    ]
    later = [(x1, x1_o), (hid, h_o), (ga, ga_o), (gb, gb_o), (n2, out)]
    copies = [pltpu.make_async_copy(a, b, osem.at[k]) for k, (a, b) in enumerate(outs + later)]
    for k in range(len(outs)):
        copies[k].start()

    at_out = 3 * half_heads
    def project_out(j, _):
        slot = begin(at_out + j)
        lane = at(j, CH)
        x1[:, lane] = tokens[:, lane].astype(FULL) + nn(att[...], weights(slot))
        return 0
    lax.fori_loop(0, half_heads, project_out, 0)
    copies[len(outs)].start()
    norm_rows(x1, mods, 1, images, n2)

    at_up = at_out + half_heads
    def widen(j, _):
        up[...] = nn(n2[...], weights(begin(at_up + 2 * j)))
        gate = nn(n2[...], weights(begin(at_up + 2 * j + 1)))
        lane_of = lambda s: pl.ds(pl.multiple_of(j * CH + s * 128, 128), 128)
        for s in range(CH // 128):
            g = gate[:, s * 128 : (s + 1) * 128]
            u = up[:, s * 128 : (s + 1) * 128]
            phi = 0.5 + 0.5 * lax.erf(g * math.sqrt(0.5))
            gelu = g * phi
            slope = phi + g * (jnp.exp(-0.5 * g * g) * (1.0 / math.sqrt(2.0 * math.pi)))
            hid[:, lane_of(s)] = (u * gelu).astype(LOW)
            ga[:, lane_of(s)] = gelu.astype(LOW)
            gb[:, lane_of(s)] = (u * slope).astype(LOW)
        return 0
    lax.fori_loop(0, hidden // CH, widen, 0)
    for k in range(1, 4):
        copies[len(outs) + k].start()

    at_down = at_up + 2 * hidden // CH
    def narrow(k, _):
        for j in range(width // CH):
            slot = begin(at_down + k * (width // CH) + j)
            part = nn(hid[:, at(k, width)], weights(slot))
            cols = slice(j * CH, (j + 1) * CH)
            acc[:, cols] = part + jnp.where(k == 0, x1[:, cols], acc[:, cols])
        return 0
    lax.fori_loop(0, hidden // width, narrow, 0)
    n2[...] = acc[...].astype(LOW)
    copies[-1].start()
    for copy in copies:
        copy.wait()
    finish()
    wait_bytes(call.at[pl.ds(0, shards - 1)], csem.at[0])
    wait_bytes(mrecv.at[pl.ds(0, shards - 1)], msem.at[0])


def forward(tokens, cond, pos, w_mod1, w_mod2, scale, w_qkv, w_out, w_up, w_down, shards):
    rows, width = tokens.shape
    R, hidden = w_out.shape[0], w_up.shape[1] // 2
    images, wide_c = cond.shape
    Z, w = shards // 2, CH
    n = (w_qkv.shape[1] + w_out.shape[1] + w_up.shape[1]) // CH + (w_down.shape[0] // R) * (width // CH)
    length = rows // images
    pairs = width // 128
    array = jax.ShapeDtypeStruct
    wide = (rows, width)
    out_shape = (
        array((n, Z, 2, R, w), LOW), array(wide, LOW), array(wide, FULL), array(wide, LOW), array(wide, LOW), array(wide, LOW),
        array(wide, FULL), array(wide, FULL), array((pairs, images, 2, length, length), LOW), array(wide, LOW),
        array((rows, hidden), LOW), array((rows, hidden), LOW), array((rows, hidden), LOW), array((8, 2 * width), FULL),
        array((shards, 16, 128), LOW), array((128, 2 * width), LOW), array((3, rows, 128), FULL), array((8, width), FULL),
    )
    vm, dma = pltpu.VMEM, pltpu.SemaphoreType.DMA
    scratch = [
        vm(wide, LOW), vm((3, *wide), LOW), vm((2, *wide), FULL), vm((pairs, images, 2, length, length), LOW), vm(wide, LOW),
        vm(wide, FULL), vm(wide, LOW), vm((rows, hidden), LOW), vm((rows, hidden), LOW), vm((rows, hidden), LOW),
        vm((rows, w), FULL), vm(wide, FULL), vm((W_SLOTS, Z, 2, R, w), LOW), vm((8, 2 * width), FULL), vm((shards, 16, 128), LOW),
        vm((shards, images, 2 * width), FULL), vm((shards, images, 2 * width), FULL), vm((shards, 16, 128), LOW), vm((16, wide_c), FULL),
        vm((128, 2 * width), LOW), vm((3, rows, 128), FULL), vm((8, width), FULL),
        dma((8, n)), dma((8, n)), dma((n,)), dma((W_SLOTS,)), dma((17,)), dma((2,)), dma((2,)),
    ]
    hbm, vmem = pl.BlockSpec(memory_space=pltpu.HBM), pl.BlockSpec(memory_space=pltpu.VMEM)
    smem = pl.BlockSpec(memory_space=pltpu.SMEM)
    return pl.pallas_call(
        functools.partial(forward_kernel, images, scale.shape[0]),
        out_shape=out_shape,
        in_specs=[vmem] * 5 + [smem] + [hbm] * 4,
        out_specs=tuple([hbm] * len(out_shape)),
        scratch_shapes=scratch,
        compiler_params=pltpu.CompilerParams(collective_id=0, has_side_effects=True, vmem_limit_bytes=VMEM_LIMIT),
    )(tokens, cond, pos, w_mod1, w_mod2, scale, w_qkv, w_out, w_up, w_down)


Q_SLOTS = 9
RING = 7
A_SLOTS = 2
B_SLOTS = 2
B_LAG = (0, 1, 3, 5, 7, 9, 10)


def of_c(i):
    return (i * 5 + 5) % 11 >= 6


def rank_c(i):
    return (i * 5 + 5) // 11


def rank_a(i):
    return i - rank_c(i)


def plus(a, b):
    return (a.astype(FULL) + b.astype(FULL)).astype(LOW)


def scatter_ops(n, queue, rc, ry, rxa, rxc, rza, rzc, rl, out, sends, recvs, credit, put):
    Z = rc.shape[1]
    z, x, y, c = place()
    def cols(k, width):
        return pl.ds(pl.multiple_of(k * width, 128), width)
    def both(i, fn_a, fn_c):
        inside = (i >= 0) & (i < n)
        @pl.when(inside & jnp.logical_not(of_c(i)))
        def _(): fn_a(rank_a(i))
        @pl.when(inside & of_c(i))
        def _(): fn_c(rank_c(i))
    def each(fn):
        lax.fori_loop(0, Z, lambda k, _: (fn(k), 0)[1], 0)
    def s0(i):
        @pl.when((i >= 0) & (i < n))
        def _():
            @pl.when(i >= RING)
            def _(): pl.semaphore_wait(credit, 1)
            remote(queue.at[i % Q_SLOTS, :, :, :, cols(1 - c, 256)], rc.at[i % RING], sends.at[0, i], recvs.at[0, i], z, x, y, 1 - c).start()
    def free(i):
        @pl.when(i >= 0)
        def _(): wait_bytes(rc.at[0], sends.at[0, i])
    def s1(i):
        w = i % RING
        def add():
            wait_bytes(rc.at[w], recvs.at[0, i])
            def one(k):
                rc[w, k] = plus(rc[w, k], queue[i % Q_SLOTS, k, :, :, cols(c, 256)])
            each(one)
        def a(k):
            add()
            remote(rc.at[w, :, :, :, cols(1 - y, 128)], ry.at[k], sends.at[1, i], recvs.at[1, i], z, x, 1 - y, c).start()
        def cc(k):
            add()
            remote(rc.at[w, :, 1 - x], rxc.at[k], sends.at[2, i], recvs.at[2, i], z, 1 - x, y, c).start()
        both(i, a, cc)
    def across(i, rx, rz, q):
        for d in range(1, Z):
            zz = (z + d) % Z
            remote(rx.at[q, zz], rz.at[q, d - 1], sends.at[3, i], recvs.at[3, i], zz, x, y, c).start()
    def s2(i):
        w = i % RING
        def a(q):
            wait_bytes(ry.at[q], recvs.at[1, i])
            def one(k):
                ry[q, k] = plus(ry[q, k], rc[w, k, :, :, cols(y, 128)])
            each(one)
            remote(ry.at[q, :, 1 - x], rxa.at[q], sends.at[2, i], recvs.at[2, i], z, 1 - x, y, c).start()
        def cc(q):
            wait_bytes(rxc.at[q], recvs.at[2, i])
            def one(k):
                rxc[q, k] = plus(rxc[q, k], rc[w, k, x])
            each(one)
            across(i, rxc, rzc, q)
        both(i, a, cc)
    def total(rx, rz, q):
        s = rx[q, z].astype(FULL)
        for d in range(1, Z):
            s = s + rz[q, d - 1].astype(FULL)
        return s.astype(LOW)
    def s3(i):
        def done():
            @pl.when(i + RING < n)
            def _(): pl.semaphore_signal(credit, inc=1, device_id=(z * 2 + x, y * 2 + 1 - c), device_id_type=MESH)
        def a(q):
            wait_bytes(rxa.at[q], recvs.at[2, i])
            def one(k):
                rxa[q, k] = plus(rxa[q, k], ry[q, k, x])
            each(one)
            across(i, rxa, rza, q)
            wait_bytes(ry.at[q], sends.at[1, i])
            done()
        def cc(q):
            wait_bytes(rzc.at[q], recvs.at[3, i])
            mine = out.at[i, :, cols(c, 256)]
            out[i, :, cols(c, 256)] = total(rxc, rzc, q)
            remote(mine, rl.at[q], sends.at[4, i], recvs.at[4, i], z, x, 1 - y, c).start()
            wait_bytes(rxc.at[q], sends.at[2, i])
            done()
        both(i, a, cc)
    def fwd(i):
        mine = out.at[i, :, cols(c, 256)]
        remote(mine, mine, sends.at[5, i], recvs.at[5, i], z, x, y, 1 - c).start()
    def s4(i):
        def a(q):
            wait_bytes(rza.at[q], recvs.at[3, i])
            mine = out.at[i, :, cols(2 * c + y, 128)]
            out[i, :, cols(2 * c + y, 128)] = total(rxa, rza, q)
            remote(mine, mine, sends.at[4, i], recvs.at[4, i], z, x, 1 - y, c).start()
        def cc(q):
            wait_bytes(rl.at[q], recvs.at[4, i])
            wait_bytes(rl.at[q], sends.at[4, i])
            out[i, :, cols(c, 256)] = plus(out[i, :, cols(c, 256)], rl[q])
            fwd(i)
        both(i, a, cc)
    def final(i):
        wait_bytes(rl.at[0], sends.at[5, i])
        wait_bytes(rl.at[0], recvs.at[5, i])
        put(i)
    def s5(i):
        def a(q):
            wait_bytes(out.at[i, :, pl.ds(0, 128)], recvs.at[4, i])
            wait_bytes(out.at[i, :, pl.ds(0, 128)], sends.at[4, i])
            fwd(i)
        both(i, a, lambda q: final(i))
    def s6(i):
        both(i, lambda q: final(i), lambda q: None)
    def finish():
        def body(i, _):
            def a(q):
                wait_bytes(rxa.at[q], sends.at[2, i])
                wait_bytes(rza.at[q], sends.at[3, i])
            def cc(q):
                wait_bytes(rzc.at[q], sends.at[3, i])
            both(i, a, cc)
            return 0
        lax.fori_loop(0, n, body, 0)
        lax.fori_loop(n - Q_SLOTS, n, lambda i, _: (free(i), 0)[1], 0)
    return s0, free, s1, s2, s3, s4, s5, s6, finish


def backward_kernel(
    images, own_map, sigma, scale, cot, tokens, mods, wm, tab, roots, call,
    buf, x1_h, qr_h, kr_h, vb_h, rq_h, rk_h, p_h, o_h, h_h, ga_h, gb_h,
    g_qkv, g_out, g_up, g_down, dtok, gmod, dcond, dscale,
    down, hid, ga, gb, x1, nrm, att, acc, dob, slots, aq, ak, av, arq, ark, ap, dmf, dmx, pm, pr, psum, py, dpart, dcr, dsc, dsr, wide_c, weight,
    grads, queue, rc, ry, rxa, rxc, rza, rzc, rl, sends, recvs, credit, wsem, lsem, asem, msem, osem, gsem,
):
    n, Z, R = buf.shape[0], buf.shape[1], buf.shape[3]
    shards = 2 * Z
    rows, width = tokens.shape
    hidden = hid.shape[1]
    length = rows // images
    per = width // CH
    n_down, n_up, n_out = hidden // width * per, 2 * hidden // CH, per
    z, x, y, c = place()
    f = z * 2 + x
    r = y * 2 + c
    barrier = pltpu.get_barrier_semaphore()
    def greet(d, _):
        pl.semaphore_signal(barrier, inc=1, device_id=((f + d) % shards, r), device_id_type=MESH)
        return 0
    lax.fori_loop(1, shards, greet, 0)
    for where in ((f, (1 - y) * 2 + c), (f, y * 2 + 1 - c)):
        pl.semaphore_signal(barrier, inc=1, device_id=where, device_id_type=MESH)
    given = pltpu.make_async_copy(cot, dob, lsem.at[6])
    given.start()
    loads = [pltpu.make_async_copy(a, b, lsem.at[k]) for k, (a, b) in enumerate(
        [(h_h, hid), (ga_h, ga), (gb_h, gb), (x1_h, x1), (o_h, att)])]
    for one in loads:
        one.start()
    def chunk_of(s):
        first = jnp.where(s < n_down, n - n_down + s, 3 * per + n_out + s - n_down)
        last = jnp.where(s < n_down + n_up + n_out, 3 * per + s - n_down - n_up, s - n_down - n_up - n_out)
        return jnp.where(s < n_down + n_up, first, last)
    def load(s):
        return pltpu.make_async_copy(buf.at[chunk_of(s)], slots.at[s % B_SLOTS], wsem.at[s % B_SLOTS])
    load(0).start()
    def weights(s):
        load(s).wait()
        @pl.when(s + 1 < n)
        def _(): load(s + 1).start()
        return slots[s % B_SLOTS].reshape(width, CH)

    blocks_d = hidden // width
    def put(i):
        def within(low, high, fn):
            @pl.when((i >= low) & (i < high))
            def _(): fn(i - low)
        def copy(src, dst):
            pltpu.make_async_copy(src, dst, gsem.at[i]).start()
        within(0, n_down, lambda j: copy(grads.at[i], g_down.at[at(j // per, R), at(j % per, CH)]))
        def to_up(j):
            side, first = j % 2, j // 2
            if R != 128:
                copy(grads.at[i], g_up.at[:, pl.ds(pl.multiple_of(side * hidden + first * CH, 128), CH)])
                return
            for b in range(CH // 128):
                unit = first * (CH // 128) + b
                spot = side * hidden + ((unit % shards) * blocks_d + unit // shards) * 128
                copy(grads.at[i, :, pl.ds(b * 128, 128)], g_up.at[:, pl.ds(pl.multiple_of(spot, 128), 128)])
        within(n_down, n_down + n_up, to_up)
        within(n_down + n_up, n_down + n_up + n_out, lambda j: copy(grads.at[i], g_out.at[:, at(j, CH)]))
        within(n_down + n_up + n_out, n, lambda j: copy(grads.at[i], g_qkv.at[:, pl.ds(pl.multiple_of((j % 3) * width + (j // 3) * CH, CH), CH)]))
    s0, free, s1, s2, s3, s4, s5, s6, finish = scatter_ops(n, queue, rc, ry, rxa, rxc, rza, rzc, rl, grads, sends, recvs, credit, put)
    def step(t):
        s0(t - B_LAG[0])
        s1(t - B_LAG[1])
        s2(t - B_LAG[2])
        s3(t - B_LAG[3])
        s4(t - B_LAG[4])
        s5(t - B_LAG[5])
        s6(t - B_LAG[6])
    def produce(i, left, right):
        free(i - Q_SLOTS)
        queue[i % Q_SLOTS] = tn(left, right).astype(LOW).reshape(Z, 2, R, CH)

    block = 64
    def blocks(fn):
        lax.fori_loop(0, rows // block, lambda i, _: (fn(at(i, block), i // (length // block)), 0)[1], 0)
    def weigh(k, image):
        down[k, :] = (dob[k, :].astype(FULL) * weight[image, 0:1, :]).astype(LOW)
    for image in range(images):
        level = jnp.full(weight.shape[1:], sigma[image].astype(FULL), FULL) / (NB - 1)
        noise = jnp.exp(-2.0 + 3.2 * level)
        weight[image] = 1.0 / (1.0 + 4.0 * noise * noise) + 0.25
    given.wait()
    blocks(weigh)
    dmf[...] = jnp.zeros_like(dmf)
    dsc[...] = jnp.zeros_like(dsc)
    pl.semaphore_wait(barrier, shards + 1)
    loads[0].wait()

    def second_product(i):
        produce(i, hid[:, at(i // per, width)], down[:, at(i % per, CH)])
    for i in range(2):
        second_product(i)
        step(i)
    loads[1].wait()
    loads[2].wait()
    def narrow(k, _):
        second_product(k + 2)
        step(k + 2)
        for j in range(per):
            part = nt(down[:, j * CH : (j + 1) * CH], weights(k * per + j))
            acc[...] = part if j == 0 else acc[...] + part
        def gate(q, image):
            ga[q, at(k, width)] = (acc[q, :] * ga[q, at(k, width)].astype(FULL)).astype(LOW)
            gb[q, at(k, width)] = (acc[q, :] * gb[q, at(k, width)].astype(FULL)).astype(LOW)
        blocks(gate)
        return 0
    lax.fori_loop(0, blocks_d, narrow, 0)
    for i in range(2 + blocks_d, n_down):
        second_product(i)
    done = 2 + blocks_d

    loads[3].wait()
    norm_rows(x1, mods, 1, images, nrm)
    acc[...] = jnp.zeros_like(acc)
    def widen(j, _):
        step(done + j)
        for side, ref in ((0, ga), (1, gb)):
            s = n_down + 2 * j + side
            produce(s, nrm[...], ref[:, at(j, CH)])
            acc[...] += nt(ref[:, at(j, CH)], weights(s))
        return 0
    lax.fori_loop(0, n_up // 2, widen, 0)
    done += n_up // 2

    def norm_back(src_ref, side, base, dst):
        def one(q, image):
            v = src_ref[q, :].astype(FULL)
            dn = acc[q, :]
            factor = lax.rsqrt(jnp.mean(v * v, axis=1, keepdims=True) + EPS)
            m = mods[pl.ds(image, 1), side * width : (side + 1) * width]
            g = dn * (1.0 + m)
            mean = jnp.mean(v * g, axis=1, keepdims=True)
            dst(q, base(q, image) + factor * g - v * (factor * factor * factor * mean))
            dmf[pl.ds(side * images + image, 1), :] += jnp.sum(v * factor * dn, axis=0, keepdims=True)
        blocks(one)
    def keep_two(q, value):
        x1[q, :] = value
        down[q, :] = value.astype(LOW)
    norm_back(x1, 1, lambda q, image: dob[q, :].astype(FULL) * weight[image, 0:1, :], keep_two)

    step(done)
    done += 1

    loads[4].wait()
    first_out = n_down + n_up
    for j in range(per):
        right = down[:, j * CH : (j + 1) * CH]
        produce(first_out + j, att[...], right)
        part = nt(right, weights(first_out + j))
        acc[...] = part if j == 0 else acc[...] + part
        step(done)
        done += 1
    dob[...] = acc[...].astype(LOW)
    fill = pltpu.make_async_copy(tokens, att, lsem.at[5])
    fill.start()

    pairs_half = CH // 128
    in_half = images * pairs_half
    def spots(k):
        half, rest = k // in_half, k % in_half
        image, s = rest // pairs_half, half * pairs_half + rest % pairs_half
        return image, s, at(image, length), pl.ds(pl.multiple_of(s * 128, 128), 128)
    def fetch(k):
        image, s, tok, lane = spots(k)
        w = k % A_SLOTS
        refs = [(qr_h.at[tok, lane], aq), (kr_h.at[tok, lane], ak), (vb_h.at[tok, lane], av), (rq_h.at[tok, lane], arq), (rk_h.at[tok, lane], ark), (p_h.at[s, image], ap)]
        return [pltpu.make_async_copy(a, b.at[w], asem.at[e, w]) for e, (a, b) in enumerate(refs)]
    for one in fetch(0):
        one.start()
    acc[...] = jnp.zeros_like(acc)
    total_pairs = images * (width // 128)
    first_qkv = first_out + n_out
    def attend(k, _):
        image, s, tok, lane = spots(k)
        w = k % A_SLOTS
        for one in fetch(k):
            one.wait()
        @pl.when(k + 1 < total_pairs)
        def _():
            for one in fetch(k + 1):
                one.start()
        q, keys, val, dout = aq[w], ak[w], av[w], dob[tok, lane]
        zero = jnp.zeros_like(q)
        dq = dk = dv = None
        for second in range(2):
            mask = head_mask(length, second)
            d_one = jnp.where(mask, dout, zero)
            p = ap[w, second]
            pf = p.astype(FULL)
            dp = nt(d_one, val)
            ds = (pf * (dp - jnp.sum(dp * pf, axis=1, keepdims=True))).astype(LOW)
            dv_one = tn(p, d_one)
            dq_one = nn(ds, jnp.where(mask, keys, zero))
            dk_one = tn(ds, jnp.where(mask, q, zero))
            dq, dk, dv = (dq_one, dk_one, dv_one) if dq is None else (dq + dq_one, dk + dk_one, dv + dv_one)
        inverse = 1.0 / (roots[0:1, lane] * roots[0:1, lane])
        hid[tok, pl.ds(pl.multiple_of(2 * width + s * 128, 128), 128)] = dv.astype(LOW)
        gain = None
        for part, (g, v, scale) in enumerate(((dq, q, arq), (dk, keys, ark))):
            v = v.astype(FULL)
            dot = g * v
            gain = dot if gain is None else gain + dot
            g = g - v * (head_sum(dot) * inverse)
            g = g * tab[0, tok, :] - pltpu.roll(g, 112, 1) * tab[2, tok, :] - pltpu.roll(g, 16, 1) * tab[1, tok, :]
            hid[tok, pl.ds(pl.multiple_of(part * width + s * 128, 128), 128)] = (g * scale[w]).astype(LOW)
        dsc[0, pl.ds(s, 1), :] += jnp.sum(gain, axis=0, keepdims=True)
        return 0
    def project(half, t):
        def some(k, t):
            attend(half * in_half + 2 * k, 0)
            attend(half * in_half + 2 * k + 1, 0)
            now = k > 0
            @pl.when(now)
            def _(): step(t)
            return t + now.astype(jnp.int32)
        t = lax.fori_loop(0, in_half // 2, some, t)
        @pl.when(half == 0)
        def _():
            fill.wait()
            norm_rows(att, mods, 0, images, nrm)
        for part in range(3):
            i = first_qkv + half * 3 + part
            cut = hid[:, pl.ds(pl.multiple_of(part * width + half * CH, CH), CH)]
            produce(i, nrm[...], cut)
            acc[...] += nt(cut, weights(i))
            step(t + part)
        return t + 3
    t = lax.fori_loop(0, per, project, jnp.int32(done))

    def keep_one(q, value):
        down[q, :] = value.astype(LOW)
    norm_back(att, 0, lambda q, image: x1[q, :], keep_one)
    result = pltpu.make_async_copy(down, dtok, osem)
    result.start()
    dmx[f] = dmf[0 : 2 * images, :].astype(LOW).astype(FULL)
    def share(d, _):
        pltpu.make_async_remote_copy(src_ref=dmx.at[f], dst_ref=dmx.at[f], send_sem=msem.at[0, 0], recv_sem=msem.at[1, 0],
            device_id=((f + d) % shards, r), device_id_type=MESH).start()
        return 0
    lax.fori_loop(1, shards, share, 0)
    def swap(k, *to):
        return remote(dsc.at[k], dsr.at[k], msem.at[0, 2 + k], msem.at[1, 2 + k], *to)
    swap(0, z, 1 - x, y, c).start()
    step(t)
    wait_bytes(dmx.at[pl.ds(0, shards - 1)], msem.at[1, 0])
    acc[0 : 8 * shards, :] = jnp.zeros((8 * shards, width), FULL)
    def spread(k, _):
        acc[pl.ds(pl.multiple_of(k * 8, 8), 2 * images), :] = dmx[k]
        return 0
    lax.fori_loop(0, shards, spread, 0)
    flat = acc[0 : 8 * shards, :].astype(LOW)
    group = call[...].astype(FULL)[:, 0:8].reshape(shards * 8, 128)
    spot = lax.broadcasted_iota(jnp.int32, group.shape, 0) % 8
    for side in range(2):
        own_rows = jnp.where((spot >= side * images) & (spot < (side + 1) * images), group, 0.0).astype(LOW)
        pm[:, side * width : (side + 1) * width] = tn(own_rows, flat)[0 : pm.shape[0]].astype(LOW)
    core_swap = remote(pm, pr, msem.at[0, 5], msem.at[1, 5], z, x, y, 1 - c)
    core_swap.start()
    back_one = nt(flat, wm[:, 0:width])
    back_two = nt(flat, wm[:, width:])
    back_all = back_one + pltpu.roll(back_two, 8 * shards - images, 0)
    dpart[...] = back_all.reshape(shards, 8, 128)
    def back(d, _):
        to = (f + d) % shards
        pltpu.make_async_remote_copy(src_ref=dpart.at[to], dst_ref=dcr.at[f], send_sem=msem.at[0, 6], recv_sem=msem.at[1, 6],
            device_id=(to, r), device_id_type=MESH).start()
        return 0
    lax.fori_loop(1, shards, back, 0)
    dcr[f] = dpart[f]
    def settle(k):
        swap(k, z, x, y, c).wait()
        dsc[k + 1] = dsc[k] + dsr[k]
    settle(0)
    swap(1, z, x, 1 - y, c).start()
    step(t + 1)
    core_swap.wait()
    half_c = pl.ds(pl.multiple_of(c * width, 128), width)
    psum[...] = plus(pm[:, half_c], pr[:, half_c])
    y_swap = remote(psum, py, msem.at[0, 7], msem.at[1, 7], z, x, 1 - y, c)
    y_swap.start()
    settle(1)
    swap(2, z, x, y, 1 - c).start()
    step(t + 2)
    settle(2)
    dsr[3] = dsc[3]
    def round_z(d):
        return remote(dsr.at[3], dsr.at[4 + z], msem.at[0, 8], msem.at[1, 8], (z + d) % Z, x, y, c)
    for d in range(1, Z):
        round_z(d).start()
    dsr[4 + z] = dsc[3]
    step(t + 3)
    y_swap.wait()
    gmod[:, half_c] = plus(psum[...], py[...])
    last = remote(gmod.at[:, half_c], gmod.at[:, half_c], msem.at[0, 9], msem.at[1, 9], z, x, y, 1 - c)
    last.start()
    wait_bytes(dsr.at[pl.ds(4, Z - 1)], msem.at[1, 8])
    total = dsr[4]
    for k in range(1, Z):
        total = total + dsr[4 + k]
    sums = head_sum(total)
    inverse = jnp.zeros(sums.shape, FULL)
    line = lax.broadcasted_iota(jnp.int32, sums.shape, 0) * 2 + lax.broadcasted_iota(jnp.int32, sums.shape, 1) // 64
    for h in range(width // 64):
        inverse = jnp.where(line == h, 0.5 / jnp.full(sums.shape, scale[h], FULL), inverse)
    dscale[...] = sums * inverse
    step(t + 4)
    wait_bytes(dcr.at[pl.ds(0, shards - 1)], msem.at[1, 6])
    wide_c[...] = jnp.zeros_like(wide_c)
    def assemble(k, _):
        one = jnp.concatenate([dcr[k], jnp.zeros((8, wide_c.shape[1] - 128), FULL)], axis=1)
        lane = lax.broadcasted_iota(jnp.int32, one.shape, 1)
        wide_c[...] += pltpu.roll(jnp.where(lane < own_map, one, 0.0), k * own_map, 1)
        return 0
    lax.fori_loop(0, shards, assemble, 0)
    dcond[...] = wide_c[0:images, :]
    lax.fori_loop(t + 5, n + B_LAG[6], lambda s, _: (step(s), 0)[1], 0)
    last.wait()
    wait_bytes(dmx.at[pl.ds(0, shards - 1)], msem.at[0, 0])
    wait_bytes(dcr.at[pl.ds(0, shards - 1)], msem.at[0, 6])
    wait_bytes(dsr.at[pl.ds(4, Z - 1)], msem.at[0, 8])
    result.wait()
    finish()
    lax.fori_loop(0, n, lambda i, _: (wait_bytes(grads.at[i], gsem.at[i]), 0)[1], 0)


def backward(sigma, scale, cot, tokens, mods, wm, tab, roots, call, saved, own_map, wide_c):
    images = sigma.shape[0]
    rows, width = tokens.shape
    n, Z, _, R, w = saved[0].shape
    hidden = saved[9].shape[1]
    length = rows // images
    shards = 2 * Z
    n_c = rank_c(n)
    n_a = n - n_c
    rows_m = -(-own_map // 16) * 16
    vm, dma = pltpu.VMEM, pltpu.SemaphoreType.DMA
    wide = (rows, width)
    slab = (A_SLOTS, length, 128)
    scratch = [
        vm(wide, LOW), vm((rows, hidden), LOW), vm((rows, hidden), LOW), vm((rows, hidden), LOW), vm(wide, FULL), vm(wide, LOW),
        vm(wide, LOW), vm(wide, FULL), vm(wide, LOW), vm((B_SLOTS, Z, 2, R, w), LOW), vm(slab, LOW), vm(slab, LOW), vm(slab, LOW),
        vm(slab, FULL), vm(slab, FULL), vm((A_SLOTS, 2, length, length), LOW), vm((16, width), FULL), vm((shards, 2 * images, width), FULL),
        vm((rows_m, 2 * width), LOW), vm((rows_m, 2 * width), LOW), vm((rows_m, width), LOW), vm((rows_m, width), LOW),
        vm((shards, 8, 128), FULL), vm((shards, 8, 128), FULL), vm((4, width // 128, 128), FULL), vm((4 + Z, width // 128, 128), FULL),
        vm((8, wide_c), FULL), vm((images, 8, width), FULL),
        vm((n, R, w), LOW), vm((Q_SLOTS, Z, 2, R, w), LOW), vm((RING, Z, 2, R, w // 2), LOW), vm((n_a, Z, 2, R, w // 4), LOW),
        vm((n_a, Z, R, w // 4), LOW), vm((n_c, Z, R, w // 2), LOW), vm((n_a, Z - 1, R, w // 4), LOW), vm((n_c, Z - 1, R, w // 2), LOW),
        vm((n_c, R, w // 2), LOW),
        dma((6, n)), dma((6, n)), pltpu.SemaphoreType.REGULAR, dma((B_SLOTS,)), dma((7,)), dma((6, A_SLOTS)), dma((2, 10)), dma, dma((n,)),
    ]
    hbm, vmem = pl.BlockSpec(memory_space=pltpu.HBM), pl.BlockSpec(memory_space=pltpu.VMEM)
    smem = pl.BlockSpec(memory_space=pltpu.SMEM)
    array = jax.ShapeDtypeStruct
    return pl.pallas_call(
        functools.partial(backward_kernel, images, own_map),
        out_shape=(
            array((R, 3 * width), LOW), array((R, width), LOW), array((R, 2 * hidden), LOW), array((hidden // shards, width), LOW),
            array(wide, LOW), array((rows_m, 2 * width), LOW), array((images, wide_c), FULL), array((width // 128, 128), FULL),
        ),
        in_specs=[smem, smem, hbm, hbm] + [vmem] * 5 + [hbm] * 12,
        out_specs=tuple([hbm] * 5 + [vmem] * 3),
        scratch_shapes=scratch,
        compiler_params=pltpu.CompilerParams(collective_id=1, has_side_effects=True, vmem_limit_bytes=VMEM_LIMIT),
    )(sigma, scale, cot, tokens, mods, wm, tab, roots, call, *saved)


def local(tokens, cond, sigma_idx, pos_rows, pos_cols, attn_scale, w_mod1, w_qkv, w_out, w_mod2, w_up, w_down, cotangent):
    shards = lax.axis_size("fsdp")
    R, width = w_out.shape
    own, wide_c = w_mod1.shape[0], cond.shape[1]
    blocks = w_down.shape[0] // R
    regroup = R != 128
    if regroup:
        w_up = w_up.reshape(R, 2, shards, blocks, R).transpose(0, 1, 3, 2, 4).reshape(R, -1)
    pos = jnp.stack([pos_rows, pos_cols])
    (chunks, out, x1, qr, kr, vb, rq, rk, probs, att, h, ga, gb, mods, call, wm, tab, roots) = forward(
        tokens, cond, pos, w_mod1, w_mod2, attn_scale, w_qkv, w_out, w_up, w_down, shards
    )
    saved = (chunks, x1, qr, kr, vb, rq, rk, probs, att, h, ga, gb)
    g_qkv, g_out, g_up, g_down, d_tokens, g_mod, d_cond, d_scale = backward(
        sigma_idx, attn_scale, cotangent, tokens, mods, wm, tab, roots, call, saved, own, wide_c
    )
    d_scale = d_scale.reshape(attn_scale.shape[0], -1)[:, 0]
    if regroup:
        g_up = g_up.reshape(R, 2, blocks, shards, R).transpose(0, 1, 3, 2, 4).reshape(R, -1)
    g_mod = g_mod[:own].astype(FULL)
    return (
        out, d_tokens, d_cond, d_scale, g_mod[:, :width], g_qkv.astype(FULL), g_out.astype(FULL), g_mod[:, width:],
        g_up.astype(FULL), g_down.astype(FULL),
    )


def solution(mesh):
    placed = (
        P(("fsdp", "rep"), None),
        P(("fsdp", "rep"), None),
        P(("fsdp", "rep")),
        P(("fsdp", "rep")),
        P(("fsdp", "rep")),
        P(),
        P("fsdp", None),
        P("fsdp", None),
        P("fsdp", None),
        P("fsdp", None),
        P("fsdp", None),
        P("fsdp", None),
        P(("fsdp", "rep"), None),
    )
    return jax.shard_map(
        local,
        mesh=mesh,
        in_specs=placed,
        out_specs=(
            P(("fsdp", "rep"), None),
            P(("fsdp", "rep"), None),
            P(("fsdp", "rep"), None),
            P(),
            P("fsdp", None),
            P("fsdp", None),
            P("fsdp", None),
            P("fsdp", None),
            P("fsdp", None),
            P("fsdp", None),
        ),
        check_vma=False,
    )
```

```python
import functools
import math

import jax
import jax.numpy as jnp
from jax import lax
from jax.experimental import pallas as pl
from jax.experimental.pallas import tpu as pltpu
from jax.sharding import PartitionSpec as P

GRID = 16
NB = 64

MESH = pl.DeviceIdType.MESH
CH = 512

def place():
    f, r = lax.axis_index("fsdp"), lax.axis_index("rep")
    return f // 2, f % 2, r // 2, r % 2

def is_c(i):
    return i % 4 == 1

def remote(src, dst, send, recv, z, x, y, c):
    return pltpu.make_async_remote_copy(src_ref=src, dst_ref=dst, send_sem=send, recv_sem=recv,
        device_id=(z * 2 + x, y * 2 + c), device_id_type=MESH)

def wait_bytes(ref, sem):
    pltpu.make_async_copy(ref, ref, sem).wait()

def gather_ops(src, buf, sends, recvs, own):
    n, Z = buf.shape[0], buf.shape[1]
    z, x, y, c = place()
    zs, xs, ys, yt, cs, ct, cu, cv = (sends.at[k] for k in range(8))
    zr, xr, yr, yq, cr, cq, cp, co = (recvs.at[k] for k in range(8))
    def cols_of(width, k):
        return pl.ds(pl.multiple_of(k * width, 128), width)
    def both(i, fn):
        inside = (i >= 0) & (i < n)
        @pl.when(inside & jnp.logical_not(is_c(i)))
        def _(): fn(128, 2 * y + c, False)
        @pl.when(inside & is_c(i))
        def _(): fn(256, c, True)
    def inside_of(i, low, high, fn):
        @pl.when((i >= low) & (i < high))
        def _(): fn(i - low)
    def stage_z(i):
        low = 0
        for count, blocks_of in src:
            def start(j, i=i, blocks_of=blocks_of):
                for ref, first, width in blocks_of(j, 0, CH):
                    pltpu.make_async_copy(ref, buf.at[i, z, x, :, pl.ds(first, width)], own.at[i]).start()
                def go(width, k, cc):
                    for ref, first, w in blocks_of(j, k * width, width):
                        cols = pl.ds(pl.multiple_of(k * width + first, 128), w)
                        for d in range(1, Z):
                            remote(ref, buf.at[i, z, x, :, cols], zs.at[i], zr.at[i], (z + d) % Z, x, y, c).start()
                        remote(ref, buf.at[i, z, x, :, cols], xs.at[i], xr.at[i], z, 1 - x, y, c).start()
                both(i, go)
            inside_of(i, low, low + count, start)
            low += count
    def others(i, cols, send, recv, *to):
        for d in range(1, Z):
            zz = (z + d) % Z
            remote(buf.at[i, zz, x, :, cols], buf.at[i, zz, x, :, cols], send, recv, *to).start()
    def partner(i, cols, send, recv, *to):
        part = buf.at[i, :, 1 - x, :, cols]
        remote(part, part, send, recv, *to).start()
    def stage_x(i):
        def go(width, k, cc):
            cols = cols_of(width, k)
            wait_bytes(buf.at[i, 0:Z - 1, 0, :, cols], zr.at[i])
            others(i, cols, xs.at[i], xr.at[i], z, 1 - x, y, c)
            if not cc:
                others(i, cols, ys.at[i], yr.at[i], z, x, 1 - y, c)
            others(i, cols, cs.at[i], cr.at[i], z, x, y, 1 - c)
        both(i, go)
    def stage_y(i):
        def go(width, k, cc):
            cols = cols_of(width, k)
            wait_bytes(buf.at[i, :, 0, :, cols], xr.at[i])
            if not cc:
                partner(i, cols, yt.at[i], yq.at[i], z, x, 1 - y, c)
            partner(i, cols, ct.at[i], cq.at[i], z, x, y, 1 - c)
        both(i, go)
    def stage_c(i):
        def go(width, k, cc):
            if cc: return
            cols = cols_of(width, k)
            wait_bytes(buf.at[i, 0:Z - 1, 0, :, cols], yr.at[i])
            wait_bytes(buf.at[i, :, 0, :, cols], yq.at[i])
            mine = cols_of(128, 2 * (1 - y) + c)
            others(i, mine, cu.at[i], cp.at[i], z, x, y, 1 - c)
            partner(i, mine, cv.at[i], co.at[i], z, x, y, 1 - c)
        both(i, go)
    def core_waits(i, one, two, three, four):
        def go(width, k, cc):
            cols = pl.ds(0, width)
            wait_bytes(buf.at[i, 0:Z - 1, 0, :, cols], one.at[i])
            wait_bytes(buf.at[i, :, 0, :, cols], two.at[i])
            if not cc:
                wait_bytes(buf.at[i, 0:Z - 1, 0, :, cols], three.at[i])
                wait_bytes(buf.at[i, :, 0, :, cols], four.at[i])
        both(i, go)
    def ready(i):
        @pl.when((i >= 0) & (i < n))
        def _(): wait_bytes(buf.at[i, z, x], own.at[i])
        core_waits(i, cr, cq, cp, co)
    def finish(i):
        def go(width, k, cc):
            cols = cols_of(width, k)
            wait_bytes(buf.at[i, 0:Z - 1, 0, :, cols], zs.at[i])
            wait_bytes(buf.at[i, :, 0, :, cols], xs.at[i])
            if not cc:
                wait_bytes(buf.at[i, 0:Z - 1, 0, :, cols], ys.at[i])
                wait_bytes(buf.at[i, :, 0, :, cols], yt.at[i])
        both(i, go)
        core_waits(i, cs, ct, cu, cv)
    return stage_z, stage_x, stage_y, stage_c, ready, finish


EPS = 1e-06
LOW = jnp.bfloat16
FULL = jnp.float32
VMEM_LIMIT = 60 * 2**20
F_LAG = (0, 2, 4, 6, 7)
F_LATE = 3
W_SLOTS = 3


def nn(a, b):
    return jnp.dot(a, b, preferred_element_type=FULL)


def nt(a, b):
    return lax.dot_general(a, b, (((1,), (1,)), ((), ())), preferred_element_type=FULL)


def tn(a, b):
    return lax.dot_general(a, b, (((0,), (0,)), ((), ())), preferred_element_type=FULL)


def at(k, size):
    return pl.ds(pl.multiple_of(k * size, size), size)


def head_sum(v):
    one = lax.broadcasted_iota(jnp.int32, (128, 128), 0) // 64
    two = lax.broadcasted_iota(jnp.int32, (128, 128), 1) // 64
    same = (one == two).astype(LOW)
    high = v.astype(LOW)
    rest = v - high.astype(FULL)
    return nn(high, same) + nn(rest.astype(LOW), same)


def head_mask(rows, second):
    lane = lax.broadcasted_iota(jnp.int32, (rows, 128), 1)
    return (lane >= 64) if second else (lane < 64)


def turn(v, cosine, sine_up, sine_down):
    return v * cosine + pltpu.roll(v, 16, 1) * sine_up + pltpu.roll(v, 112, 1) * sine_down


def norm_rows(src_ref, mods_ref, side, images, dst_ref, x_ref=None):
    rows, width = src_ref.shape
    length = rows // images
    block = 64
    def body(i, _):
        r = at(i, block)
        v = src_ref[r, :].astype(FULL)
        factor = lax.rsqrt(jnp.mean(v * v, axis=1, keepdims=True) + EPS)
        m = mods_ref[pl.ds(i // (length // block), 1), side * width : (side + 1) * width]
        dst_ref[r, :] = (v * factor * (1.0 + m)).astype(LOW)
        return 0
    lax.fori_loop(0, rows // block, body, 0)


def three(v):
    one = v.astype(LOW)
    rest = v - one.astype(FULL)
    two = rest.astype(LOW)
    return one, two, (rest - two.astype(FULL)).astype(LOW)


def rope_tables(pos, tab, head):
    grid = lax.broadcasted_iota(jnp.int32, (2 * GRID, 128), 0)
    lane = lax.broadcasted_iota(jnp.int32, (2 * GRID, 128), 1) % head
    pairs = head // 4
    quarter = pairs // 2
    j = lane % pairs
    place = ((grid % GRID).astype(FULL) + 0.5) * (2.0 / GRID) - 1.0
    freq = math.pi * jnp.exp(math.log(10.0) * (j % quarter).astype(FULL) / max(quarter - 1, 1))
    angle = place * freq
    mine = (lane < 2 * pairs) & ((grid // GRID) == (j // quarter))
    cos, sin = jnp.cos(angle), jnp.sin(angle)
    zero = jnp.zeros_like(cos)
    kinds = (
        jnp.where(mine, cos, zero),
        jnp.where(mine & (lane >= pairs), sin, zero),
        jnp.where(mine & (lane < pairs), -sin, zero),
    )
    rows = pos.shape[1]
    spot = lax.broadcasted_iota(jnp.int32, (GRID, rows), 0)
    hot = jnp.concatenate([(spot == pos[0:1, :]).astype(FULL), (spot == pos[1:2, :]).astype(FULL)], axis=0).astype(LOW)
    for k, kind in enumerate(kinds):
        total = None
        for part in three(kind):
            one = tn(hot, part)
            total = one if total is None else total + one
        if k == 0:
            plain = lax.broadcasted_iota(jnp.int32, (rows, 128), 1) % head >= 2 * pairs
            total = total + plain.astype(FULL)
        tab[k] = total


def forward_kernel(
    images, heads, tokens, cond, pos, w_mod1, w_mod2, scale, w_qkv, w_out, w_up, w_down,
    buf, out, x1_o, qr_o, kr_o, vb_o, rq_o, rk_o, p_o, o_o, h_o, ga_o, gb_o, mods_o, call_o, wm_o, tab_o, roots_o,
    n1, qkv, rqk, probs, att, x1, n2, hid, ga, gb, up, acc, slots, mods, call, mpart, mrecv, cparts, wide_c, wm, tab, roots,
    sends, recvs, own, wsem, osem, csem, msem,
):
    n, Z, R = buf.shape[0], buf.shape[1], buf.shape[3]
    shards = 2 * Z
    rows, width = tokens.shape
    hidden = hid.shape[1]
    length = rows // images
    half_heads = width // CH
    z, x, y, c = place()
    f = z * 2 + x
    r = y * 2 + c
    barrier = pltpu.get_barrier_semaphore()
    def greet(d, _):
        pl.semaphore_signal(barrier, inc=1, device_id=((f + d) % shards, r), device_id_type=MESH)
        return 0
    lax.fori_loop(1, shards, greet, 0)
    for where in ((f, (1 - y) * 2 + c), (f, y * 2 + 1 - c)):
        pl.semaphore_signal(barrier, inc=1, device_id=where, device_id_type=MESH)
    wide_c[...] = jnp.zeros_like(wide_c)
    for k in range(2):
        wide_c[k * images : (k + 1) * images, :] = cond[...].astype(FULL)
    map_rows = w_mod1.shape[0]
    def cut(k, _):
        full = wide_c.shape[1]
        moved = pltpu.roll(wide_c[...], (full - k * map_rows) % full, 1)[:, 0:128]
        lane = lax.broadcasted_iota(jnp.int32, moved.shape, 1)
        cparts[k] = jnp.where(lane < map_rows, moved, 0.0).astype(LOW)
        return 0
    lax.fori_loop(0, shards, cut, 0)
    call[f] = cparts[f]
    pl.semaphore_wait(barrier, shards + 1)

    blocks = w_down.shape[0] // R
    def columns(ref, at_row, at_col):
        def of(j, first, size):
            return [(ref.at[at_row(j), pl.ds(pl.multiple_of(at_col(j) + first, 128), size)], 0, size)]
        return of
    every = lambda j: slice(None)
    def of_up(j, first, size):
        if R != 128:
            return columns(w_up, every, lambda j: (j % 2) * hidden + (j // 2) * CH)(j, first, size)
        found = []
        for b in range(size // 128):
            unit = (j // 2) * (CH // 128) + first // 128 + b
            spot = (j % 2) * hidden + ((unit % shards) * blocks + unit // shards) * 128
            found.append((w_up.at[:, pl.ds(pl.multiple_of(spot, 128), 128)], b * 128, 128))
        return found
    src = [
        (3 * half_heads, columns(w_qkv, every, lambda j: (j % 3) * width + (j // 3) * CH)),
        (half_heads, columns(w_out, every, lambda j: j * CH)),
        (2 * hidden // CH, of_up),
        (blocks * half_heads, columns(w_down, lambda j: at(j // half_heads, R), lambda j: (j % half_heads) * CH)),
    ]
    stage_z, stage_x, stage_y, stage_c, ready, finish = gather_ops(src, buf, sends, recvs, own)

    def give(d, _):
        to = (f + d) % shards
        pltpu.make_async_remote_copy(src_ref=cparts.at[to], dst_ref=call.at[f], send_sem=csem.at[0], recv_sem=csem.at[1],
            device_id=(to, r), device_id_type=MESH).start()
        return 0

    def load(j):
        return pltpu.make_async_copy(buf.at[j], slots.at[j % W_SLOTS], wsem.at[j % W_SLOTS])

    def step(t):
        @pl.when(t >= 2)
        def _(): stage_z(t)
        stage_x(t - F_LAG[1])
        stage_y(t - F_LAG[2])
        stage_c(t - F_LAG[3])
        ready(t - F_LAG[4])
        finish(t - F_LAG[4] - F_LATE)
        @pl.when((t >= F_LAG[4]) & (t < n + F_LAG[4]))
        def _(): load(t - F_LAG[4]).start()

    def begin(j):
        step(j + F_LAG[4] + 1)
        load(j).wait()
        return j % W_SLOTS

    def weights(slot):
        return slots[slot].reshape(width, CH)

    stage_z(0)
    lax.fori_loop(1, shards, give, 0)
    stage_z(1)
    for side, ref in enumerate((w_mod1, w_mod2)):
        acc[0:128, :] = jnp.zeros((128, width), FULL)
        acc[0:map_rows, :] = ref[...].astype(FULL)
        wm[:, side * width : (side + 1) * width] = acc[0:128, :].astype(LOW)
    step(2)
    wait_bytes(call.at[pl.ds(0, shards - 1)], csem.at[1])
    flat = call[...].reshape(shards * 16, 128)
    mpart[...] = nn(flat, wm[...]).reshape(shards, 16, 2 * width)[:, 0:images]
    def back(d, _):
        to = (f + d) % shards
        pltpu.make_async_remote_copy(src_ref=mpart.at[to], dst_ref=mrecv.at[f], send_sem=msem.at[0], recv_sem=msem.at[1],
            device_id=(to, r), device_id_type=MESH).start()
        return 0
    lax.fori_loop(1, shards, back, 0)
    mrecv[f] = mpart[f]
    step(3)
    which = lax.broadcasted_iota(jnp.int32, roots.shape, 1) // (width // heads)
    row = jnp.zeros(roots.shape, FULL)
    for h in range(heads):
        row = jnp.where(which == h, scale[h], row)
    roots[...] = jnp.sqrt(row)
    rope_tables(pos, tab, width // heads)
    step(4)
    wait_bytes(mrecv.at[pl.ds(0, shards - 1)], msem.at[1])
    mods[...] = jnp.zeros_like(mods)
    total = mrecv[0]
    for k in range(1, shards):
        total = total + mrecv[k]
    mods[0:images, :] = total
    step(5)
    norm_rows(tokens, mods, 0, images, n1)
    lax.fori_loop(6, F_LAG[4] + 1, lambda t, _: (step(t), 0)[1], 0)

    def project(half, _):
        lanes_of = lambda s: pl.ds(pl.multiple_of(half * CH + s * 128, 128), 128)
        for part in range(2):
            slot = begin(half * 3 + part)
            v = nn(n1[...], weights(slot))
            for s in range(CH // 128):
                one = v[:, s * 128 : (s + 1) * 128]
                scale = lax.rsqrt(head_sum(one * one) + EPS) * roots[0:1, lanes_of(s)]
                rqk[part, :, lanes_of(s)] = scale
                qkv[part, :, lanes_of(s)] = turn(one * scale, tab[0], tab[1], tab[2]).astype(LOW)
        slot = begin(half * 3 + 2)
        qkv[2, :, at(half, CH)] = nn(n1[...], weights(slot)).astype(LOW)
        def pair(k, _):
            image, s = k // (CH // 128), k % (CH // 128)
            tok = at(image, length)
            lane = pl.ds(pl.multiple_of(half * CH + s * 128, 128), 128)
            q, keys, val = qkv[0, tok, lane], qkv[1, tok, lane], qkv[2, tok, lane]
            total = None
            for second in range(2):
                mask = head_mask(length, second)
                scores = jnp.exp(nt(jnp.where(mask, q, jnp.zeros_like(q)), keys))
                p = (scores * (1.0 / jnp.sum(scores, axis=1, keepdims=True))).astype(LOW)
                probs[half * (CH // 128) + s, image, second] = p
                o = nn(p, jnp.where(mask, val, jnp.zeros_like(val)))
                total = o if total is None else total + o
            att[tok, lane] = total.astype(LOW)
            return 0
        lax.fori_loop(0, images * (CH // 128), pair, 0)
        return 0
    lax.fori_loop(0, half_heads, project, 0)
    outs = [
        (qkv.at[0], qr_o), (qkv.at[1], kr_o), (qkv.at[2], vb_o), (rqk.at[0], rq_o), (rqk.at[1], rk_o), (probs, p_o), (att, o_o),
        (mods, mods_o), (call, call_o), (wm, wm_o), (tab, tab_o), (roots, roots_o),
    ]
    later = [(x1, x1_o), (hid, h_o), (ga, ga_o), (gb, gb_o), (n2, out)]
    copies = [pltpu.make_async_copy(a, b, osem.at[k]) for k, (a, b) in enumerate(outs + later)]
    for k in range(len(outs)):
        copies[k].start()

    at_out = 3 * half_heads
    def project_out(j, _):
        slot = begin(at_out + j)
        lane = at(j, CH)
        x1[:, lane] = tokens[:, lane].astype(FULL) + nn(att[...], weights(slot))
        return 0
    lax.fori_loop(0, half_heads, project_out, 0)
    copies[len(outs)].start()
    norm_rows(x1, mods, 1, images, n2)

    at_up = at_out + half_heads
    def widen(j, _):
        up[...] = nn(n2[...], weights(begin(at_up + 2 * j)))
        gate = nn(n2[...], weights(begin(at_up + 2 * j + 1)))
        lane_of = lambda s: pl.ds(pl.multiple_of(j * CH + s * 128, 128), 128)
        for s in range(CH // 128):
            g = gate[:, s * 128 : (s + 1) * 128]
            u = up[:, s * 128 : (s + 1) * 128]
            phi = 0.5 + 0.5 * lax.erf(g * math.sqrt(0.5))
            gelu = g * phi
            slope = phi + g * (jnp.exp(-0.5 * g * g) * (1.0 / math.sqrt(2.0 * math.pi)))
            hid[:, lane_of(s)] = (u * gelu).astype(LOW)
            ga[:, lane_of(s)] = gelu.astype(LOW)
            gb[:, lane_of(s)] = (u * slope).astype(LOW)
        return 0
    lax.fori_loop(0, hidden // CH, widen, 0)
    for k in range(1, 4):
        copies[len(outs) + k].start()

    at_down = at_up + 2 * hidden // CH
    def narrow(k, _):
        for j in range(width // CH):
            slot = begin(at_down + k * (width // CH) + j)
            part = nn(hid[:, at(k, width)], weights(slot))
            cols = slice(j * CH, (j + 1) * CH)
            acc[:, cols] = part + jnp.where(k == 0, x1[:, cols], acc[:, cols])
        return 0
    lax.fori_loop(0, hidden // width, narrow, 0)
    n2[...] = acc[...].astype(LOW)
    copies[-1].start()
    for copy in copies:
        copy.wait()
    lax.fori_loop(n + 1 - F_LATE, n, lambda i, _: (finish(i), 0)[1], 0)
    wait_bytes(call.at[pl.ds(0, shards - 1)], csem.at[0])
    wait_bytes(mrecv.at[pl.ds(0, shards - 1)], msem.at[0])


def forward(tokens, cond, pos, w_mod1, w_mod2, scale, w_qkv, w_out, w_up, w_down, shards):
    rows, width = tokens.shape
    R, hidden = w_out.shape[0], w_up.shape[1] // 2
    images, wide_c = cond.shape
    Z, w = shards // 2, CH
    n = (w_qkv.shape[1] + w_out.shape[1] + w_up.shape[1]) // CH + (w_down.shape[0] // R) * (width // CH)
    length = rows // images
    pairs = width // 128
    array = jax.ShapeDtypeStruct
    wide = (rows, width)
    out_shape = (
        array((n, Z, 2, R, w), LOW), array(wide, LOW), array(wide, FULL), array(wide, LOW), array(wide, LOW), array(wide, LOW),
        array(wide, FULL), array(wide, FULL), array((pairs, images, 2, length, length), LOW), array(wide, LOW),
        array((rows, hidden), LOW), array((rows, hidden), LOW), array((rows, hidden), LOW), array((8, 2 * width), FULL),
        array((shards, 16, 128), LOW), array((128, 2 * width), LOW), array((3, rows, 128), FULL), array((8, width), FULL),
    )
    vm, dma = pltpu.VMEM, pltpu.SemaphoreType.DMA
    scratch = [
        vm(wide, LOW), vm((3, *wide), LOW), vm((2, *wide), FULL), vm((pairs, images, 2, length, length), LOW), vm(wide, LOW),
        vm(wide, FULL), vm(wide, LOW), vm((rows, hidden), LOW), vm((rows, hidden), LOW), vm((rows, hidden), LOW),
        vm((rows, w), FULL), vm(wide, FULL), vm((W_SLOTS, Z, 2, R, w), LOW), vm((8, 2 * width), FULL), vm((shards, 16, 128), LOW),
        vm((shards, images, 2 * width), FULL), vm((shards, images, 2 * width), FULL), vm((shards, 16, 128), LOW), vm((16, wide_c), FULL),
        vm((128, 2 * width), LOW), vm((3, rows, 128), FULL), vm((8, width), FULL),
        dma((8, n)), dma((8, n)), dma((n,)), dma((W_SLOTS,)), dma((17,)), dma((2,)), dma((2,)),
    ]
    hbm, vmem = pl.BlockSpec(memory_space=pltpu.HBM), pl.BlockSpec(memory_space=pltpu.VMEM)
    smem = pl.BlockSpec(memory_space=pltpu.SMEM)
    return pl.pallas_call(
        functools.partial(forward_kernel, images, scale.shape[0]),
        out_shape=out_shape,
        in_specs=[vmem] * 5 + [smem] + [hbm] * 4,
        out_specs=tuple([hbm] * len(out_shape)),
        scratch_shapes=scratch,
        compiler_params=pltpu.CompilerParams(collective_id=0, has_side_effects=True, vmem_limit_bytes=VMEM_LIMIT),
    )(tokens, cond, pos, w_mod1, w_mod2, scale, w_qkv, w_out, w_up, w_down)


Q_SLOTS = 9
RING = 7
A_SLOTS = 2
B_SLOTS = 2
B_LAG = (0, 1, 3, 5, 7, 9, 11, 12)


def plus(a, b):
    return (a.astype(FULL) + b.astype(FULL)).astype(LOW)


def scatter_ops(n, queue, rc, ry, rxa, rxc, rza, rzc, rya, ryc, rl, out, sends, recvs, credit, gsem, put):
    half_z = rc.shape[1]
    Z = 2 * half_z
    z, x, y, c = place()
    def cols(k, width):
        return pl.ds(pl.multiple_of(k * width, 128), width)
    def inside(i, fn):
        @pl.when((i >= 0) & (i < n))
        def _(): fn(i % 2)
    def by_kind(i, fn_a, fn_c):
        ok = (i >= 0) & (i < n)
        @pl.when(ok & (z % 2 != i % 2))
        def _(): fn_a()
        @pl.when(ok & (z % 2 == i % 2))
        def _(): fn_c()
    def each(fn):
        lax.fori_loop(0, half_z, lambda k, _: (fn(k), 0)[1], 0)
    def s0(i):
        def go(p):
            @pl.when(i >= RING)
            def _(): pl.semaphore_wait(credit, 1)
            remote(queue.at[i % Q_SLOTS, :, :, :, :, cols(1 - c, 256)], rc.at[i % RING], sends.at[0, i], recvs.at[0, i], z, x, y, 1 - c).start()
        inside(i, go)
    def free(i):
        @pl.when(i >= 0)
        def _(): wait_bytes(rc.at[0], sends.at[0, i])
    def s1(i):
        w = i % RING
        def go(p):
            wait_bytes(rc.at[w], recvs.at[0, i])
            def one(k):
                rc[w, k] = plus(rc[w, k], queue[i % Q_SLOTS, k, :, :, :, cols(c, 256)])
            each(one)
            remote(rc.at[w, :, 1 - p, :, :, cols(1 - y, 128)], ry.at[i], sends.at[1, i], recvs.at[1, i], z, x, 1 - y, c).start()
            remote(rc.at[w, :, p, 1 - x], rxc.at[i], sends.at[2, i], recvs.at[2, i], z, 1 - x, y, c).start()
        inside(i, go)
    mate = z + 1 - 2 * (z % 2)
    def next_door(i, rx, rz, row):
        remote(rx.at[i], rz.at[i // 2], sends.at[row, i], recvs.at[row, i], mate, x, y, c).start()
    def far(i, rx, rz, row):
        for d in range(1, half_z):
            to = (z // 2 + d) % half_z
            remote(rx.at[i, to], rz.at[i // 2, d - 1], sends.at[row, i], recvs.at[row, i], 2 * to + z % 2, x, y, c).start()
    def join(i, rx, rz):
        def one(k):
            rx[i, k] = plus(rx[i, k], rz[i // 2, k])
        each(one)
    def s2(i):
        w = i % RING
        def go(p):
            wait_bytes(ry.at[i], recvs.at[1, i])
            def one(k):
                ry[i, k] = plus(ry[i, k], rc[w, k, 1 - p, :, :, cols(y, 128)])
            each(one)
            remote(ry.at[i, :, 1 - x], rxa.at[i], sends.at[3, i], recvs.at[3, i], z, 1 - x, y, c).start()
            wait_bytes(rxc.at[i], recvs.at[2, i])
            def two(k):
                rxc[i, k] = plus(rxc[i, k], rc[w, k, p, x])
            each(two)
            @pl.when(z % 2 != p)
            def _(): next_door(i, rxc, rzc, 4)
            wait_bytes(ry.at[i], sends.at[1, i])
            wait_bytes(rxc.at[i], sends.at[2, i])
            @pl.when(i + RING < n)
            def _(): pl.semaphore_signal(credit, inc=1, device_id=(z * 2 + x, y * 2 + 1 - c), device_id_type=MESH)
        inside(i, go)
    def total(rx, rz, i):
        s = rx[i, z // 2].astype(FULL)
        for d in range(1, half_z):
            s = s + rz[i // 2, d - 1].astype(FULL)
        return s.astype(LOW)
    def arrived(i, rz, row):
        if half_z > 1:
            wait_bytes(rz.at[i // 2], recvs.at[row, i])
    def s3(i):
        def go(p):
            wait_bytes(rxa.at[i], recvs.at[3, i])
            def one(k):
                rxa[i, k] = plus(rxa[i, k], ry[i, k, x])
            each(one)
            @pl.when(z % 2 == p)
            def _(): next_door(i, rxa, rza, 5)
        inside(i, go)
        def cc():
            wait_bytes(rzc.at[i // 2], recvs.at[4, i])
            join(i, rxc, rzc)
            far(i, rxc, ryc, 8)
        by_kind(i, lambda: None, cc)
    def fwd(i):
        mine = out.at[i, :, cols(c, 256)]
        remote(mine, mine, sends.at[7, i], recvs.at[7, i], z, x, y, 1 - c).start()
    def s4(i):
        def a():
            wait_bytes(rza.at[i // 2], recvs.at[5, i])
            join(i, rxa, rza)
            far(i, rxa, rya, 8)
        def cc():
            arrived(i, ryc, 8)
            mine = out.at[i, :, cols(c, 256)]
            out[i, :, cols(c, 256)] = total(rxc, ryc, i)
            remote(mine, rl.at[i // 2], sends.at[6, i], recvs.at[6, i], z, x, 1 - y, c).start()
        by_kind(i, a, cc)
    def final(i):
        wait_bytes(rl.at[0], sends.at[7, i])
        wait_bytes(rl.at[0], recvs.at[7, i])
        put(i)
    def s5(i):
        def a():
            arrived(i, rya, 8)
            mine = out.at[i, :, cols(2 * c + y, 128)]
            out[i, :, cols(2 * c + y, 128)] = total(rxa, rya, i)
            remote(mine, mine, sends.at[6, i], recvs.at[6, i], z, x, 1 - y, c).start()
        def cc():
            wait_bytes(rl.at[0], recvs.at[6, i])
            wait_bytes(rl.at[0], sends.at[6, i])
            out[i, :, cols(c, 256)] = plus(out[i, :, cols(c, 256)], rl[i // 2])
            fwd(i)
        by_kind(i, a, cc)
    def s6(i):
        def a():
            wait_bytes(out.at[i, :, pl.ds(0, 128)], recvs.at[6, i])
            wait_bytes(out.at[i, :, pl.ds(0, 128)], sends.at[6, i])
            fwd(i)
        by_kind(i, a, lambda: final(i))
    def s7(i):
        by_kind(i, lambda: final(i), lambda: None)
    def finish(i):
        def go(p):
            wait_bytes(rxa.at[i], sends.at[3, i])
            wait_bytes(out.at[i], gsem.at[i])
        inside(i, go)
        def a():
            wait_bytes(rzc.at[0], sends.at[4, i])
            if half_z > 1:
                wait_bytes(rya.at[0], sends.at[8, i])
        def cc():
            wait_bytes(rza.at[0], sends.at[5, i])
            if half_z > 1:
                wait_bytes(ryc.at[0], sends.at[8, i])
        by_kind(i, a, cc)
    return s0, free, s1, s2, s3, s4, s5, s6, s7, finish


def backward_kernel(
    images, own_map, sigma, scale, cot, tokens, mods, wm, tab, roots, call,
    buf, x1_h, qr_h, kr_h, vb_h, rq_h, rk_h, p_h, o_h, h_h, ga_h, gb_h,
    g_qkv, g_out, g_up, g_down, dtok, gmod, dcond, dscale,
    down, hid, ga, gb, x1, nrm, att, acc, dob, slots, aq, ak, av, arq, ark, ap, dmf, dmx, pm, pr, psum, py, dpart, dcr, dsc, dsr, wide_c, weight,
    grads, queue, rc, ry, rxa, rxc, rza, rzc, rya, ryc, rl, sends, recvs, credit, wsem, lsem, asem, msem, osem, gsem,
):
    n, Z, R = buf.shape[0], buf.shape[1], buf.shape[3]
    shards = 2 * Z
    rows, width = tokens.shape
    hidden = hid.shape[1]
    length = rows // images
    per = width // CH
    n_down, n_up, n_out = hidden // width * per, 2 * hidden // CH, per
    z, x, y, c = place()
    f = z * 2 + x
    r = y * 2 + c
    barrier = pltpu.get_barrier_semaphore()
    def greet(d, _):
        pl.semaphore_signal(barrier, inc=1, device_id=((f + d) % shards, r), device_id_type=MESH)
        return 0
    lax.fori_loop(1, shards, greet, 0)
    for where in ((f, (1 - y) * 2 + c), (f, y * 2 + 1 - c)):
        pl.semaphore_signal(barrier, inc=1, device_id=where, device_id_type=MESH)
    given = pltpu.make_async_copy(cot, dob, lsem.at[6])
    given.start()
    loads = [pltpu.make_async_copy(a, b, lsem.at[k]) for k, (a, b) in enumerate(
        [(h_h, hid), (ga_h, ga), (gb_h, gb), (x1_h, x1), (o_h, att)])]
    for one in loads:
        one.start()
    def chunk_of(s):
        first = jnp.where(s < n_down, n - n_down + s, 3 * per + n_out + s - n_down)
        last = jnp.where(s < n_down + n_up + n_out, 3 * per + s - n_down - n_up, s - n_down - n_up - n_out)
        return jnp.where(s < n_down + n_up, first, last)
    def load(s):
        return pltpu.make_async_copy(buf.at[chunk_of(s)], slots.at[s % B_SLOTS], wsem.at[s % B_SLOTS])
    load(0).start()
    def weights(s):
        load(s).wait()
        @pl.when(s + 1 < n)
        def _(): load(s + 1).start()
        return slots[s % B_SLOTS].reshape(width, CH)

    blocks_d = hidden // width
    def put(i):
        def within(low, high, fn):
            @pl.when((i >= low) & (i < high))
            def _(): fn(i - low)
        def copy(src, dst):
            pltpu.make_async_copy(src, dst, gsem.at[i]).start()
        within(0, n_down, lambda j: copy(grads.at[i], g_down.at[at(j // per, R), at(j % per, CH)]))
        def to_up(j):
            side, first = j % 2, j // 2
            if R != 128:
                copy(grads.at[i], g_up.at[:, pl.ds(pl.multiple_of(side * hidden + first * CH, 128), CH)])
                return
            for b in range(CH // 128):
                unit = first * (CH // 128) + b
                spot = side * hidden + ((unit % shards) * blocks_d + unit // shards) * 128
                copy(grads.at[i, :, pl.ds(b * 128, 128)], g_up.at[:, pl.ds(pl.multiple_of(spot, 128), 128)])
        within(n_down, n_down + n_up, to_up)
        within(n_down + n_up, n_down + n_up + n_out, lambda j: copy(grads.at[i], g_out.at[:, at(j, CH)]))
        within(n_down + n_up + n_out, n, lambda j: copy(grads.at[i], g_qkv.at[:, pl.ds(pl.multiple_of((j % 3) * width + (j // 3) * CH, CH), CH)]))
    s0, free, s1, s2, s3, s4, s5, s6, s7, finish = scatter_ops(n, queue, rc, ry, rxa, rxc, rza, rzc, rya, ryc, rl, grads, sends, recvs, credit, gsem, put)
    def step(t):
        s0(t - B_LAG[0])
        s1(t - B_LAG[1])
        s2(t - B_LAG[2])
        s3(t - B_LAG[3])
        s4(t - B_LAG[4])
        s5(t - B_LAG[5])
        s6(t - B_LAG[6])
        s7(t - B_LAG[7])
        finish(t - B_LAG[7] - 1)
    def produce(i, left, right):
        free(i - Q_SLOTS)
        queue[i % Q_SLOTS] = tn(left, right).astype(LOW).reshape(Z // 2, 2, 2, R, CH)

    block = 64
    def blocks(fn):
        lax.fori_loop(0, rows // block, lambda i, _: (fn(at(i, block), i // (length // block)), 0)[1], 0)
    def weigh(k, image):
        down[k, :] = (dob[k, :].astype(FULL) * weight[image, 0:1, :]).astype(LOW)
    for image in range(images):
        level = jnp.full(weight.shape[1:], sigma[image].astype(FULL), FULL) / (NB - 1)
        noise = jnp.exp(-2.0 + 3.2 * level)
        weight[image] = 1.0 / (1.0 + 4.0 * noise * noise) + 0.25
    given.wait()
    blocks(weigh)
    dmf[...] = jnp.zeros_like(dmf)
    dsc[...] = jnp.zeros_like(dsc)
    pl.semaphore_wait(barrier, shards + 1)
    loads[0].wait()

    def second_product(i):
        produce(i, hid[:, at(i // per, width)], down[:, at(i % per, CH)])
    for i in range(2):
        second_product(i)
        step(i)
    loads[1].wait()
    loads[2].wait()
    def narrow(k, _):
        second_product(k + 2)
        step(k + 2)
        for j in range(per):
            part = nt(down[:, j * CH : (j + 1) * CH], weights(k * per + j))
            acc[...] = part if j == 0 else acc[...] + part
        def gate(q, image):
            ga[q, at(k, width)] = (acc[q, :] * ga[q, at(k, width)].astype(FULL)).astype(LOW)
            gb[q, at(k, width)] = (acc[q, :] * gb[q, at(k, width)].astype(FULL)).astype(LOW)
        blocks(gate)
        return 0
    lax.fori_loop(0, blocks_d, narrow, 0)
    for i in range(2 + blocks_d, n_down):
        second_product(i)
    done = 2 + blocks_d

    loads[3].wait()
    norm_rows(x1, mods, 1, images, nrm)
    acc[...] = jnp.zeros_like(acc)
    def widen(j, _):
        step(done + j)
        for side, ref in ((0, ga), (1, gb)):
            s = n_down + 2 * j + side
            produce(s, nrm[...], ref[:, at(j, CH)])
            acc[...] += nt(ref[:, at(j, CH)], weights(s))
        return 0
    lax.fori_loop(0, n_up // 2, widen, 0)
    done += n_up // 2

    def norm_back(src_ref, side, base, dst):
        def one(q, image):
            v = src_ref[q, :].astype(FULL)
            dn = acc[q, :]
            factor = lax.rsqrt(jnp.mean(v * v, axis=1, keepdims=True) + EPS)
            m = mods[pl.ds(image, 1), side * width : (side + 1) * width]
            g = dn * (1.0 + m)
            mean = jnp.mean(v * g, axis=1, keepdims=True)
            dst(q, base(q, image) + factor * g - v * (factor * factor * factor * mean))
            dmf[pl.ds(side * images + image, 1), :] += jnp.sum(v * factor * dn, axis=0, keepdims=True)
        blocks(one)
    def keep_two(q, value):
        x1[q, :] = value
        down[q, :] = value.astype(LOW)
    norm_back(x1, 1, lambda q, image: dob[q, :].astype(FULL) * weight[image, 0:1, :], keep_two)

    step(done)
    done += 1

    loads[4].wait()
    first_out = n_down + n_up
    for j in range(per):
        right = down[:, j * CH : (j + 1) * CH]
        produce(first_out + j, att[...], right)
        part = nt(right, weights(first_out + j))
        acc[...] = part if j == 0 else acc[...] + part
        step(done)
        done += 1
    dob[...] = acc[...].astype(LOW)
    fill = pltpu.make_async_copy(tokens, att, lsem.at[5])
    fill.start()

    pairs_half = CH // 128
    in_half = images * pairs_half
    def spots(k):
        half, rest = k // in_half, k % in_half
        image, s = rest // pairs_half, half * pairs_half + rest % pairs_half
        return image, s, at(image, length), pl.ds(pl.multiple_of(s * 128, 128), 128)
    def fetch(k):
        image, s, tok, lane = spots(k)
        w = k % A_SLOTS
        refs = [(qr_h.at[tok, lane], aq), (kr_h.at[tok, lane], ak), (vb_h.at[tok, lane], av), (rq_h.at[tok, lane], arq), (rk_h.at[tok, lane], ark), (p_h.at[s, image], ap)]
        return [pltpu.make_async_copy(a, b.at[w], asem.at[e, w]) for e, (a, b) in enumerate(refs)]
    for one in fetch(0):
        one.start()
    acc[...] = jnp.zeros_like(acc)
    total_pairs = images * (width // 128)
    first_qkv = first_out + n_out
    def attend(k, _):
        image, s, tok, lane = spots(k)
        w = k % A_SLOTS
        for one in fetch(k):
            one.wait()
        @pl.when(k + 1 < total_pairs)
        def _():
            for one in fetch(k + 1):
                one.start()
        q, keys, val, dout = aq[w], ak[w], av[w], dob[tok, lane]
        zero = jnp.zeros_like(q)
        dq = dk = dv = None
        for second in range(2):
            mask = head_mask(length, second)
            d_one = jnp.where(mask, dout, zero)
            p = ap[w, second]
            pf = p.astype(FULL)
            dp = nt(d_one, val)
            ds = (pf * (dp - jnp.sum(dp * pf, axis=1, keepdims=True))).astype(LOW)
            dv_one = tn(p, d_one)
            dq_one = nn(ds, jnp.where(mask, keys, zero))
            dk_one = tn(ds, jnp.where(mask, q, zero))
            dq, dk, dv = (dq_one, dk_one, dv_one) if dq is None else (dq + dq_one, dk + dk_one, dv + dv_one)
        inverse = 1.0 / (roots[0:1, lane] * roots[0:1, lane])
        hid[tok, pl.ds(pl.multiple_of(2 * width + s * 128, 128), 128)] = dv.astype(LOW)
        gain = None
        for part, (g, v, scale) in enumerate(((dq, q, arq), (dk, keys, ark))):
            v = v.astype(FULL)
            dot = g * v
            gain = dot if gain is None else gain + dot
            g = g - v * (head_sum(dot) * inverse)
            g = g * tab[0, tok, :] - pltpu.roll(g, 112, 1) * tab[2, tok, :] - pltpu.roll(g, 16, 1) * tab[1, tok, :]
            hid[tok, pl.ds(pl.multiple_of(part * width + s * 128, 128), 128)] = (g * scale[w]).astype(LOW)
        dsc[0, pl.ds(s, 1), :] += jnp.sum(gain, axis=0, keepdims=True)
        return 0
    def project(half, t):
        def some(k, t):
            attend(half * in_half + 2 * k, 0)
            attend(half * in_half + 2 * k + 1, 0)
            now = k > 0
            @pl.when(now)
            def _(): step(t)
            return t + now.astype(jnp.int32)
        t = lax.fori_loop(0, in_half // 2, some, t)
        @pl.when(half == 0)
        def _():
            fill.wait()
            norm_rows(att, mods, 0, images, nrm)
        for part in range(3):
            i = first_qkv + half * 3 + part
            cut = hid[:, pl.ds(pl.multiple_of(part * width + half * CH, CH), CH)]
            produce(i, nrm[...], cut)
            acc[...] += nt(cut, weights(i))
            step(t + part)
        return t + 3
    t = lax.fori_loop(0, per, project, jnp.int32(done))

    def keep_one(q, value):
        down[q, :] = value.astype(LOW)
    norm_back(att, 0, lambda q, image: x1[q, :], keep_one)
    result = pltpu.make_async_copy(down, dtok, osem)
    result.start()
    dmx[f] = dmf[0 : 2 * images, :].astype(LOW).astype(FULL)
    def share(d, _):
        pltpu.make_async_remote_copy(src_ref=dmx.at[f], dst_ref=dmx.at[f], send_sem=msem.at[0, 0], recv_sem=msem.at[1, 0],
            device_id=((f + d) % shards, r), device_id_type=MESH).start()
        return 0
    lax.fori_loop(1, shards, share, 0)
    def swap(k, *to):
        return remote(dsc.at[k], dsr.at[k], msem.at[0, 2 + k], msem.at[1, 2 + k], *to)
    swap(0, z, 1 - x, y, c).start()
    step(t)
    wait_bytes(dmx.at[pl.ds(0, shards - 1)], msem.at[1, 0])
    acc[0 : 8 * shards, :] = jnp.zeros((8 * shards, width), FULL)
    def spread(k, _):
        acc[pl.ds(pl.multiple_of(k * 8, 8), 2 * images), :] = dmx[k]
        return 0
    lax.fori_loop(0, shards, spread, 0)
    flat = acc[0 : 8 * shards, :].astype(LOW)
    group = call[...].astype(FULL)[:, 0:8].reshape(shards * 8, 128)
    spot = lax.broadcasted_iota(jnp.int32, group.shape, 0) % 8
    for side in range(2):
        own_rows = jnp.where((spot >= side * images) & (spot < (side + 1) * images), group, 0.0).astype(LOW)
        pm[:, side * width : (side + 1) * width] = tn(own_rows, flat)[0 : pm.shape[0]].astype(LOW)
    core_swap = remote(pm, pr, msem.at[0, 5], msem.at[1, 5], z, x, y, 1 - c)
    core_swap.start()
    back_one = nt(flat, wm[:, 0:width])
    back_two = nt(flat, wm[:, width:])
    back_all = back_one + pltpu.roll(back_two, 8 * shards - images, 0)
    dpart[...] = back_all.reshape(shards, 8, 128)
    def back(d, _):
        to = (f + d) % shards
        pltpu.make_async_remote_copy(src_ref=dpart.at[to], dst_ref=dcr.at[f], send_sem=msem.at[0, 6], recv_sem=msem.at[1, 6],
            device_id=(to, r), device_id_type=MESH).start()
        return 0
    lax.fori_loop(1, shards, back, 0)
    dcr[f] = dpart[f]
    def settle(k):
        swap(k, z, x, y, c).wait()
        dsc[k + 1] = dsc[k] + dsr[k]
    settle(0)
    swap(1, z, x, 1 - y, c).start()
    step(t + 1)
    core_swap.wait()
    half_c = pl.ds(pl.multiple_of(c * width, 128), width)
    psum[...] = plus(pm[:, half_c], pr[:, half_c])
    y_swap = remote(psum, py, msem.at[0, 7], msem.at[1, 7], z, x, 1 - y, c)
    y_swap.start()
    settle(1)
    swap(2, z, x, y, 1 - c).start()
    step(t + 2)
    settle(2)
    dsr[3] = dsc[3]
    def round_z(d):
        return remote(dsr.at[3], dsr.at[4 + z], msem.at[0, 8], msem.at[1, 8], (z + d) % Z, x, y, c)
    for d in range(1, Z):
        round_z(d).start()
    dsr[4 + z] = dsc[3]
    step(t + 3)
    y_swap.wait()
    gmod[:, half_c] = plus(psum[...], py[...])
    last = remote(gmod.at[:, half_c], gmod.at[:, half_c], msem.at[0, 9], msem.at[1, 9], z, x, y, 1 - c)
    last.start()
    wait_bytes(dsr.at[pl.ds(4, Z - 1)], msem.at[1, 8])
    total = dsr[4]
    for k in range(1, Z):
        total = total + dsr[4 + k]
    sums = head_sum(total)
    inverse = jnp.zeros(sums.shape, FULL)
    line = lax.broadcasted_iota(jnp.int32, sums.shape, 0) * 2 + lax.broadcasted_iota(jnp.int32, sums.shape, 1) // 64
    for h in range(width // 64):
        inverse = jnp.where(line == h, 0.5 / jnp.full(sums.shape, scale[h], FULL), inverse)
    dscale[...] = sums * inverse
    step(t + 4)
    wait_bytes(dcr.at[pl.ds(0, shards - 1)], msem.at[1, 6])
    wide_c[...] = jnp.zeros_like(wide_c)
    def assemble(k, _):
        one = jnp.concatenate([dcr[k], jnp.zeros((8, wide_c.shape[1] - 128), FULL)], axis=1)
        lane = lax.broadcasted_iota(jnp.int32, one.shape, 1)
        wide_c[...] += pltpu.roll(jnp.where(lane < own_map, one, 0.0), k * own_map, 1)
        return 0
    lax.fori_loop(0, shards, assemble, 0)
    dcond[...] = wide_c[0:images, :]
    lax.fori_loop(t + 5, n + B_LAG[7], lambda s, _: (step(s), 0)[1], 0)
    last.wait()
    wait_bytes(dmx.at[pl.ds(0, shards - 1)], msem.at[0, 0])
    wait_bytes(dcr.at[pl.ds(0, shards - 1)], msem.at[0, 6])
    wait_bytes(dsr.at[pl.ds(4, Z - 1)], msem.at[0, 8])
    result.wait()
    finish(n - 1)
    lax.fori_loop(n - Q_SLOTS, n, lambda i, _: (free(i), 0)[1], 0)


def backward(sigma, scale, cot, tokens, mods, wm, tab, roots, call, saved, own_map, wide_c):
    images = sigma.shape[0]
    rows, width = tokens.shape
    n, Z, _, R, w = saved[0].shape
    hidden = saved[9].shape[1]
    length = rows // images
    shards = 2 * Z
    half_z, some = Z // 2, (n + 1) // 2
    rows_m = -(-own_map // 16) * 16
    vm, dma = pltpu.VMEM, pltpu.SemaphoreType.DMA
    wide = (rows, width)
    slab = (A_SLOTS, length, 128)
    scratch = [
        vm(wide, LOW), vm((rows, hidden), LOW), vm((rows, hidden), LOW), vm((rows, hidden), LOW), vm(wide, FULL), vm(wide, LOW),
        vm(wide, LOW), vm(wide, FULL), vm(wide, LOW), vm((B_SLOTS, Z, 2, R, w), LOW), vm(slab, LOW), vm(slab, LOW), vm(slab, LOW),
        vm(slab, FULL), vm(slab, FULL), vm((A_SLOTS, 2, length, length), LOW), vm((16, width), FULL), vm((shards, 2 * images, width), FULL),
        vm((rows_m, 2 * width), LOW), vm((rows_m, 2 * width), LOW), vm((rows_m, width), LOW), vm((rows_m, width), LOW),
        vm((shards, 8, 128), FULL), vm((shards, 8, 128), FULL), vm((4, width // 128, 128), FULL), vm((4 + Z, width // 128, 128), FULL),
        vm((8, wide_c), FULL), vm((images, 8, width), FULL),
        vm((n, R, w), LOW), vm((Q_SLOTS, half_z, 2, 2, R, w), LOW), vm((RING, half_z, 2, 2, R, w // 2), LOW), vm((n, half_z, 2, R, w // 4), LOW),
        vm((n, half_z, R, w // 4), LOW), vm((n, half_z, R, w // 2), LOW), vm((some, half_z, R, w // 4), LOW), vm((some, half_z, R, w // 2), LOW),
        vm((some, max(half_z - 1, 1), R, w // 4), LOW), vm((some, max(half_z - 1, 1), R, w // 2), LOW),
        vm((some, R, w // 2), LOW),
        dma((9, n)), dma((9, n)), pltpu.SemaphoreType.REGULAR, dma((B_SLOTS,)), dma((7,)), dma((6, A_SLOTS)), dma((2, 10)), dma, dma((n,)),
    ]
    hbm, vmem = pl.BlockSpec(memory_space=pltpu.HBM), pl.BlockSpec(memory_space=pltpu.VMEM)
    smem = pl.BlockSpec(memory_space=pltpu.SMEM)
    array = jax.ShapeDtypeStruct
    return pl.pallas_call(
        functools.partial(backward_kernel, images, own_map),
        out_shape=(
            array((R, 3 * width), LOW), array((R, width), LOW), array((R, 2 * hidden), LOW), array((hidden // shards, width), LOW),
            array(wide, LOW), array((rows_m, 2 * width), LOW), array((images, wide_c), FULL), array((width // 128, 128), FULL),
        ),
        in_specs=[smem, smem, hbm, hbm] + [vmem] * 5 + [hbm] * 12,
        out_specs=tuple([hbm] * 5 + [vmem] * 3),
        scratch_shapes=scratch,
        compiler_params=pltpu.CompilerParams(collective_id=1, has_side_effects=True, vmem_limit_bytes=VMEM_LIMIT),
    )(sigma, scale, cot, tokens, mods, wm, tab, roots, call, *saved)


def local(tokens, cond, sigma_idx, pos_rows, pos_cols, attn_scale, w_mod1, w_qkv, w_out, w_mod2, w_up, w_down, cotangent):
    shards = lax.axis_size("fsdp")
    R, width = w_out.shape
    own, wide_c = w_mod1.shape[0], cond.shape[1]
    blocks = w_down.shape[0] // R
    regroup = R != 128
    if regroup:
        w_up = w_up.reshape(R, 2, shards, blocks, R).transpose(0, 1, 3, 2, 4).reshape(R, -1)
    pos = jnp.stack([pos_rows, pos_cols])
    (chunks, out, x1, qr, kr, vb, rq, rk, probs, att, h, ga, gb, mods, call, wm, tab, roots) = forward(
        tokens, cond, pos, w_mod1, w_mod2, attn_scale, w_qkv, w_out, w_up, w_down, shards
    )
    saved = (chunks, x1, qr, kr, vb, rq, rk, probs, att, h, ga, gb)
    g_qkv, g_out, g_up, g_down, d_tokens, g_mod, d_cond, d_scale = backward(
        sigma_idx, attn_scale, cotangent, tokens, mods, wm, tab, roots, call, saved, own, wide_c
    )
    d_scale = d_scale.reshape(attn_scale.shape[0], -1)[:, 0]
    if regroup:
        g_up = g_up.reshape(R, 2, blocks, shards, R).transpose(0, 1, 3, 2, 4).reshape(R, -1)
    g_mod = g_mod[:own].astype(FULL)
    return (
        out, d_tokens, d_cond, d_scale, g_mod[:, :width], g_qkv.astype(FULL), g_out.astype(FULL), g_mod[:, width:],
        g_up.astype(FULL), g_down.astype(FULL),
    )


def solution(mesh):
    placed = (
        P(("fsdp", "rep"), None),
        P(("fsdp", "rep"), None),
        P(("fsdp", "rep")),
        P(("fsdp", "rep")),
        P(("fsdp", "rep")),
        P(),
        P("fsdp", None),
        P("fsdp", None),
        P("fsdp", None),
        P("fsdp", None),
        P("fsdp", None),
        P("fsdp", None),
        P(("fsdp", "rep"), None),
    )
    return jax.shard_map(
        local,
        mesh=mesh,
        in_specs=placed,
        out_specs=(
            P(("fsdp", "rep"), None),
            P(("fsdp", "rep"), None),
            P(("fsdp", "rep"), None),
            P(),
            P("fsdp", None),
            P("fsdp", None),
            P("fsdp", None),
            P("fsdp", None),
            P("fsdp", None),
            P("fsdp", None),
        ),
        check_vma=False,
    )
```

```python
import functools
import math

import jax
import jax.numpy as jnp
from jax import lax
from jax.experimental import pallas as pl
from jax.experimental.pallas import tpu as pltpu
from jax.sharding import PartitionSpec as P

GRID = 16
NB = 64

MESH = pl.DeviceIdType.MESH
CH = 512

def place():
    f, r = lax.axis_index("fsdp"), lax.axis_index("rep")
    return f // 2, f % 2, r // 2, r % 2

def is_c(i, n):
    return (i % 4 == 2) | (i == n - 1)

def remote(src, dst, send, recv, z, x, y, c):
    return pltpu.make_async_remote_copy(src_ref=src, dst_ref=dst, send_sem=send, recv_sem=recv,
        device_id=(z * 2 + x, y * 2 + c), device_id_type=MESH)

def wait_bytes(ref, sem):
    pltpu.make_async_copy(ref, ref, sem).wait()

def gather_ops(src, buf, sends, recvs, own):
    n, Z = buf.shape[0], buf.shape[1]
    z, x, y, c = place()
    zs, xs, ys, yt, cs, ct, cu, cv = (sends.at[k] for k in range(8))
    zr, xr, yr, yq, cr, cq, cp, co = (recvs.at[k] for k in range(8))
    def cols_of(width, k):
        return pl.ds(pl.multiple_of(k * width, 128), width)
    def both(i, fn):
        inside = (i >= 0) & (i < n)
        @pl.when(inside & jnp.logical_not(is_c(i, n)))
        def _(): fn(128, 2 * y + c, False)
        @pl.when(inside & is_c(i, n))
        def _(): fn(256, c, True)
    def inside_of(i, low, high, fn):
        @pl.when((i >= low) & (i < high))
        def _(): fn(i - low)
    def stage_z(i):
        low = 0
        for count, blocks_of in src:
            def start(j, i=i, blocks_of=blocks_of):
                for ref, first, width in blocks_of(j, 0, CH):
                    pltpu.make_async_copy(ref, buf.at[i, z, x, :, pl.ds(first, width)], own.at[i]).start()
                def go(width, k, cc):
                    for ref, first, w in blocks_of(j, k * width, width):
                        cols = pl.ds(pl.multiple_of(k * width + first, 128), w)
                        for d in range(1, Z):
                            remote(ref, buf.at[i, z, x, :, cols], zs.at[i], zr.at[i], (z + d) % Z, x, y, c).start()
                        remote(ref, buf.at[i, z, x, :, cols], xs.at[i], xr.at[i], z, 1 - x, y, c).start()
                both(i, go)
            inside_of(i, low, low + count, start)
            low += count
    def others(i, cols, send, recv, *to):
        for d in range(1, Z):
            zz = (z + d) % Z
            remote(buf.at[i, zz, x, :, cols], buf.at[i, zz, x, :, cols], send, recv, *to).start()
    def partner(i, cols, send, recv, *to):
        part = buf.at[i, :, 1 - x, :, cols]
        remote(part, part, send, recv, *to).start()
    def stage_x(i):
        def go(width, k, cc):
            cols = cols_of(width, k)
            wait_bytes(buf.at[i, 0:Z - 1, 0, :, cols], zr.at[i])
            others(i, cols, xs.at[i], xr.at[i], z, 1 - x, y, c)
            if not cc:
                others(i, cols, ys.at[i], yr.at[i], z, x, 1 - y, c)
            others(i, cols, cs.at[i], cr.at[i], z, x, y, 1 - c)
        both(i, go)
    def stage_y(i):
        def go(width, k, cc):
            cols = cols_of(width, k)
            wait_bytes(buf.at[i, :, 0, :, cols], xr.at[i])
            if not cc:
                partner(i, cols, yt.at[i], yq.at[i], z, x, 1 - y, c)
            partner(i, cols, ct.at[i], cq.at[i], z, x, y, 1 - c)
        both(i, go)
    def stage_c(i):
        def go(width, k, cc):
            if cc: return
            cols = cols_of(width, k)
            wait_bytes(buf.at[i, 0:Z - 1, 0, :, cols], yr.at[i])
            wait_bytes(buf.at[i, :, 0, :, cols], yq.at[i])
            mine = cols_of(128, 2 * (1 - y) + c)
            others(i, mine, cu.at[i], cp.at[i], z, x, y, 1 - c)
            partner(i, mine, cv.at[i], co.at[i], z, x, y, 1 - c)
        both(i, go)
    def core_waits(i, one, two, three, four):
        def go(width, k, cc):
            cols = pl.ds(0, width)
            wait_bytes(buf.at[i, 0:Z - 1, 0, :, cols], one.at[i])
            wait_bytes(buf.at[i, :, 0, :, cols], two.at[i])
            if not cc:
                wait_bytes(buf.at[i, 0:Z - 1, 0, :, cols], three.at[i])
                wait_bytes(buf.at[i, :, 0, :, cols], four.at[i])
        both(i, go)
    def ready(i):
        @pl.when((i >= 0) & (i < n))
        def _(): wait_bytes(buf.at[i, z, x], own.at[i])
        core_waits(i, cr, cq, cp, co)
    def finish(i):
        def go(width, k, cc):
            cols = cols_of(width, k)
            wait_bytes(buf.at[i, 0:Z - 1, 0, :, cols], zs.at[i])
            wait_bytes(buf.at[i, :, 0, :, cols], xs.at[i])
            if not cc:
                wait_bytes(buf.at[i, 0:Z - 1, 0, :, cols], ys.at[i])
                wait_bytes(buf.at[i, :, 0, :, cols], yt.at[i])
        both(i, go)
        core_waits(i, cs, ct, cu, cv)
    return stage_z, stage_x, stage_y, stage_c, ready, finish


EPS = 1e-06
LOW = jnp.bfloat16
FULL = jnp.float32
VMEM_LIMIT = 60 * 2**20
F_LAG = (0, 2, 4, 6, 7)
F_LATE = 3
W_SLOTS = 3


def nn(a, b):
    return jnp.dot(a, b, preferred_element_type=FULL)


def nt(a, b):
    return lax.dot_general(a, b, (((1,), (1,)), ((), ())), preferred_element_type=FULL)


def tn(a, b):
    return lax.dot_general(a, b, (((0,), (0,)), ((), ())), preferred_element_type=FULL)


def at(k, size):
    return pl.ds(pl.multiple_of(k * size, size), size)


def head_sum(v):
    one = lax.broadcasted_iota(jnp.int32, (128, 128), 0) // 64
    two = lax.broadcasted_iota(jnp.int32, (128, 128), 1) // 64
    same = (one == two).astype(LOW)
    high = v.astype(LOW)
    rest = v - high.astype(FULL)
    return nn(high, same) + nn(rest.astype(LOW), same)


def head_mask(rows, second):
    lane = lax.broadcasted_iota(jnp.int32, (rows, 128), 1)
    return (lane >= 64) if second else (lane < 64)


def turn(v, cosine, sine_up, sine_down):
    return v * cosine + pltpu.roll(v, 16, 1) * sine_up + pltpu.roll(v, 112, 1) * sine_down


def norm_rows(src_ref, mods_ref, side, images, dst_ref, x_ref=None):
    rows, width = src_ref.shape
    length = rows // images
    block = 64
    def body(i, _):
        r = at(i, block)
        v = src_ref[r, :].astype(FULL)
        factor = lax.rsqrt(jnp.mean(v * v, axis=1, keepdims=True) + EPS)
        m = mods_ref[pl.ds(i // (length // block), 1), side * width : (side + 1) * width]
        dst_ref[r, :] = (v * factor * (1.0 + m)).astype(LOW)
        return 0
    lax.fori_loop(0, rows // block, body, 0)


def three(v):
    one = v.astype(LOW)
    rest = v - one.astype(FULL)
    two = rest.astype(LOW)
    return one, two, (rest - two.astype(FULL)).astype(LOW)


def rope_tables(pos, tab, head):
    grid = lax.broadcasted_iota(jnp.int32, (2 * GRID, 128), 0)
    lane = lax.broadcasted_iota(jnp.int32, (2 * GRID, 128), 1) % head
    pairs = head // 4
    quarter = pairs // 2
    j = lane % pairs
    place = ((grid % GRID).astype(FULL) + 0.5) * (2.0 / GRID) - 1.0
    freq = math.pi * jnp.exp(math.log(10.0) * (j % quarter).astype(FULL) / max(quarter - 1, 1))
    angle = place * freq
    mine = (lane < 2 * pairs) & ((grid // GRID) == (j // quarter))
    cos, sin = jnp.cos(angle), jnp.sin(angle)
    zero = jnp.zeros_like(cos)
    kinds = (
        jnp.where(mine, cos, zero),
        jnp.where(mine & (lane >= pairs), sin, zero),
        jnp.where(mine & (lane < pairs), -sin, zero),
    )
    rows = pos.shape[1]
    spot = lax.broadcasted_iota(jnp.int32, (GRID, rows), 0)
    hot = jnp.concatenate([(spot == pos[0:1, :]).astype(FULL), (spot == pos[1:2, :]).astype(FULL)], axis=0).astype(LOW)
    for k, kind in enumerate(kinds):
        total = None
        for part in three(kind):
            one = tn(hot, part)
            total = one if total is None else total + one
        if k == 0:
            plain = lax.broadcasted_iota(jnp.int32, (rows, 128), 1) % head >= 2 * pairs
            total = total + plain.astype(FULL)
        tab[k] = total


def forward_kernel(
    images, heads, tokens, cond, pos, w_mod1, w_mod2, scale, w_qkv, w_out, w_up, w_down,
    buf, out, x1_o, qr_o, kr_o, vb_o, rq_o, rk_o, p_o, o_o, h_o, ga_o, gb_o, mods_o, call_o, wm_o, tab_o, roots_o,
    n1, qkv, rqk, probs, att, x1, n2, hid, ga, gb, up, acc, slots, mods, call, mpart, mrecv, cparts, wide_c, wm, tab, roots,
    sends, recvs, own, wsem, osem, csem, msem,
):
    n, Z, R = buf.shape[0], buf.shape[1], buf.shape[3]
    shards = 2 * Z
    rows, width = tokens.shape
    hidden = hid.shape[1]
    length = rows // images
    half_heads = width // CH
    z, x, y, c = place()
    f = z * 2 + x
    r = y * 2 + c
    barrier = pltpu.get_barrier_semaphore()
    def greet(d, _):
        pl.semaphore_signal(barrier, inc=1, device_id=((f + d) % shards, r), device_id_type=MESH)
        return 0
    lax.fori_loop(1, shards, greet, 0)
    for where in ((f, (1 - y) * 2 + c), (f, y * 2 + 1 - c)):
        pl.semaphore_signal(barrier, inc=1, device_id=where, device_id_type=MESH)
    wide_c[...] = jnp.zeros_like(wide_c)
    for k in range(2):
        wide_c[k * images : (k + 1) * images, :] = cond[...].astype(FULL)
    map_rows = w_mod1.shape[0]
    def cut(k, _):
        full = wide_c.shape[1]
        moved = pltpu.roll(wide_c[...], (full - k * map_rows) % full, 1)[:, 0:128]
        lane = lax.broadcasted_iota(jnp.int32, moved.shape, 1)
        cparts[k] = jnp.where(lane < map_rows, moved, 0.0).astype(LOW)
        return 0
    lax.fori_loop(0, shards, cut, 0)
    call[f] = cparts[f]
    pl.semaphore_wait(barrier, shards + 1)

    blocks = w_down.shape[0] // R
    def columns(ref, at_row, at_col):
        def of(j, first, size):
            return [(ref.at[at_row(j), pl.ds(pl.multiple_of(at_col(j) + first, 128), size)], 0, size)]
        return of
    every = lambda j: slice(None)
    def of_up(j, first, size):
        if R != 128:
            return columns(w_up, every, lambda j: (j % 2) * hidden + (j // 2) * CH)(j, first, size)
        found = []
        for b in range(size // 128):
            unit = (j // 2) * (CH // 128) + first // 128 + b
            spot = (j % 2) * hidden + ((unit % shards) * blocks + unit // shards) * 128
            found.append((w_up.at[:, pl.ds(pl.multiple_of(spot, 128), 128)], b * 128, 128))
        return found
    src = [
        (3 * half_heads, columns(w_qkv, every, lambda j: (j % 3) * width + (j // 3) * CH)),
        (half_heads, columns(w_out, every, lambda j: j * CH)),
        (2 * hidden // CH, of_up),
        (blocks * half_heads, columns(w_down, lambda j: at(j // half_heads, R), lambda j: (j % half_heads) * CH)),
    ]
    stage_z, stage_x, stage_y, stage_c, ready, finish = gather_ops(src, buf, sends, recvs, own)

    def give(d, _):
        to = (f + d) % shards
        pltpu.make_async_remote_copy(src_ref=cparts.at[to], dst_ref=call.at[f], send_sem=csem.at[0], recv_sem=csem.at[1],
            device_id=(to, r), device_id_type=MESH).start()
        return 0

    def load(j):
        return pltpu.make_async_copy(buf.at[j], slots.at[j % W_SLOTS], wsem.at[j % W_SLOTS])

    def step(t):
        @pl.when(t >= 2)
        def _(): stage_z(t)
        stage_x(t - F_LAG[1])
        stage_y(t - F_LAG[2])
        stage_c(t - F_LAG[3])
        ready(t - F_LAG[4])
        finish(t - F_LAG[4] - F_LATE)
        @pl.when((t >= F_LAG[4]) & (t < n + F_LAG[4]))
        def _(): load(t - F_LAG[4]).start()

    def begin(j):
        step(j + F_LAG[4] + 1)
        load(j).wait()
        return j % W_SLOTS

    def weights(slot):
        return slots[slot].reshape(width, CH)

    stage_z(0)
    lax.fori_loop(1, shards, give, 0)
    stage_z(1)
    for side, ref in enumerate((w_mod1, w_mod2)):
        acc[0:128, :] = jnp.zeros((128, width), FULL)
        acc[0:map_rows, :] = ref[...].astype(FULL)
        wm[:, side * width : (side + 1) * width] = acc[0:128, :].astype(LOW)
    step(2)
    wait_bytes(call.at[pl.ds(0, shards - 1)], csem.at[1])
    flat = call[...].reshape(shards * 16, 128)
    mpart[...] = nn(flat, wm[...]).reshape(shards, 16, 2 * width)[:, 0:images]
    def back(d, _):
        to = (f + d) % shards
        pltpu.make_async_remote_copy(src_ref=mpart.at[to], dst_ref=mrecv.at[f], send_sem=msem.at[0], recv_sem=msem.at[1],
            device_id=(to, r), device_id_type=MESH).start()
        return 0
    lax.fori_loop(1, shards, back, 0)
    mrecv[f] = mpart[f]
    step(3)
    which = lax.broadcasted_iota(jnp.int32, roots.shape, 1) // (width // heads)
    row = jnp.zeros(roots.shape, FULL)
    for h in range(heads):
        row = jnp.where(which == h, scale[h], row)
    roots[...] = jnp.sqrt(row)
    rope_tables(pos, tab, width // heads)
    step(4)
    wait_bytes(mrecv.at[pl.ds(0, shards - 1)], msem.at[1])
    mods[...] = jnp.zeros_like(mods)
    total = mrecv[0]
    for k in range(1, shards):
        total = total + mrecv[k]
    mods[0:images, :] = total
    step(5)
    norm_rows(tokens, mods, 0, images, n1)
    lax.fori_loop(6, F_LAG[4] + 1, lambda t, _: (step(t), 0)[1], 0)

    def project(half, _):
        lanes_of = lambda s: pl.ds(pl.multiple_of(half * CH + s * 128, 128), 128)
        for part in range(2):
            slot = begin(half * 3 + part)
            v = nn(n1[...], weights(slot))
            for s in range(CH // 128):
                one = v[:, s * 128 : (s + 1) * 128]
                scale = lax.rsqrt(head_sum(one * one) + EPS) * roots[0:1, lanes_of(s)]
                rqk[part, :, lanes_of(s)] = scale
                qkv[part, :, lanes_of(s)] = turn(one * scale, tab[0], tab[1], tab[2]).astype(LOW)
        slot = begin(half * 3 + 2)
        qkv[2, :, at(half, CH)] = nn(n1[...], weights(slot)).astype(LOW)
        def pair(k, _):
            image, s = k // (CH // 128), k % (CH // 128)
            tok = at(image, length)
            lane = pl.ds(pl.multiple_of(half * CH + s * 128, 128), 128)
            q, keys, val = qkv[0, tok, lane], qkv[1, tok, lane], qkv[2, tok, lane]
            total = None
            for second in range(2):
                mask = head_mask(length, second)
                scores = jnp.exp(nt(jnp.where(mask, q, jnp.zeros_like(q)), keys))
                p = (scores * (1.0 / jnp.sum(scores, axis=1, keepdims=True))).astype(LOW)
                probs[half * (CH // 128) + s, image, second] = p
                o = nn(p, jnp.where(mask, val, jnp.zeros_like(val)))
                total = o if total is None else total + o
            att[tok, lane] = total.astype(LOW)
            return 0
        lax.fori_loop(0, images * (CH // 128), pair, 0)
        return 0
    lax.fori_loop(0, half_heads, project, 0)
    outs = [
        (qkv.at[0], qr_o), (qkv.at[1], kr_o), (qkv.at[2], vb_o), (rqk.at[0], rq_o), (rqk.at[1], rk_o), (probs, p_o), (att, o_o),
        (mods, mods_o), (call, call_o), (wm, wm_o), (tab, tab_o), (roots, roots_o),
    ]
    later = [(x1, x1_o), (hid, h_o), (ga, ga_o), (gb, gb_o), (n2, out)]
    copies = [pltpu.make_async_copy(a, b, osem.at[k]) for k, (a, b) in enumerate(outs + later)]
    for k in range(len(outs)):
        copies[k].start()

    at_out = 3 * half_heads
    def project_out(j, _):
        slot = begin(at_out + j)
        lane = at(j, CH)
        x1[:, lane] = tokens[:, lane].astype(FULL) + nn(att[...], weights(slot))
        return 0
    lax.fori_loop(0, half_heads, project_out, 0)
    copies[len(outs)].start()
    norm_rows(x1, mods, 1, images, n2)

    at_up = at_out + half_heads
    def widen(j, _):
        up[...] = nn(n2[...], weights(begin(at_up + 2 * j)))
        gate = nn(n2[...], weights(begin(at_up + 2 * j + 1)))
        lane_of = lambda s: pl.ds(pl.multiple_of(j * CH + s * 128, 128), 128)
        for s in range(CH // 128):
            g = gate[:, s * 128 : (s + 1) * 128]
            u = up[:, s * 128 : (s + 1) * 128]
            phi = 0.5 + 0.5 * lax.erf(g * math.sqrt(0.5))
            gelu = g * phi
            slope = phi + g * (jnp.exp(-0.5 * g * g) * (1.0 / math.sqrt(2.0 * math.pi)))
            hid[:, lane_of(s)] = (u * gelu).astype(LOW)
            ga[:, lane_of(s)] = gelu.astype(LOW)
            gb[:, lane_of(s)] = (u * slope).astype(LOW)
        return 0
    lax.fori_loop(0, hidden // CH, widen, 0)
    for k in range(1, 4):
        copies[len(outs) + k].start()

    at_down = at_up + 2 * hidden // CH
    def narrow(k, _):
        for j in range(width // CH):
            slot = begin(at_down + k * (width // CH) + j)
            part = nn(hid[:, at(k, width)], weights(slot))
            cols = slice(j * CH, (j + 1) * CH)
            acc[:, cols] = part + jnp.where(k == 0, x1[:, cols], acc[:, cols])
        return 0
    lax.fori_loop(0, hidden // width, narrow, 0)
    n2[...] = acc[...].astype(LOW)
    copies[-1].start()
    for copy in copies:
        copy.wait()
    lax.fori_loop(n + 1 - F_LATE, n, lambda i, _: (finish(i), 0)[1], 0)
    wait_bytes(call.at[pl.ds(0, shards - 1)], csem.at[0])
    wait_bytes(mrecv.at[pl.ds(0, shards - 1)], msem.at[0])


def forward(tokens, cond, pos, w_mod1, w_mod2, scale, w_qkv, w_out, w_up, w_down, shards):
    rows, width = tokens.shape
    R, hidden = w_out.shape[0], w_up.shape[1] // 2
    images, wide_c = cond.shape
    Z, w = shards // 2, CH
    n = (w_qkv.shape[1] + w_out.shape[1] + w_up.shape[1]) // CH + (w_down.shape[0] // R) * (width // CH)
    length = rows // images
    pairs = width // 128
    array = jax.ShapeDtypeStruct
    wide = (rows, width)
    out_shape = (
        array((n, Z, 2, R, w), LOW), array(wide, LOW), array(wide, FULL), array(wide, LOW), array(wide, LOW), array(wide, LOW),
        array(wide, FULL), array(wide, FULL), array((pairs, images, 2, length, length), LOW), array(wide, LOW),
        array((rows, hidden), LOW), array((rows, hidden), LOW), array((rows, hidden), LOW), array((8, 2 * width), FULL),
        array((shards, 16, 128), LOW), array((128, 2 * width), LOW), array((3, rows, 128), FULL), array((8, width), FULL),
    )
    vm, dma = pltpu.VMEM, pltpu.SemaphoreType.DMA
    scratch = [
        vm(wide, LOW), vm((3, *wide), LOW), vm((2, *wide), FULL), vm((pairs, images, 2, length, length), LOW), vm(wide, LOW),
        vm(wide, FULL), vm(wide, LOW), vm((rows, hidden), LOW), vm((rows, hidden), LOW), vm((rows, hidden), LOW),
        vm((rows, w), FULL), vm(wide, FULL), vm((W_SLOTS, Z, 2, R, w), LOW), vm((8, 2 * width), FULL), vm((shards, 16, 128), LOW),
        vm((shards, images, 2 * width), FULL), vm((shards, images, 2 * width), FULL), vm((shards, 16, 128), LOW), vm((16, wide_c), FULL),
        vm((128, 2 * width), LOW), vm((3, rows, 128), FULL), vm((8, width), FULL),
        dma((8, n)), dma((8, n)), dma((n,)), dma((W_SLOTS,)), dma((17,)), dma((2,)), dma((2,)),
    ]
    hbm, vmem = pl.BlockSpec(memory_space=pltpu.HBM), pl.BlockSpec(memory_space=pltpu.VMEM)
    smem = pl.BlockSpec(memory_space=pltpu.SMEM)
    return pl.pallas_call(
        functools.partial(forward_kernel, images, scale.shape[0]),
        out_shape=out_shape,
        in_specs=[vmem] * 5 + [smem] + [hbm] * 4,
        out_specs=tuple([hbm] * len(out_shape)),
        scratch_shapes=scratch,
        compiler_params=pltpu.CompilerParams(collective_id=0, has_side_effects=True, vmem_limit_bytes=VMEM_LIMIT),
    )(tokens, cond, pos, w_mod1, w_mod2, scale, w_qkv, w_out, w_up, w_down)


Q_SLOTS = 9
RING = 7
A_SLOTS = 2
B_SLOTS = 2
B_LAG = (0, 1, 3, 5, 7, 9, 11, 12)


def plus(a, b):
    return (a.astype(FULL) + b.astype(FULL)).astype(LOW)


def scatter_ops(n, queue, rc, ry, rxa, rxc, rza, rzc, rya, ryc, rl, out, sends, recvs, credit, gsem, put):
    half_z = rc.shape[1]
    Z = 2 * half_z
    z, x, y, c = place()
    def cols(k, width):
        return pl.ds(pl.multiple_of(k * width, 128), width)
    def inside(i, fn):
        @pl.when((i >= 0) & (i < n))
        def _(): fn(i % 2)
    def by_kind(i, fn_a, fn_c):
        ok = (i >= 0) & (i < n)
        @pl.when(ok & (z % 2 != i % 2))
        def _(): fn_a()
        @pl.when(ok & (z % 2 == i % 2))
        def _(): fn_c()
    def each(fn):
        lax.fori_loop(0, half_z, lambda k, _: (fn(k), 0)[1], 0)
    def s0(i):
        def go(p):
            @pl.when(i >= RING)
            def _(): pl.semaphore_wait(credit, 1)
            remote(queue.at[i % Q_SLOTS, :, :, :, :, cols(1 - c, 256)], rc.at[i % RING], sends.at[0, i], recvs.at[0, i], z, x, y, 1 - c).start()
        inside(i, go)
    def free(i):
        @pl.when(i >= 0)
        def _(): wait_bytes(rc.at[0], sends.at[0, i])
    def s1(i):
        w = i % RING
        def go(p):
            wait_bytes(rc.at[w], recvs.at[0, i])
            def one(k):
                rc[w, k] = plus(rc[w, k], queue[i % Q_SLOTS, k, :, :, :, cols(c, 256)])
            each(one)
            remote(rc.at[w, :, 1 - p, :, :, cols(1 - y, 128)], ry.at[i], sends.at[1, i], recvs.at[1, i], z, x, 1 - y, c).start()
            remote(rc.at[w, :, p, 1 - x], rxc.at[i], sends.at[2, i], recvs.at[2, i], z, 1 - x, y, c).start()
        inside(i, go)
    mate = z + 1 - 2 * (z % 2)
    def next_door(i, rx, rz, row):
        remote(rx.at[i], rz.at[i // 2], sends.at[row, i], recvs.at[row, i], mate, x, y, c).start()
    def far(i, rx, rz, row):
        for d in range(1, half_z):
            to = (z // 2 + d) % half_z
            remote(rx.at[i, to], rz.at[i // 2, d - 1], sends.at[row, i], recvs.at[row, i], 2 * to + z % 2, x, y, c).start()
    def join(i, rx, rz):
        def one(k):
            rx[i, k] = plus(rx[i, k], rz[i // 2, k])
        each(one)
    def s2(i):
        w = i % RING
        def go(p):
            wait_bytes(ry.at[i], recvs.at[1, i])
            def one(k):
                ry[i, k] = plus(ry[i, k], rc[w, k, 1 - p, :, :, cols(y, 128)])
            each(one)
            remote(ry.at[i, :, 1 - x], rxa.at[i], sends.at[3, i], recvs.at[3, i], z, 1 - x, y, c).start()
            wait_bytes(rxc.at[i], recvs.at[2, i])
            def two(k):
                rxc[i, k] = plus(rxc[i, k], rc[w, k, p, x])
            each(two)
            @pl.when(z % 2 != p)
            def _(): next_door(i, rxc, rzc, 4)
            wait_bytes(ry.at[i], sends.at[1, i])
            wait_bytes(rxc.at[i], sends.at[2, i])
            @pl.when(i + RING < n)
            def _(): pl.semaphore_signal(credit, inc=1, device_id=(z * 2 + x, y * 2 + 1 - c), device_id_type=MESH)
        inside(i, go)
    def total(rx, rz, i):
        s = rx[i, z // 2].astype(FULL)
        for d in range(1, half_z):
            s = s + rz[i // 2, d - 1].astype(FULL)
        return s.astype(LOW)
    def arrived(i, rz, row):
        if half_z > 1:
            wait_bytes(rz.at[i // 2], recvs.at[row, i])
    def s3(i):
        def go(p):
            wait_bytes(rxa.at[i], recvs.at[3, i])
            def one(k):
                rxa[i, k] = plus(rxa[i, k], ry[i, k, x])
            each(one)
            @pl.when(z % 2 == p)
            def _(): next_door(i, rxa, rza, 5)
        inside(i, go)
        def cc():
            wait_bytes(rzc.at[i // 2], recvs.at[4, i])
            join(i, rxc, rzc)
            far(i, rxc, ryc, 8)
        by_kind(i, lambda: None, cc)
    def fwd(i):
        mine = out.at[i, :, cols(c, 256)]
        remote(mine, mine, sends.at[7, i], recvs.at[7, i], z, x, y, 1 - c).start()
    def s4(i):
        def a():
            wait_bytes(rza.at[i // 2], recvs.at[5, i])
            join(i, rxa, rza)
            far(i, rxa, rya, 8)
        def cc():
            arrived(i, ryc, 8)
            mine = out.at[i, :, cols(c, 256)]
            out[i, :, cols(c, 256)] = total(rxc, ryc, i)
            remote(mine, rl.at[i // 2], sends.at[6, i], recvs.at[6, i], z, x, 1 - y, c).start()
        by_kind(i, a, cc)
    def final(i):
        wait_bytes(rl.at[0], sends.at[7, i])
        wait_bytes(rl.at[0], recvs.at[7, i])
        put(i)
    def s5(i):
        def a():
            arrived(i, rya, 8)
            mine = out.at[i, :, cols(2 * c + y, 128)]
            out[i, :, cols(2 * c + y, 128)] = total(rxa, rya, i)
            remote(mine, mine, sends.at[6, i], recvs.at[6, i], z, x, 1 - y, c).start()
        def cc():
            wait_bytes(rl.at[0], recvs.at[6, i])
            wait_bytes(rl.at[0], sends.at[6, i])
            out[i, :, cols(c, 256)] = plus(out[i, :, cols(c, 256)], rl[i // 2])
            fwd(i)
        by_kind(i, a, cc)
    def s6(i):
        def a():
            wait_bytes(out.at[i, :, pl.ds(0, 128)], recvs.at[6, i])
            wait_bytes(out.at[i, :, pl.ds(0, 128)], sends.at[6, i])
            fwd(i)
        by_kind(i, a, lambda: final(i))
    def s7(i):
        by_kind(i, lambda: final(i), lambda: None)
    def finish(i):
        def go(p):
            wait_bytes(rxa.at[i], sends.at[3, i])
            wait_bytes(out.at[i], gsem.at[i])
        inside(i, go)
        def a():
            wait_bytes(rzc.at[0], sends.at[4, i])
            if half_z > 1:
                wait_bytes(rya.at[0], sends.at[8, i])
        def cc():
            wait_bytes(rza.at[0], sends.at[5, i])
            if half_z > 1:
                wait_bytes(ryc.at[0], sends.at[8, i])
        by_kind(i, a, cc)
    return s0, free, s1, s2, s3, s4, s5, s6, s7, finish


def backward_kernel(
    images, own_map, sigma, scale, cot, tokens, mods, wm, tab, roots, call,
    buf, x1_h, qr_h, kr_h, vb_h, rq_h, rk_h, p_h, o_h, h_h, ga_h, gb_h,
    g_qkv, g_out, g_up, g_down, dtok, gmod, dcond, dscale,
    down, hid, ga, gb, x1, nrm, att, acc, dob, slots, aq, ak, av, arq, ark, ap, dmf, dmx, pm, pr, psum, py, dpart, dcr, dsc, dsr, wide_c, weight,
    grads, queue, rc, ry, rxa, rxc, rza, rzc, rya, ryc, rl, sends, recvs, credit, wsem, lsem, asem, msem, osem, gsem,
):
    n, Z, R = buf.shape[0], buf.shape[1], buf.shape[3]
    shards = 2 * Z
    rows, width = tokens.shape
    hidden = hid.shape[1]
    length = rows // images
    per = width // CH
    n_down, n_up, n_out = hidden // width * per, 2 * hidden // CH, per
    z, x, y, c = place()
    f = z * 2 + x
    r = y * 2 + c
    barrier = pltpu.get_barrier_semaphore()
    def greet(d, _):
        pl.semaphore_signal(barrier, inc=1, device_id=((f + d) % shards, r), device_id_type=MESH)
        return 0
    lax.fori_loop(1, shards, greet, 0)
    for where in ((f, (1 - y) * 2 + c), (f, y * 2 + 1 - c)):
        pl.semaphore_signal(barrier, inc=1, device_id=where, device_id_type=MESH)
    given = pltpu.make_async_copy(cot, dob, lsem.at[6])
    given.start()
    loads = [pltpu.make_async_copy(a, b, lsem.at[k]) for k, (a, b) in enumerate(
        [(h_h, hid), (ga_h, ga), (gb_h, gb), (x1_h, x1), (o_h, att)])]
    for one in loads:
        one.start()
    def chunk_of(s):
        first = jnp.where(s < n_down, n - n_down + s, 3 * per + n_out + s - n_down)
        last = jnp.where(s < n_down + n_up + n_out, 3 * per + s - n_down - n_up, s - n_down - n_up - n_out)
        return jnp.where(s < n_down + n_up, first, last)
    def load(s):
        return pltpu.make_async_copy(buf.at[chunk_of(s)], slots.at[s % B_SLOTS], wsem.at[s % B_SLOTS])
    load(0).start()
    def weights(s):
        load(s).wait()
        @pl.when(s + 1 < n)
        def _(): load(s + 1).start()
        return slots[s % B_SLOTS].reshape(width, CH)

    blocks_d = hidden // width
    def put(i):
        def within(low, high, fn):
            @pl.when((i >= low) & (i < high))
            def _(): fn(i - low)
        def copy(src, dst):
            pltpu.make_async_copy(src, dst, gsem.at[i]).start()
        within(0, n_down, lambda j: copy(grads.at[i], g_down.at[at(j // per, R), at(j % per, CH)]))
        def to_up(j):
            side, first = j % 2, j // 2
            if R != 128:
                copy(grads.at[i], g_up.at[:, pl.ds(pl.multiple_of(side * hidden + first * CH, 128), CH)])
                return
            for b in range(CH // 128):
                unit = first * (CH // 128) + b
                spot = side * hidden + ((unit % shards) * blocks_d + unit // shards) * 128
                copy(grads.at[i, :, pl.ds(b * 128, 128)], g_up.at[:, pl.ds(pl.multiple_of(spot, 128), 128)])
        within(n_down, n_down + n_up, to_up)
        within(n_down + n_up, n_down + n_up + n_out, lambda j: copy(grads.at[i], g_out.at[:, at(j, CH)]))
        within(n_down + n_up + n_out, n, lambda j: copy(grads.at[i], g_qkv.at[:, pl.ds(pl.multiple_of((j % 3) * width + (j // 3) * CH, CH), CH)]))
    s0, free, s1, s2, s3, s4, s5, s6, s7, finish = scatter_ops(n, queue, rc, ry, rxa, rxc, rza, rzc, rya, ryc, rl, grads, sends, recvs, credit, gsem, put)
    def step(t):
        s0(t - B_LAG[0])
        s1(t - B_LAG[1])
        s2(t - B_LAG[2])
        s3(t - B_LAG[3])
        s4(t - B_LAG[4])
        s5(t - B_LAG[5])
        s6(t - B_LAG[6])
        s7(t - B_LAG[7])
        finish(t - B_LAG[7] - 1)
    def produce(i, left, right):
        free(i - Q_SLOTS)
        queue[i % Q_SLOTS] = tn(left, right).astype(LOW).reshape(Z // 2, 2, 2, R, CH)

    block = 64
    def blocks(fn):
        lax.fori_loop(0, rows // block, lambda i, _: (fn(at(i, block), i // (length // block)), 0)[1], 0)
    def weigh(k, image):
        down[k, :] = (dob[k, :].astype(FULL) * weight[image, 0:1, :]).astype(LOW)
    for image in range(images):
        level = jnp.full(weight.shape[1:], sigma[image].astype(FULL), FULL) / (NB - 1)
        noise = jnp.exp(-2.0 + 3.2 * level)
        weight[image] = 1.0 / (1.0 + 4.0 * noise * noise) + 0.25
    given.wait()
    blocks(weigh)
    dmf[...] = jnp.zeros_like(dmf)
    dsc[...] = jnp.zeros_like(dsc)
    pl.semaphore_wait(barrier, shards + 1)
    loads[0].wait()

    def second_product(i):
        produce(i, hid[:, at(i // per, width)], down[:, at(i % per, CH)])
    for i in range(2):
        second_product(i)
        step(i)
    loads[1].wait()
    loads[2].wait()
    def narrow(k, _):
        second_product(k + 2)
        step(k + 2)
        for j in range(per):
            part = nt(down[:, j * CH : (j + 1) * CH], weights(k * per + j))
            acc[...] = part if j == 0 else acc[...] + part
        def gate(q, image):
            ga[q, at(k, width)] = (acc[q, :] * ga[q, at(k, width)].astype(FULL)).astype(LOW)
            gb[q, at(k, width)] = (acc[q, :] * gb[q, at(k, width)].astype(FULL)).astype(LOW)
        blocks(gate)
        return 0
    lax.fori_loop(0, blocks_d, narrow, 0)
    for i in range(2 + blocks_d, n_down):
        second_product(i)
    done = 2 + blocks_d

    loads[3].wait()
    norm_rows(x1, mods, 1, images, nrm)
    acc[...] = jnp.zeros_like(acc)
    def widen(j, _):
        step(done + j)
        for side, ref in ((0, ga), (1, gb)):
            s = n_down + 2 * j + side
            produce(s, nrm[...], ref[:, at(j, CH)])
            acc[...] += nt(ref[:, at(j, CH)], weights(s))
        return 0
    lax.fori_loop(0, n_up // 2, widen, 0)
    done += n_up // 2

    def norm_back(src_ref, side, base, dst):
        def one(q, image):
            v = src_ref[q, :].astype(FULL)
            dn = acc[q, :]
            factor = lax.rsqrt(jnp.mean(v * v, axis=1, keepdims=True) + EPS)
            m = mods[pl.ds(image, 1), side * width : (side + 1) * width]
            g = dn * (1.0 + m)
            mean = jnp.mean(v * g, axis=1, keepdims=True)
            dst(q, base(q, image) + factor * g - v * (factor * factor * factor * mean))
            dmf[pl.ds(side * images + image, 1), :] += jnp.sum(v * factor * dn, axis=0, keepdims=True)
        blocks(one)
    def keep_two(q, value):
        x1[q, :] = value
        down[q, :] = value.astype(LOW)
    norm_back(x1, 1, lambda q, image: dob[q, :].astype(FULL) * weight[image, 0:1, :], keep_two)

    step(done)
    done += 1

    loads[4].wait()
    first_out = n_down + n_up
    for j in range(per):
        right = down[:, j * CH : (j + 1) * CH]
        produce(first_out + j, att[...], right)
        part = nt(right, weights(first_out + j))
        acc[...] = part if j == 0 else acc[...] + part
        step(done)
        done += 1
    dob[...] = acc[...].astype(LOW)
    fill = pltpu.make_async_copy(tokens, att, lsem.at[5])
    fill.start()

    pairs_half = CH // 128
    in_half = images * pairs_half
    def spots(k):
        half, rest = k // in_half, k % in_half
        image, s = rest // pairs_half, half * pairs_half + rest % pairs_half
        return image, s, at(image, length), pl.ds(pl.multiple_of(s * 128, 128), 128)
    def fetch(k):
        image, s, tok, lane = spots(k)
        w = k % A_SLOTS
        refs = [(qr_h.at[tok, lane], aq), (kr_h.at[tok, lane], ak), (vb_h.at[tok, lane], av), (rq_h.at[tok, lane], arq), (rk_h.at[tok, lane], ark), (p_h.at[s, image], ap)]
        return [pltpu.make_async_copy(a, b.at[w], asem.at[e, w]) for e, (a, b) in enumerate(refs)]
    for one in fetch(0):
        one.start()
    acc[...] = jnp.zeros_like(acc)
    total_pairs = images * (width // 128)
    first_qkv = first_out + n_out
    def attend(k, _):
        image, s, tok, lane = spots(k)
        w = k % A_SLOTS
        for one in fetch(k):
            one.wait()
        @pl.when(k + 1 < total_pairs)
        def _():
            for one in fetch(k + 1):
                one.start()
        q, keys, val, dout = aq[w], ak[w], av[w], dob[tok, lane]
        zero = jnp.zeros_like(q)
        dq = dk = dv = None
        for second in range(2):
            mask = head_mask(length, second)
            d_one = jnp.where(mask, dout, zero)
            p = ap[w, second]
            pf = p.astype(FULL)
            dp = nt(d_one, val)
            ds = (pf * (dp - jnp.sum(dp * pf, axis=1, keepdims=True))).astype(LOW)
            dv_one = tn(p, d_one)
            dq_one = nn(ds, jnp.where(mask, keys, zero))
            dk_one = tn(ds, jnp.where(mask, q, zero))
            dq, dk, dv = (dq_one, dk_one, dv_one) if dq is None else (dq + dq_one, dk + dk_one, dv + dv_one)
        inverse = 1.0 / (roots[0:1, lane] * roots[0:1, lane])
        hid[tok, pl.ds(pl.multiple_of(2 * width + s * 128, 128), 128)] = dv.astype(LOW)
        gain = None
        for part, (g, v, scale) in enumerate(((dq, q, arq), (dk, keys, ark))):
            v = v.astype(FULL)
            dot = g * v
            gain = dot if gain is None else gain + dot
            g = g - v * (head_sum(dot) * inverse)
            g = g * tab[0, tok, :] - pltpu.roll(g, 112, 1) * tab[2, tok, :] - pltpu.roll(g, 16, 1) * tab[1, tok, :]
            hid[tok, pl.ds(pl.multiple_of(part * width + s * 128, 128), 128)] = (g * scale[w]).astype(LOW)
        dsc[0, pl.ds(s, 1), :] += jnp.sum(gain, axis=0, keepdims=True)
        return 0
    def project(half, t):
        def some(k, t):
            attend(half * in_half + 2 * k, 0)
            attend(half * in_half + 2 * k + 1, 0)
            now = k > 0
            @pl.when(now)
            def _(): step(t)
            return t + now.astype(jnp.int32)
        t = lax.fori_loop(0, in_half // 2, some, t)
        @pl.when(half == 0)
        def _():
            fill.wait()
            norm_rows(att, mods, 0, images, nrm)
        for part in range(3):
            i = first_qkv + half * 3 + part
            cut = hid[:, pl.ds(pl.multiple_of(part * width + half * CH, CH), CH)]
            produce(i, nrm[...], cut)
            acc[...] += nt(cut, weights(i))
            step(t + part)
        return t + 3
    t = lax.fori_loop(0, per, project, jnp.int32(done))

    def keep_one(q, value):
        down[q, :] = value.astype(LOW)
    norm_back(att, 0, lambda q, image: x1[q, :], keep_one)
    result = pltpu.make_async_copy(down, dtok, osem)
    result.start()
    dmx[f] = dmf[0 : 2 * images, :].astype(LOW).astype(FULL)
    def share(d, _):
        pltpu.make_async_remote_copy(src_ref=dmx.at[f], dst_ref=dmx.at[f], send_sem=msem.at[0, 0], recv_sem=msem.at[1, 0],
            device_id=((f + d) % shards, r), device_id_type=MESH).start()
        return 0
    lax.fori_loop(1, shards, share, 0)
    def swap(k, *to):
        return remote(dsc.at[k], dsr.at[k], msem.at[0, 2 + k], msem.at[1, 2 + k], *to)
    swap(0, z, 1 - x, y, c).start()
    step(t)
    wait_bytes(dmx.at[pl.ds(0, shards - 1)], msem.at[1, 0])
    acc[0 : 8 * shards, :] = jnp.zeros((8 * shards, width), FULL)
    def spread(k, _):
        acc[pl.ds(pl.multiple_of(k * 8, 8), 2 * images), :] = dmx[k]
        return 0
    lax.fori_loop(0, shards, spread, 0)
    flat = acc[0 : 8 * shards, :].astype(LOW)
    group = call[...].astype(FULL)[:, 0:8].reshape(shards * 8, 128)
    spot = lax.broadcasted_iota(jnp.int32, group.shape, 0) % 8
    for side in range(2):
        own_rows = jnp.where((spot >= side * images) & (spot < (side + 1) * images), group, 0.0).astype(LOW)
        pm[:, side * width : (side + 1) * width] = tn(own_rows, flat)[0 : pm.shape[0]].astype(LOW)
    core_swap = remote(pm, pr, msem.at[0, 5], msem.at[1, 5], z, x, y, 1 - c)
    core_swap.start()
    back_one = nt(flat, wm[:, 0:width])
    back_two = nt(flat, wm[:, width:])
    back_all = back_one + pltpu.roll(back_two, 8 * shards - images, 0)
    dpart[...] = back_all.reshape(shards, 8, 128)
    def back(d, _):
        to = (f + d) % shards
        pltpu.make_async_remote_copy(src_ref=dpart.at[to], dst_ref=dcr.at[f], send_sem=msem.at[0, 6], recv_sem=msem.at[1, 6],
            device_id=(to, r), device_id_type=MESH).start()
        return 0
    lax.fori_loop(1, shards, back, 0)
    dcr[f] = dpart[f]
    def settle(k):
        swap(k, z, x, y, c).wait()
        dsc[k + 1] = dsc[k] + dsr[k]
    settle(0)
    swap(1, z, x, 1 - y, c).start()
    step(t + 1)
    core_swap.wait()
    half_c = pl.ds(pl.multiple_of(c * width, 128), width)
    psum[...] = plus(pm[:, half_c], pr[:, half_c])
    y_swap = remote(psum, py, msem.at[0, 7], msem.at[1, 7], z, x, 1 - y, c)
    y_swap.start()
    settle(1)
    swap(2, z, x, y, 1 - c).start()
    step(t + 2)
    settle(2)
    dsr[3] = dsc[3]
    def round_z(d):
        return remote(dsr.at[3], dsr.at[4 + z], msem.at[0, 8], msem.at[1, 8], (z + d) % Z, x, y, c)
    for d in range(1, Z):
        round_z(d).start()
    dsr[4 + z] = dsc[3]
    step(t + 3)
    y_swap.wait()
    gmod[:, half_c] = plus(psum[...], py[...])
    last = remote(gmod.at[:, half_c], gmod.at[:, half_c], msem.at[0, 9], msem.at[1, 9], z, x, y, 1 - c)
    last.start()
    wait_bytes(dsr.at[pl.ds(4, Z - 1)], msem.at[1, 8])
    total = dsr[4]
    for k in range(1, Z):
        total = total + dsr[4 + k]
    sums = head_sum(total)
    inverse = jnp.zeros(sums.shape, FULL)
    line = lax.broadcasted_iota(jnp.int32, sums.shape, 0) * 2 + lax.broadcasted_iota(jnp.int32, sums.shape, 1) // 64
    for h in range(width // 64):
        inverse = jnp.where(line == h, 0.5 / jnp.full(sums.shape, scale[h], FULL), inverse)
    dscale[...] = sums * inverse
    step(t + 4)
    wait_bytes(dcr.at[pl.ds(0, shards - 1)], msem.at[1, 6])
    wide_c[...] = jnp.zeros_like(wide_c)
    def assemble(k, _):
        one = jnp.concatenate([dcr[k], jnp.zeros((8, wide_c.shape[1] - 128), FULL)], axis=1)
        lane = lax.broadcasted_iota(jnp.int32, one.shape, 1)
        wide_c[...] += pltpu.roll(jnp.where(lane < own_map, one, 0.0), k * own_map, 1)
        return 0
    lax.fori_loop(0, shards, assemble, 0)
    dcond[...] = wide_c[0:images, :]
    lax.fori_loop(t + 5, n + B_LAG[7], lambda s, _: (step(s), 0)[1], 0)
    last.wait()
    wait_bytes(dmx.at[pl.ds(0, shards - 1)], msem.at[0, 0])
    wait_bytes(dcr.at[pl.ds(0, shards - 1)], msem.at[0, 6])
    wait_bytes(dsr.at[pl.ds(4, Z - 1)], msem.at[0, 8])
    result.wait()
    finish(n - 1)
    lax.fori_loop(n - Q_SLOTS, n, lambda i, _: (free(i), 0)[1], 0)


def backward(sigma, scale, cot, tokens, mods, wm, tab, roots, call, saved, own_map, wide_c):
    images = sigma.shape[0]
    rows, width = tokens.shape
    n, Z, _, R, w = saved[0].shape
    hidden = saved[9].shape[1]
    length = rows // images
    shards = 2 * Z
    half_z, some = Z // 2, (n + 1) // 2
    rows_m = -(-own_map // 16) * 16
    vm, dma = pltpu.VMEM, pltpu.SemaphoreType.DMA
    wide = (rows, width)
    slab = (A_SLOTS, length, 128)
    scratch = [
        vm(wide, LOW), vm((rows, hidden), LOW), vm((rows, hidden), LOW), vm((rows, hidden), LOW), vm(wide, FULL), vm(wide, LOW),
        vm(wide, LOW), vm(wide, FULL), vm(wide, LOW), vm((B_SLOTS, Z, 2, R, w), LOW), vm(slab, LOW), vm(slab, LOW), vm(slab, LOW),
        vm(slab, FULL), vm(slab, FULL), vm((A_SLOTS, 2, length, length), LOW), vm((16, width), FULL), vm((shards, 2 * images, width), FULL),
        vm((rows_m, 2 * width), LOW), vm((rows_m, 2 * width), LOW), vm((rows_m, width), LOW), vm((rows_m, width), LOW),
        vm((shards, 8, 128), FULL), vm((shards, 8, 128), FULL), vm((4, width // 128, 128), FULL), vm((4 + Z, width // 128, 128), FULL),
        vm((8, wide_c), FULL), vm((images, 8, width), FULL),
        vm((n, R, w), LOW), vm((Q_SLOTS, half_z, 2, 2, R, w), LOW), vm((RING, half_z, 2, 2, R, w // 2), LOW), vm((n, half_z, 2, R, w // 4), LOW),
        vm((n, half_z, R, w // 4), LOW), vm((n, half_z, R, w // 2), LOW), vm((some, half_z, R, w // 4), LOW), vm((some, half_z, R, w // 2), LOW),
        vm((some, max(half_z - 1, 1), R, w // 4), LOW), vm((some, max(half_z - 1, 1), R, w // 2), LOW),
        vm((some, R, w // 2), LOW),
        dma((9, n)), dma((9, n)), pltpu.SemaphoreType.REGULAR, dma((B_SLOTS,)), dma((7,)), dma((6, A_SLOTS)), dma((2, 10)), dma, dma((n,)),
    ]
    hbm, vmem = pl.BlockSpec(memory_space=pltpu.HBM), pl.BlockSpec(memory_space=pltpu.VMEM)
    smem = pl.BlockSpec(memory_space=pltpu.SMEM)
    array = jax.ShapeDtypeStruct
    return pl.pallas_call(
        functools.partial(backward_kernel, images, own_map),
        out_shape=(
            array((R, 3 * width), LOW), array((R, width), LOW), array((R, 2 * hidden), LOW), array((hidden // shards, width), LOW),
            array(wide, LOW), array((rows_m, 2 * width), LOW), array((images, wide_c), FULL), array((width // 128, 128), FULL),
        ),
        in_specs=[smem, smem, hbm, hbm] + [vmem] * 5 + [hbm] * 12,
        out_specs=tuple([hbm] * 5 + [vmem] * 3),
        scratch_shapes=scratch,
        compiler_params=pltpu.CompilerParams(collective_id=1, has_side_effects=True, vmem_limit_bytes=VMEM_LIMIT),
    )(sigma, scale, cot, tokens, mods, wm, tab, roots, call, *saved)


def local(tokens, cond, sigma_idx, pos_rows, pos_cols, attn_scale, w_mod1, w_qkv, w_out, w_mod2, w_up, w_down, cotangent):
    shards = lax.axis_size("fsdp")
    R, width = w_out.shape
    own, wide_c = w_mod1.shape[0], cond.shape[1]
    blocks = w_down.shape[0] // R
    regroup = R != 128
    if regroup:
        w_up = w_up.reshape(R, 2, shards, blocks, R).transpose(0, 1, 3, 2, 4).reshape(R, -1)
    pos = jnp.stack([pos_rows, pos_cols])
    (chunks, out, x1, qr, kr, vb, rq, rk, probs, att, h, ga, gb, mods, call, wm, tab, roots) = forward(
        tokens, cond, pos, w_mod1, w_mod2, attn_scale, w_qkv, w_out, w_up, w_down, shards
    )
    saved = (chunks, x1, qr, kr, vb, rq, rk, probs, att, h, ga, gb)
    g_qkv, g_out, g_up, g_down, d_tokens, g_mod, d_cond, d_scale = backward(
        sigma_idx, attn_scale, cotangent, tokens, mods, wm, tab, roots, call, saved, own, wide_c
    )
    d_scale = d_scale.reshape(attn_scale.shape[0], -1)[:, 0]
    if regroup:
        g_up = g_up.reshape(R, 2, blocks, shards, R).transpose(0, 1, 3, 2, 4).reshape(R, -1)
    g_mod = g_mod[:own].astype(FULL)
    return (
        out, d_tokens, d_cond, d_scale, g_mod[:, :width], g_qkv.astype(FULL), g_out.astype(FULL), g_mod[:, width:],
        g_up.astype(FULL), g_down.astype(FULL),
    )


def solution(mesh):
    placed = (
        P(("fsdp", "rep"), None),
        P(("fsdp", "rep"), None),
        P(("fsdp", "rep")),
        P(("fsdp", "rep")),
        P(("fsdp", "rep")),
        P(),
        P("fsdp", None),
        P("fsdp", None),
        P("fsdp", None),
        P("fsdp", None),
        P("fsdp", None),
        P("fsdp", None),
        P(("fsdp", "rep"), None),
    )
    return jax.shard_map(
        local,
        mesh=mesh,
        in_specs=placed,
        out_specs=(
            P(("fsdp", "rep"), None),
            P(("fsdp", "rep"), None),
            P(("fsdp", "rep"), None),
            P(),
            P("fsdp", None),
            P("fsdp", None),
            P("fsdp", None),
            P("fsdp", None),
            P("fsdp", None),
            P("fsdp", None),
        ),
        check_vma=False,
    )
```
